32 devices in a mesh: seq: 8 (over z, x), grp: 4 (over y, core).
Axes of the slice: x: 2, y: 2, z: 4, core: 2. Of those that a mesh axis runs over, the one named last changes fastest.
Arguments:
- query: bfloat16 [128, 24576], P(('grp', 'seq')), parts along dimension 0
- dec_query: bfloat16 [32, 24576], P(('grp', 'seq')), parts along dimension 0
- cache_kv: bfloat16 [32768, 576], P(('grp', 'seq')), parts along dimension 0
- span_kv: bfloat16 [128, 576], P(('grp', 'seq')), parts along dimension 0, may hold values from -4 to 4
- dec_kv: bfloat16 [32, 576], P(('grp', 'seq')), parts along dimension 0
- cache_fill: int32 [32], P('grp'), parts along dimension 0, may hold values from 128 to 992, as said below
- owner: int32 [128], P('grp'), parts along dimension 0, may hold values from 0 to 7, as said below
- slot: int32 [128], P('grp'), parts along dimension 0, may hold values from 128 to 1023, as said below
- dec_len: int32 [32], P('grp'), parts along dimension 0, may hold values from 1 to 32
- w_uk: bfloat16 [128, 128, 512], P('seq'), may hold values from -0.5 to 0.5
- w_uv: bfloat16 [128, 512, 128], P('seq'), may hold values from -0.25 to 0.25
Outputs:
- span_out: bfloat16 [128, 16384], P('grp', 'seq'), parts along dimension 0
- dec_out: bfloat16 [32, 16384], P('grp', 'seq'), parts along dimension 0
- new_cache: bfloat16 [32768, 576], P(('grp', 'seq')), parts along dimension 0
The draws below stay inside these ranges and needn't reach their ends.
There are 4 independent parts, one for each index of `grp`. The reference program is written for one: setup_inputs(seed, part) draws one part's arguments, and reference() takes and returns one part's arrays. A program takes and returns all parts, laid end to end along the dimension named above; an argument that names none is the same for every part. Nothing has to cross between parts.
Inputs may be any that keep to these rules, and one draw needn't show every extreme that they name: `cache_fill`: every block keeps at least 128 filled slots and room for all 32 new rows. `owner`: a block index for each prefill token; blocks receive unequal numbers of rows. slot[t] = cache_fill[owner[t]] plus the number of earlier prefill tokens with the same owner.
All inputs are finite; a program needn't handle non-finite values.
Results may differ from the reference program's by a relative error of at most 0.014.
Values may be sent and summed in bfloat16 or wider, within the bound.
No kernel may reach another device: no remote copies, remote signals or barrier semaphores. Data moves between devices by JAX's collectives and lax.ppermute only.
A program may use at most 192 MiB of HBM per device.

```python
import jax
import jax.numpy as jnp
from jax import lax

H = 128
DN = 128
DR = 64
DC = 512
DV = 128
POS_DEV = 1024
SPAN = 32
ROWS = 8
CACHE = 8192
N_SEQ = 8


def decode_rope(key):
    return jax.random.normal(jax.random.fold_in(key, 901), (ROWS, DR), jnp.float32)


def placement_draw(key):
    key = jax.random.fold_in(key, 500)
    fill = jax.random.randint(jax.random.fold_in(key, 1), (N_SEQ,), POS_DEV // 8, POS_DEV - SPAN + 1)
    weights = jax.random.randint(jax.random.fold_in(key, 2), (N_SEQ,), 1, 9)
    cumul = jnp.cumsum(weights)
    pick = jax.random.randint(jax.random.fold_in(key, 3), (SPAN,), 0, cumul[N_SEQ - 1])
    owner = jnp.sum((cumul[None, :] <= pick[:, None]).astype(jnp.int32), axis=1).astype(jnp.int32)
    onehot = (owner[:, None] == jnp.arange(N_SEQ, dtype=jnp.int32)[None, :]).astype(jnp.int32)
    earlier = jnp.cumsum(onehot, axis=0) - onehot
    rank = jnp.sum(earlier * onehot, axis=1)
    base = jnp.sum(onehot * fill[None, :], axis=1)
    return (fill.astype(jnp.int32), owner, (base + rank).astype(jnp.int32))


def draw_cache_fill(key, part):
    return placement_draw(key)[0]


def draw_owner(key, part):
    return placement_draw(key)[1]


def draw_slot(key, part):
    return placement_draw(key)[2]


def draw_query(key, part):
    key = jax.random.fold_in(key, 1)
    values = jax.random.normal(key, (SPAN, H, DN + DR), jnp.float32)
    return values.reshape(SPAN, H * (DN + DR)).astype(jnp.bfloat16)


def draw_dec_query(key, part):
    shared = decode_rope(key)
    key = jax.random.fold_in(key, 2)
    values = jax.random.normal(key, (ROWS, H, DN + DR), jnp.float32)
    rope = 1.1 * shared[:, None, :] + 0.5 * values[:, :, DN:]
    values = jnp.concatenate([values[:, :, :DN], rope], axis=2)
    return values.reshape(ROWS, H * (DN + DR)).astype(jnp.bfloat16)


def draw_dec_kv(key, part):
    shared = decode_rope(key)
    key = jax.random.fold_in(key, 3)
    latent = 0.5 * jax.random.normal(key, (ROWS, DC), jnp.float32)
    return jnp.concatenate([latent, shared], axis=1).astype(jnp.bfloat16)


def draw_cache_kv(key, part):
    key = jax.random.fold_in(key, 4)
    values = jax.random.normal(key, (CACHE, DC + DR), jnp.float32)
    latent = 0.5 * values[:, :DC]
    rope = values[:, DC:]
    return jnp.concatenate([latent, rope], axis=1).astype(jnp.bfloat16)


def touch_ends(values, key, low, high):
    longest = values.shape.index(max(values.shape))
    spots = []
    for shift in (0, 1):
        where = [jax.random.randint(jax.random.fold_in(key, axis), (), 0, length) for axis, length in enumerate(values.shape)]
        where[longest] = (where[longest] + shift) % values.shape[longest]
        spots.append(tuple(where))
    return values.at[spots[0]].set(low).at[spots[1]].set(high)


def block_levels(key, extent, pieces, low, high):
    def one(position, shards_of):
        steps = jax.random.uniform(jax.random.fold_in(jax.random.fold_in(key, 6), position), (shards_of,), jnp.float32, low / len(pieces), high / len(pieces))
        return jnp.repeat(jnp.exp(steps), extent[position] // shards_of).reshape((-1,) + (1,) * (len(extent) - position - 1))

    loudness = one(*pieces[0])
    for cut in pieces[1:]:
        loudness = loudness * one(*cut)
    return loudness


def gaussian(rng, extent, spread, most, cuts=(), kind=jnp.bfloat16):
    drawn = jax.random.normal(rng, extent, jnp.float32) * spread
    if len(cuts) > 0:
        drawn = block_levels(rng, extent, cuts, -0.22, 0.18) * drawn
    return jnp.clip(drawn, min=-most, max=most).astype(kind)


def setup_inputs(seed: int = 0, part: int = 0) -> dict:
    key_of = jax.random.split(jax.random.key(seed), 12)
    own_keys = jax.random.split(jax.random.fold_in(key_of[11], part), 12)
    query = draw_query(jax.random.fold_in(jax.random.fold_in(key_of[11], part), 71), part)
    dec_query = draw_dec_query(jax.random.fold_in(jax.random.fold_in(key_of[11], part), 71), part)
    cache_kv = draw_cache_kv(jax.random.fold_in(jax.random.fold_in(key_of[11], part), 71), part)
    span_kv = gaussian(own_keys[3], (SPAN, DC + DR), 0.5, 4.0, ((0, 8),))
    dec_kv = draw_dec_kv(jax.random.fold_in(jax.random.fold_in(key_of[11], part), 71), part)
    cache_fill = draw_cache_fill(jax.random.fold_in(jax.random.fold_in(key_of[11], part), 71), part)
    owner = draw_owner(jax.random.fold_in(jax.random.fold_in(key_of[11], part), 71), part)
    slot = draw_slot(jax.random.fold_in(jax.random.fold_in(key_of[11], part), 71), part)
    dec_len = touch_ends(jax.random.randint(own_keys[8], (ROWS,), 1, SPAN + 1), jax.random.fold_in(own_keys[8], 1), 1, SPAN).astype(jnp.int32)
    w_uk = gaussian(key_of[9], (H, DN, DC), DN ** -0.5, 0.5, ((0, 8),))
    w_uv = gaussian(key_of[10], (H, DC, DV), DC ** -0.5, 0.25, ((0, 8),))
    return {"query": query, "dec_query": dec_query, "cache_kv": cache_kv, "span_kv": span_kv, "dec_kv": dec_kv, "cache_fill": cache_fill, "owner": owner, "slot": slot, "dec_len": dec_len, "w_uk": w_uk, "w_uv": w_uv}


score_scale = 0.1353


def tag_rows(rows, cache_fill, owner, slot, pos_dev, span):
    block = rows // pos_dev
    local = rows % pos_dev
    count = cache_fill.shape[0]
    fills = jnp.sum(jnp.where(block[:, None] == jnp.arange(count, dtype=jnp.int32)[None, :], cache_fill[None, :], 0), axis=1)
    base = jnp.where(local < fills, -1, span + 1)
    target = owner * pos_dev + slot
    token = jnp.arange(span, dtype=jnp.int32)
    placed = jnp.sum(jnp.where(rows[:, None] == target[None, :], token[None, :] + 1, 0), axis=1)
    return jnp.where(placed > 0, placed - 1, base).astype(jnp.int32)


def combine(state, peak, total, output):
    old_peak, old_total, old_acc = state
    top = jnp.maximum(old_peak, peak)
    keep = jnp.exp(old_peak - top)
    fresh = jnp.exp(peak - top)
    return top, old_total * keep + total * fresh, old_acc * keep[..., None] + output * fresh[..., None]


def block_partial(absorbed, keys, tags, limits):
    scores = jnp.einsum("qhc,pc->qhp", absorbed.astype(jnp.float32), keys.astype(jnp.float32)) * score_scale
    visible = tags[None, None, :] < limits[:, None, None]
    peak = jnp.max(jnp.where(visible, scores, -1e30), axis=2)
    weights = jnp.where(visible, jnp.exp(scores - peak[..., None]), 0.0)
    total = jnp.sum(weights, axis=2)
    rounded = lax.optimization_barrier(weights.astype(jnp.bfloat16)).astype(jnp.float32)
    output = jnp.einsum("qhp,pc->qhc", rounded, keys[:, :DC].astype(jnp.float32))
    return peak, total, output


def absorb(query, w_uk):
    shaped = query.reshape(query.shape[0], H, DN + DR)
    latent = jnp.einsum("thn,hnc->thc", shaped[:, :, :DN].astype(jnp.float32), w_uk.astype(jnp.float32)).astype(jnp.bfloat16)
    return jnp.concatenate([latent, shaped[:, :, DN:]], axis=2)


def reference(query, dec_query, cache_kv, span_kv, dec_kv, cache_fill, owner, slot, dec_len, w_uk, w_uv):
    index = (owner * POS_DEV + slot).astype(jnp.int32)
    new_cache = cache_kv.at[index].set(span_kv)
    tags = tag_rows(jnp.arange(CACHE, dtype=jnp.int32), cache_fill, owner, slot, POS_DEV, SPAN)
    absorbed = jnp.concatenate([absorb(query, w_uk), absorb(dec_query, w_uk)], axis=0)
    limits = jnp.concatenate([jnp.arange(1, SPAN + 1, dtype=jnp.int32), dec_len.astype(jnp.int32)])
    count = SPAN + ROWS
    init = (jnp.full((count, H), -1e30, jnp.float32), jnp.zeros((count, H), jnp.float32), jnp.zeros((count, H, DC), jnp.float32))

    def step(carry, block):
        start = (block * POS_DEV).astype(jnp.int32)
        keys = lax.dynamic_slice_in_dim(new_cache, start, POS_DEV, 0)
        block_tags = lax.dynamic_slice_in_dim(tags, start, POS_DEV, 0)
        return combine(carry, *block_partial(absorbed, keys, block_tags, limits)), None

    (peak, total, acc), unused = lax.scan(step, init, jnp.arange(N_SEQ, dtype=jnp.int32))
    dec_abs = absorbed[SPAN:].astype(jnp.float32)
    own = jnp.einsum("rhc,rc->rh", dec_abs, dec_kv.astype(jnp.float32)) * score_scale
    own_out = jnp.broadcast_to(dec_kv[:, None, :DC].astype(jnp.float32), (ROWS, H, DC))
    dec_state = combine((peak[SPAN:], total[SPAN:], acc[SPAN:]), own, jnp.ones((ROWS, H), jnp.float32), own_out)
    total = jnp.concatenate([total[:SPAN], dec_state[1]], axis=0)
    acc = jnp.concatenate([acc[:SPAN], dec_state[2]], axis=0)
    latent_out = (acc / total[..., None]).astype(jnp.bfloat16)
    result = jnp.einsum("qhc,hcv->qhv", latent_out.astype(jnp.float32), w_uv.astype(jnp.float32)).astype(jnp.bfloat16)
    result = result.reshape(count, H * DV)
    return result[:SPAN], result[SPAN:], new_cache
```

```python
import functools

import jax
import jax.numpy as jnp
from jax import lax
from jax.experimental import pallas as pl
from jax.experimental.pallas import tpu as pltpu
from jax.sharding import PartitionSpec as P

DN = 128
DC = 512
LANES = 128
CHUNKS = 4

score_scale = 0.1353
LOG2E = 1.4426950408889634
HIDDEN = -1e30
FLOOR = -1e25


def lanes(x, width):
    return jnp.concatenate([x] * (width // LANES), axis=1) if width > LANES else x


def attend_kernel(pieces, extra, first, last, *refs):
    refs = list(refs)
    fills = refs.pop(0)
    q_ref = refs.pop(0)
    keys = [refs.pop(0) for _ in pieces]
    if extra:
        new_ref = refs.pop(0)
        bias_ref = refs.pop(0)
    if not first:
        m_in, l_in, acc_in = refs.pop(0), refs.pop(0), refs.pop(0)
    q = q_ref[...]
    rows = q.shape[0]
    scores = []
    for (start, width, which), ref in zip(pieces, keys):
        s = jnp.dot(q, ref[...], preferred_element_type=jnp.float32)
        slot = start + lax.broadcasted_iota(jnp.int32, (1, width), 1)
        scores.append(jnp.where(slot < fills[which], s, HIDDEN))
    if extra:
        s = lax.dot_general(
            q, new_ref[...], (((1,), (1,)), ((), ())), preferred_element_type=jnp.float32
        )
        bias = bias_ref[...]
        scores.append(s + jnp.concatenate([bias] * (rows // bias.shape[0]), axis=0))
    peak = functools.reduce(jnp.maximum, [jnp.max(s, axis=1, keepdims=True) for s in scores])
    peak = jnp.maximum(peak, FLOOR)
    if not first:
        old = m_in[...]
        peak = jnp.maximum(peak, old[:, :1])
    scale = score_scale * LOG2E
    total = 0.0
    acc = 0.0
    for i, s in enumerate(scores):
        e = jnp.exp2((s - peak) * scale)
        total = total + jnp.sum(e, axis=1, keepdims=True)
        w = e.astype(jnp.bfloat16)
        if i < len(pieces):
            acc = acc + lax.dot_general(
                w, keys[i][:DC, :], (((1,), (1,)), ((), ())), preferred_element_type=jnp.float32
            )
        else:
            acc = acc + jnp.dot(w, new_ref[:, :DC], preferred_element_type=jnp.float32)
    if not first:
        keep = jnp.exp2((old[:, :1] - peak) * scale)
        total = total + l_in[:, :1] * keep
        acc = acc + acc_in[...] * keep
    if not last:
        m_out, l_out, acc_out = refs
        m_out[...] = jnp.broadcast_to(peak, (rows, LANES))
        l_out[...] = jnp.broadcast_to(total, (rows, LANES))
        acc_out[...] = acc
        return
    (out,) = refs
    out[:rows, :] = (acc * (1.0 / total)).astype(jnp.bfloat16)
    weight = jnp.broadcast_to(peak * scale + jnp.log2(total), (rows, LANES))
    tail = out.shape[0] - rows
    place = lax.broadcasted_iota(jnp.int32, (tail, LANES), 0)
    packed = jnp.zeros((tail, LANES), jnp.float32)
    for g in range(rows // LANES):
        turned = jnp.transpose(weight[g * LANES : (g + 1) * LANES, :])
        packed = jnp.where(place == g, turned[:tail, :], packed)
    high = packed.astype(jnp.bfloat16)
    rest = packed - high.astype(jnp.float32)
    mid = rest.astype(jnp.bfloat16)
    low = (rest - mid.astype(jnp.float32)).astype(jnp.bfloat16)
    out[rows:, :] = jnp.concatenate([high, mid, low, jnp.zeros_like(low)], axis=1)


def attend(fills, q, pieces, new=None, state=None, last=False, tile=None):
    rows, width = q.shape
    tile = rows if tile is None else tile
    spec = tuple((start, keys.shape[1], which) for start, which, keys in pieces)
    operands = [fills, q]
    in_specs = [
        pl.BlockSpec(memory_space=pltpu.SMEM),
        pl.BlockSpec((tile, width), lambda i: (i, 0)),
    ]
    for _, _, keys in pieces:
        operands.append(keys)
        in_specs.append(pl.BlockSpec(keys.shape, lambda i: (0, 0)))
    if new is not None:
        for x in new:
            operands.append(x)
            in_specs.append(pl.BlockSpec(x.shape, lambda i: (0, 0)))
    state_specs = [
        pl.BlockSpec((tile, LANES), lambda i: (i, 0)),
        pl.BlockSpec((tile, LANES), lambda i: (i, 0)),
        pl.BlockSpec((tile, DC), lambda i: (i, 0)),
    ]
    if state is not None:
        operands += list(state)
        in_specs += state_specs
    if last:
        tail = -(-rows // (LANES * 16)) * 16
        out_shape = jax.ShapeDtypeStruct((rows + tail, DC), jnp.bfloat16)
        out_specs = pl.BlockSpec((rows + tail, DC), lambda i: (0, 0))
    else:
        out_shape = (
            jax.ShapeDtypeStruct((rows, LANES), jnp.float32),
            jax.ShapeDtypeStruct((rows, LANES), jnp.float32),
            jax.ShapeDtypeStruct((rows, DC), jnp.float32),
        )
        out_specs = tuple(state_specs)
    count = sum(piece[1] for piece in spec)
    return pl.pallas_call(
        functools.partial(attend_kernel, spec, new is not None, state is None, last),
        grid=(rows // tile,),
        in_specs=in_specs,
        out_specs=out_specs,
        out_shape=out_shape,
        compiler_params=pltpu.CompilerParams(vmem_limit_bytes=40 * 1024 * 1024),
        cost_estimate=pl.CostEstimate(
            flops=2 * rows * count * (width + DC),
            bytes_accessed=2 * count * width + 4 * rows * DC * 2,
            transcendentals=rows * count,
        ),
        name="attend",
    )(*operands)


def finish_kernel(count, m_ref, l_ref, acc_ref, far_ref, w_ref, out_ref):
    rows = m_ref.shape[0]
    heads = w_ref.shape[0]
    scale = score_scale * LOG2E
    parts = far_ref[rows:, :].astype(jnp.float32)
    packed = parts[:, :LANES] + parts[:, LANES : 2 * LANES] + parts[:, 2 * LANES : 3 * LANES]
    columns = []
    for g in range(rows // LANES):
        row = jnp.broadcast_to(packed[g : g + 1, :], (LANES, LANES))
        columns.append(jnp.transpose(row))
    far = jnp.concatenate(columns, axis=0)
    near = m_ref[...] * scale
    top = jnp.maximum(near, far)
    w_near = jnp.exp2(near - top)
    w_far = jnp.exp2(far - top)
    total = l_ref[...] * w_near + w_far
    inverse = 1.0 / total
    w_near = lanes(w_near * inverse, DC)
    w_far = lanes(w_far * inverse, DC)
    for h in range(heads):
        a, b = h * count, (h + 1) * count
        near_part = acc_ref[a:b, :] * w_near[a:b, :]
        far_part = far_ref[:rows, :].astype(jnp.float32)[a:b, :] * w_far[a:b, :]
        latent = (near_part + far_part).astype(jnp.bfloat16)
        out_ref[:, h * LANES : (h + 1) * LANES] = jnp.dot(
            latent, w_ref[h], preferred_element_type=jnp.float32
        ).astype(jnp.bfloat16)


def finish(count, state, far, w_uv):
    heads = w_uv.shape[0]
    return pl.pallas_call(
        functools.partial(finish_kernel, count),
        out_shape=jax.ShapeDtypeStruct((count, heads * w_uv.shape[2]), jnp.bfloat16),
        compiler_params=pltpu.CompilerParams(vmem_limit_bytes=40 * 1024 * 1024),
        cost_estimate=pl.CostEstimate(
            flops=2 * count * heads * DC * w_uv.shape[2],
            bytes_accessed=2 * w_uv.size + 6 * state[2].size,
            transcendentals=0,
        ),
        name="finish",
    )(*state, far, w_uv)


def body(query, dec_query, cache_kv, span_kv, dec_kv, cache_fill, owner, slot, dec_len, w_uk, w_uv):
    me = lax.axis_index("seq")
    n = lax.axis_size("seq")
    pos_dev = cache_kv.shape[0]
    span = owner.shape[0]
    rows_dec = dec_len.shape[0]
    count = span + rows_dec
    heads = w_uk.shape[0]
    row = cache_kv.shape[1]
    width = query.shape[1] // (heads * n)

    def swap(x, stride):
        return lax.ppermute(x, "seq", [(i, i ^ stride) for i in range(n)])

    far, pair = n // 2, n // 4
    near = [1 << b for b in range(pair.bit_length() - 1)]
    keys = cache_kv.T
    size = pos_dev // CHUNKS

    mine = jnp.concatenate([query, dec_query], axis=0)
    local = mine.shape[0]
    mine = jnp.swapaxes(mine.reshape(local, n, heads * width), 0, 1)
    fresh = jnp.concatenate([span_kv, dec_kv], axis=0)
    mine = jnp.concatenate([mine, jnp.broadcast_to(fresh[None], (n, local, row))], axis=2)
    got = lax.all_to_all(mine, "seq", split_axis=0, concat_axis=0, tiled=True)

    blocks = [(jnp.int32(0), [keys])]
    for stride in near:
        blocks += [(offset ^ stride, [swap(x, stride) for x in held]) for offset, held in blocks]
    pieces = []
    for c in range(CHUNKS):
        part = [(jnp.int32(far), swap(keys[:, c * size : (c + 1) * size], far))]
        for stride in near:
            part += [(offset ^ stride, swap(x, stride)) for offset, x in part]
        pieces.append(part)

    per = span // n
    got_span = got[:, :per].reshape(span, -1)
    got_dec = got[:, per:].reshape(rows_dec, -1)
    both = jnp.concatenate([got_span, got_dec], axis=0)
    new_rows = both[:, heads * width :]
    q = both[:, : heads * width].reshape(count, heads, width)
    latent = jnp.einsum(
        "thn,hnc->htc", q[:, :, :DN], w_uk, preferred_element_type=jnp.float32
    ).astype(jnp.bfloat16)
    absorbed = jnp.concatenate([latent, jnp.swapaxes(q[:, :, DN:], 0, 1)], axis=2)
    absorbed = absorbed.reshape(heads * count, row)
    other = swap(absorbed, pair)

    target = jnp.where(owner == me, slot, -1)
    onehot = jnp.arange(pos_dev, dtype=jnp.int32)[None, :] == target[:, None]
    placed = lax.dot_general(
        new_rows[:span],
        onehot.astype(jnp.bfloat16),
        (((0,), (0,)), ((), ())),
        preferred_element_type=jnp.float32,
    ).astype(jnp.bfloat16)
    new_cache = jnp.where(jnp.any(onehot, axis=0)[None, :], placed, keys).T

    limits = jnp.concatenate([jnp.arange(1, span + 1, dtype=jnp.int32), dec_len])
    index = jnp.arange(LANES, dtype=jnp.int32)
    queries = jnp.arange(count, dtype=jnp.int32)
    seen = (index[None, :] < span) & (index[None, :] < limits[:, None])
    seen |= (index[None, :] >= span) & (index[None, :] == queries[:, None])
    bias = jnp.where(seen, 0.0, HIDDEN).astype(jnp.float32)
    extra = jnp.zeros((LANES, row), jnp.bfloat16).at[:count].set(new_rows)

    held = [offset for offset, _ in blocks]
    offsets = held + [offset ^ far for offset in held]
    which = jnp.stack([me ^ offset for offset in offsets])
    fills = jnp.sum(
        jnp.where(which[:, None] == jnp.arange(n, dtype=jnp.int32)[None, :], cache_fill[None, :], 0),
        axis=1,
    )
    base = len(blocks)
    tile = heads // 2 * count
    stages = [[(0, i, xs[0]) for i, (_, xs) in enumerate(blocks)]]
    flat = [[(c * size, base + i, x) for i, (_, x) in enumerate(part)] for c, part in enumerate(pieces)]
    half = CHUNKS // 2
    stages.append([p for part in flat[:half] for p in part])
    stages.append([p for part in flat[half:-1] for p in part] + flat[-1][:1])
    final = flat[-1][1:]

    state = attend(fills, absorbed, stages[0], new=(extra, bias), tile=tile)
    guest = attend(fills, other, stages[0], tile=tile)
    for stage in stages[1:]:
        guest = attend(fills, other, stage, state=guest, tile=tile)
        state = attend(fills, absorbed, stage, state=state, tile=tile)
    sent = attend(fills, other, final, state=guest, last=True)
    back = swap(sent, pair)
    state = attend(fills, absorbed, final, state=state, tile=tile)
    result = finish(count, state, back, w_uv)
    return (result[:span], result[span:], new_cache)


def solution(mesh):
    in_specs = (
        P(("grp", "seq"), None),
        P(("grp", "seq"), None),
        P(("grp", "seq"), None),
        P(("grp", "seq"), None),
        P(("grp", "seq"), None),
        P("grp"),
        P("grp"),
        P("grp"),
        P("grp"),
        P("seq", None, None),
        P("seq", None, None),
    )
    out_specs = (P("grp", "seq"), P("grp", "seq"), P(("grp", "seq"), None))
    return jax.shard_map(body, mesh=mesh, in_specs=in_specs, out_specs=out_specs, check_vma=False)
```

```python
import functools

import jax
import jax.numpy as jnp
from jax import lax
from jax.experimental import pallas as pl
from jax.experimental.pallas import tpu as pltpu
from jax.sharding import PartitionSpec as P

DN = 128
DC = 512
LANES = 128
CHUNKS = 4

score_scale = 0.1353
LOG2E = 1.4426950408889634
HIDDEN = -1e30
FLOOR = -1e25


def lanes(x, width):
    return jnp.concatenate([x] * (width // LANES), axis=1) if width > LANES else x


def attend_kernel(pieces, extra, first, last, through, *refs):
    refs = list(refs)
    fills = refs.pop(0)
    q_ref = refs.pop(0)
    keys = [refs.pop(0) for _ in pieces]
    if extra:
        new_ref = refs.pop(0)
        bias_ref = refs.pop(0)
    if not first:
        m_in, l_in, acc_in = refs.pop(0), refs.pop(0), refs.pop(0)
    refs = refs[through : len(refs) - through]
    rows = q_ref.shape[0]
    q = q_ref[:, : keys[0].shape[0]]
    scores = []
    for (start, width, which), ref in zip(pieces, keys):
        s = jnp.dot(q, ref[...], preferred_element_type=jnp.float32)
        slot = start + lax.broadcasted_iota(jnp.int32, (1, width), 1)
        scores.append(jnp.where(slot < fills[which], s, HIDDEN))
    if extra:
        s = lax.dot_general(
            q, new_ref[...], (((1,), (1,)), ((), ())), preferred_element_type=jnp.float32
        )
        bias = bias_ref[...]
        scores.append(s + jnp.concatenate([bias] * (rows // bias.shape[0]), axis=0))
    peak = functools.reduce(jnp.maximum, [jnp.max(s, axis=1, keepdims=True) for s in scores])
    peak = jnp.maximum(peak, FLOOR)
    if not first:
        old = m_in[...]
        peak = jnp.maximum(peak, old[:, :1])
    scale = score_scale * LOG2E
    total = 0.0
    acc = 0.0
    for i, s in enumerate(scores):
        e = jnp.exp2((s - peak) * scale)
        total = total + jnp.sum(e, axis=1, keepdims=True)
        w = e.astype(jnp.bfloat16)
        if i < len(pieces):
            acc = acc + lax.dot_general(
                w, keys[i][:DC, :], (((1,), (1,)), ((), ())), preferred_element_type=jnp.float32
            )
        else:
            acc = acc + jnp.dot(w, new_ref[:, :DC], preferred_element_type=jnp.float32)
    if not first:
        keep = jnp.exp2((old[:, :1] - peak) * scale)
        total = total + l_in[:, :1] * keep
        acc = acc + acc_in[...] * keep
    if not last:
        m_out, l_out, acc_out = refs
        m_out[...] = jnp.broadcast_to(peak, (rows, LANES))
        l_out[...] = jnp.broadcast_to(total, (rows, LANES))
        acc_out[...] = acc
        return
    (out,) = refs
    out[:rows, :] = (acc * (1.0 / total)).astype(jnp.bfloat16)
    weight = jnp.broadcast_to(peak * scale + jnp.log2(total), (rows, LANES))
    tail = out.shape[0] - rows
    place = lax.broadcasted_iota(jnp.int32, (tail, LANES), 0)
    packed = jnp.zeros((tail, LANES), jnp.float32)
    for g in range(rows // LANES):
        turned = jnp.transpose(weight[g * LANES : (g + 1) * LANES, :])
        packed = jnp.where(place == g, turned[:tail, :], packed)
    high = packed.astype(jnp.bfloat16)
    rest = packed - high.astype(jnp.float32)
    mid = rest.astype(jnp.bfloat16)
    low = (rest - mid.astype(jnp.float32)).astype(jnp.bfloat16)
    out[rows:, :] = jnp.concatenate([high, mid, low, jnp.zeros_like(low)], axis=1)


def attend(fills, q, pieces, new=None, state=None, last=False, tile=None, through=()):
    rows, width = q.shape
    tile = rows if tile is None else tile
    spec = tuple((start, keys.shape[1], which) for start, which, keys in pieces)
    operands = [fills, q]
    in_specs = [
        pl.BlockSpec(memory_space=pltpu.SMEM),
        pl.BlockSpec((tile, width), lambda i: (i, 0)),
    ]
    for _, _, keys in pieces:
        operands.append(keys)
        in_specs.append(pl.BlockSpec(keys.shape, lambda i: (0, 0)))
    if new is not None:
        for x in new:
            operands.append(x)
            in_specs.append(pl.BlockSpec(x.shape, lambda i: (0, 0)))
    state_specs = [
        pl.BlockSpec((tile, LANES), lambda i: (i, 0)),
        pl.BlockSpec((tile, LANES), lambda i: (i, 0)),
        pl.BlockSpec((tile, DC), lambda i: (i, 0)),
    ]
    if state is not None:
        operands += list(state)
        in_specs += state_specs
    if last:
        tail = -(-rows // (LANES * 16)) * 16
        out_shape = [jax.ShapeDtypeStruct((rows + tail, DC), jnp.bfloat16)]
        out_specs = [pl.BlockSpec((rows + tail, DC), lambda i: (0, 0))]
    else:
        out_shape = [
            jax.ShapeDtypeStruct((rows, LANES), jnp.float32),
            jax.ShapeDtypeStruct((rows, LANES), jnp.float32),
            jax.ShapeDtypeStruct((rows, DC), jnp.float32),
        ]
        out_specs = list(state_specs)
    aliases = {len(operands) + i: len(out_shape) + i for i in range(len(through))}
    operands += list(through)
    in_specs += [pl.BlockSpec(memory_space=pl.ANY)] * len(through)
    made = len(out_shape)
    out_shape += [jax.ShapeDtypeStruct(x.shape, x.dtype) for x in through]
    out_specs += [pl.BlockSpec(memory_space=pl.ANY)] * len(through)
    count = sum(piece[1] for piece in spec)
    out = pl.pallas_call(
        functools.partial(attend_kernel, spec, new is not None, state is None, last, len(through)),
        grid=(rows // tile,),
        in_specs=in_specs,
        out_specs=out_specs,
        out_shape=out_shape,
        compiler_params=pltpu.CompilerParams(vmem_limit_bytes=40 * 1024 * 1024),
        cost_estimate=pl.CostEstimate(
            flops=2 * rows * count * (width + DC),
            bytes_accessed=2 * count * width + 4 * rows * DC * 2,
            transcendentals=rows * count,
        ),
        input_output_aliases=aliases,
        name="attend",
    )(*operands)
    result = out[0] if last else tuple(out[:made])
    return (result, *out[made:]) if through else result


def absorb_kernel(span_ref, dec_ref, w_ref, absorbed_ref, extra_ref):
    heads = w_ref.shape[0]
    row = extra_ref.shape[1]
    width = (span_ref.shape[1] - row) // heads
    count = span_ref.shape[0] + dec_ref.shape[0]
    rows = jnp.concatenate(
        [span_ref[...].astype(jnp.float32), dec_ref[...].astype(jnp.float32)], axis=0
    )
    q = rows.astype(jnp.bfloat16)
    blank = jnp.zeros((count, absorbed_ref.shape[1] - row), jnp.float32)
    for h in range(0, heads, 2):
        parts = []
        for g in (h, h + 1):
            mine = q[:, g * width : (g + 1) * width]
            latent = jnp.dot(mine[:, :DN], w_ref[g], preferred_element_type=jnp.float32)
            rope = mine[:, DN:].astype(jnp.float32)
            parts.append(jnp.concatenate([latent, rope, blank], axis=1))
        pair = jnp.concatenate(parts, axis=0).astype(jnp.bfloat16)
        absorbed_ref[h * count : (h + 2) * count, :] = pair
    blank = jnp.zeros((extra_ref.shape[0] - count, row), jnp.float32)
    new = jnp.concatenate([rows[:, heads * width :], blank], axis=0)
    extra_ref[...] = new.astype(jnp.bfloat16)


def absorb(got_span, got_dec, w_uk, row):
    heads = w_uk.shape[0]
    count = got_span.shape[0] + got_dec.shape[0]
    return pl.pallas_call(
        absorb_kernel,
        out_shape=(
            jax.ShapeDtypeStruct((heads * count, -(-row // LANES) * LANES), jnp.bfloat16),
            jax.ShapeDtypeStruct((LANES, row), jnp.bfloat16),
        ),
        compiler_params=pltpu.CompilerParams(vmem_limit_bytes=40 * 1024 * 1024),
        cost_estimate=pl.CostEstimate(
            flops=2 * count * heads * DN * DC,
            bytes_accessed=2 * w_uk.size + 4 * got_span.size,
            transcendentals=0,
        ),
        name="absorb",
    )(got_span, got_dec, w_uk)


def split_kernel(size, skip, x_ref, after_ref, *out_refs):
    for i, ref in enumerate(out_refs):
        ref[...] = x_ref[:, (skip + i) * size : (skip + i + 1) * size]


def split(x, size, skip, after):
    pieces = x.shape[1] // size - skip
    return pl.pallas_call(
        functools.partial(split_kernel, size, skip),
        in_specs=[
            pl.BlockSpec(memory_space=pltpu.VMEM),
            pl.BlockSpec(memory_space=pl.ANY),
        ],
        out_shape=[jax.ShapeDtypeStruct((x.shape[0], size), x.dtype)] * pieces,
        compiler_params=pltpu.CompilerParams(vmem_limit_bytes=16 * 1024 * 1024),
        name="split",
    )(x, after)


def finish_kernel(count, m_ref, l_ref, acc_ref, far_ref, w_ref, span_ref, dec_ref):
    rows = m_ref.shape[0]
    heads = w_ref.shape[0]
    scale = score_scale * LOG2E
    parts = far_ref[rows:, :].astype(jnp.float32)
    packed = parts[:, :LANES] + parts[:, LANES : 2 * LANES] + parts[:, 2 * LANES : 3 * LANES]
    columns = []
    for g in range(rows // LANES):
        row = jnp.broadcast_to(packed[g : g + 1, :], (LANES, LANES))
        columns.append(jnp.transpose(row))
    far = jnp.concatenate(columns, axis=0)
    near = m_ref[...] * scale
    top = jnp.maximum(near, far)
    w_near = jnp.exp2(near - top)
    w_far = jnp.exp2(far - top)
    total = l_ref[...] * w_near + w_far
    inverse = 1.0 / total
    w_near = lanes(w_near * inverse, DC)
    w_far = lanes(w_far * inverse, DC)
    for h in range(heads):
        a, b = h * count, (h + 1) * count
        near_part = acc_ref[a:b, :] * w_near[a:b, :]
        far_part = far_ref[:rows, :].astype(jnp.float32)[a:b, :] * w_far[a:b, :]
        latent = (near_part + far_part).astype(jnp.bfloat16)
        done = jnp.dot(latent, w_ref[h], preferred_element_type=jnp.float32)
        span = span_ref.shape[0]
        span_ref[:, h * LANES : (h + 1) * LANES] = done[:span].astype(jnp.bfloat16)
        dec_ref[:, h * LANES : (h + 1) * LANES] = done[span:].astype(jnp.bfloat16)


def finish(count, span, state, far, w_uv):
    heads = w_uv.shape[0]
    wide = heads * w_uv.shape[2]
    return pl.pallas_call(
        functools.partial(finish_kernel, count),
        out_shape=(
            jax.ShapeDtypeStruct((span, wide), jnp.bfloat16),
            jax.ShapeDtypeStruct((count - span, wide), jnp.bfloat16),
        ),
        compiler_params=pltpu.CompilerParams(vmem_limit_bytes=40 * 1024 * 1024),
        cost_estimate=pl.CostEstimate(
            flops=2 * count * heads * DC * w_uv.shape[2],
            bytes_accessed=2 * w_uv.size + 6 * state[2].size,
            transcendentals=0,
        ),
        name="finish",
    )(*state, far, w_uv)


def body(query, dec_query, cache_kv, span_kv, dec_kv, cache_fill, owner, slot, dec_len, w_uk, w_uv):
    me = lax.axis_index("seq")
    n = lax.axis_size("seq")
    pos_dev = cache_kv.shape[0]
    span = owner.shape[0]
    rows_dec = dec_len.shape[0]
    count = span + rows_dec
    heads = w_uk.shape[0]
    row = cache_kv.shape[1]
    width = query.shape[1] // (heads * n)

    def swap(x, stride):
        return lax.ppermute(x, "seq", [(i, i ^ stride) for i in range(n)])

    far, pair = n // 2, n // 4
    near = [1 << b for b in range(pair.bit_length() - 1)]
    keys = cache_kv.T
    size = pos_dev // CHUNKS

    per, per_dec = span // n, rows_dec // n
    mine = jnp.swapaxes(query.reshape(per, n, heads * width), 0, 1)
    fresh = jnp.broadcast_to(span_kv[None], (n, per, row))
    mine_dec = jnp.swapaxes(dec_query.reshape(per_dec, n, heads * width), 0, 1)
    fresh_dec = jnp.broadcast_to(dec_kv[None], (n, per_dec, row))
    mine_dec = jnp.concatenate([mine_dec, fresh_dec], axis=2).reshape(n, per, -1)
    mine = jnp.concatenate([mine, fresh, mine_dec], axis=2)
    got = lax.all_to_all(mine, "seq", split_axis=0, concat_axis=0, tiled=True)
    full = heads * width + row
    got_span = got[:, :, :full].reshape(span, full)
    got_dec = got[:, :, full:].reshape(rows_dec, full)
    absorbed, extra = absorb(got_span, got_dec, w_uk, row)
    new_rows = extra[:span]
    other = swap(absorbed, pair)

    blocks = [(jnp.int32(0), [keys])]
    for stride in near:
        blocks += [(offset ^ stride, [swap(x, stride) for x in held]) for offset, held in blocks]
    cuts = [keys[:, :size]] + list(split(keys, size, 1, extra))

    def spread(x):
        part = [(far, x)]
        for stride in near:
            part += [(offset ^ stride, swap(y, stride)) for offset, y in part]
        return part

    pieces = [swap(x, far) for x in cuts]

    target = jnp.where(owner == me, slot, -1)
    onehot = jnp.arange(pos_dev, dtype=jnp.int32)[None, :] == target[:, None]
    placed = lax.dot_general(
        new_rows,
        onehot.astype(jnp.bfloat16),
        (((0,), (0,)), ((), ())),
        preferred_element_type=jnp.float32,
    ).astype(jnp.bfloat16)
    new_cache = jnp.where(jnp.any(onehot, axis=0)[None, :], placed, keys).T

    limits = jnp.concatenate([jnp.arange(1, span + 1, dtype=jnp.int32), dec_len])
    index = jnp.arange(LANES, dtype=jnp.int32)
    queries = jnp.arange(count, dtype=jnp.int32)
    seen = (index[None, :] < span) & (index[None, :] < limits[:, None])
    seen |= (index[None, :] >= span) & (index[None, :] == queries[:, None])
    bias = jnp.where(seen, 0.0, HIDDEN).astype(jnp.float32)
    held = [offset for offset, _ in blocks]
    offsets = held + [offset ^ far for offset in held]
    which = jnp.stack([me ^ offset for offset in offsets])
    fills = jnp.sum(
        jnp.where(which[:, None] == jnp.arange(n, dtype=jnp.int32)[None, :], cache_fill[None, :], 0),
        axis=1,
    )
    base = len(blocks)
    tile = heads // 2 * count

    def stage_of(c, part):
        return [(c * size, base + i, x) for i, (_, x) in enumerate(part)]

    home = [(0, i, xs[0]) for i, (_, xs) in enumerate(blocks)]
    first = stage_of(0, spread(pieces[0]))
    state, pieces[1] = attend(
        fills, absorbed, home, new=(extra, bias), tile=tile, through=(pieces[1],)
    )
    first += stage_of(1, spread(pieces[1]))
    guest, pieces[2] = attend(fills, other, home, tile=tile, through=(pieces[2],))
    second = stage_of(2, spread(pieces[2]))
    guest, pieces[3] = attend(fills, other, first, state=guest, tile=tile, through=(pieces[3],))
    third = stage_of(3, spread(pieces[3]))
    second, third = second + third[:1], third[1:]
    state = attend(fills, absorbed, first, state=state, tile=tile)
    guest = attend(fills, other, second, state=guest, tile=tile)
    sent = attend(fills, other, third, state=guest, last=True)
    back = swap(sent, pair)
    state = attend(fills, absorbed, second, state=state, tile=tile)
    state = attend(fills, absorbed, third, state=state, tile=tile)
    span_out, dec_out = finish(count, span, state, back, w_uv)
    return (span_out, dec_out, new_cache)


def solution(mesh):
    in_specs = (
        P(("grp", "seq"), None),
        P(("grp", "seq"), None),
        P(("grp", "seq"), None),
        P(("grp", "seq"), None),
        P(("grp", "seq"), None),
        P("grp"),
        P("grp"),
        P("grp"),
        P("grp"),
        P("seq", None, None),
        P("seq", None, None),
    )
    out_specs = (P("grp", "seq"), P("grp", "seq"), P(("grp", "seq"), None))
    return jax.shard_map(body, mesh=mesh, in_specs=in_specs, out_specs=out_specs, check_vma=False)
```

```python
import functools

import jax
import jax.numpy as jnp
from jax import lax
from jax.experimental import pallas as pl
from jax.experimental.pallas import tpu as pltpu
from jax.sharding import PartitionSpec as P

DN = 128
DC = 512
LANES = 128
VMEM = 60 * 1024 * 1024

score_scale = 0.1353
LOG2E = 1.4426950408889634
HIDDEN = -1e30
FLOOR = -1e25


def lanes(x, width):
    return jnp.concatenate([x] * (width // LANES), axis=1) if width > LANES else x


def attend_kernel(pieces, extra, first, last, *refs):
    refs = list(refs)
    fills = refs.pop(0)
    q_ref = refs.pop(0)
    keys = [refs.pop(0) for _ in pieces]
    if extra:
        new_ref = refs.pop(0)
        bias_ref = refs.pop(0)
    if not first:
        m_in, l_in, acc_in = refs.pop(0), refs.pop(0), refs.pop(0)
    rows = q_ref.shape[0]
    q = q_ref[:, : keys[0].shape[0]]
    scores = []
    for (start, width, which), ref in zip(pieces, keys):
        s = jnp.dot(q, ref[...], preferred_element_type=jnp.float32)
        slot = start + lax.broadcasted_iota(jnp.int32, (1, width), 1)
        scores.append(jnp.where(slot < fills[which], s, HIDDEN))
    if extra:
        s = lax.dot_general(
            q, new_ref[...], (((1,), (1,)), ((), ())), preferred_element_type=jnp.float32
        )
        bias = bias_ref[...]
        scores.append(s + jnp.concatenate([bias] * (rows // bias.shape[0]), axis=0))
    peak = functools.reduce(jnp.maximum, [jnp.max(s, axis=1, keepdims=True) for s in scores])
    peak = jnp.maximum(peak, FLOOR)
    if not first:
        old = m_in[...]
        peak = jnp.maximum(peak, old[:, :1])
    scale = score_scale * LOG2E
    total = 0.0
    acc = 0.0
    for i, s in enumerate(scores):
        e = jnp.exp2((s - peak) * scale)
        total = total + jnp.sum(e, axis=1, keepdims=True)
        w = e.astype(jnp.bfloat16)
        if i < len(pieces):
            acc = acc + lax.dot_general(
                w, keys[i][:DC, :], (((1,), (1,)), ((), ())), preferred_element_type=jnp.float32
            )
        else:
            acc = acc + jnp.dot(w, new_ref[:, :DC], preferred_element_type=jnp.float32)
    if not first:
        keep = jnp.exp2((old[:, :1] - peak) * scale)
        total = total + l_in[:, :1] * keep
        acc = acc + acc_in[...] * keep
    if not last:
        m_out, l_out, acc_out = refs
        m_out[...] = jnp.broadcast_to(peak, (rows, LANES))
        l_out[...] = jnp.broadcast_to(total, (rows, LANES))
        acc_out[...] = acc
        return
    (out,) = refs
    out[:rows, :] = (acc * (1.0 / total)).astype(jnp.bfloat16)
    weight = jnp.broadcast_to(peak * scale + jnp.log2(total), (rows, LANES))
    tail = out.shape[0] - rows
    place = lax.broadcasted_iota(jnp.int32, (tail, LANES), 0)
    packed = jnp.zeros((tail, LANES), jnp.float32)
    for g in range(rows // LANES):
        turned = jnp.transpose(weight[g * LANES : (g + 1) * LANES, :])
        packed = jnp.where(place == g, turned[:tail, :], packed)
    high = packed.astype(jnp.bfloat16)
    rest = packed - high.astype(jnp.float32)
    mid = rest.astype(jnp.bfloat16)
    low = (rest - mid.astype(jnp.float32)).astype(jnp.bfloat16)
    out[rows:, :] = jnp.concatenate([high, mid, low, jnp.zeros_like(low)], axis=1)


def attend(fills, q, pieces, new=None, state=None, last=False, tile=None):
    rows, width = q.shape
    tile = rows if tile is None else tile
    spec = tuple((start, keys.shape[1], which) for start, which, keys in pieces)
    operands = [fills, q]
    in_specs = [
        pl.BlockSpec(memory_space=pltpu.SMEM),
        pl.BlockSpec((tile, width), lambda i: (i, 0)),
    ]
    for _, _, keys in pieces:
        operands.append(keys)
        in_specs.append(pl.BlockSpec(keys.shape, lambda i: (0, 0)))
    if new is not None:
        for x in new:
            operands.append(x)
            in_specs.append(pl.BlockSpec(x.shape, lambda i: (0, 0)))
    state_specs = [
        pl.BlockSpec((tile, LANES), lambda i: (i, 0)),
        pl.BlockSpec((tile, LANES), lambda i: (i, 0)),
        pl.BlockSpec((tile, DC), lambda i: (i, 0)),
    ]
    if state is not None:
        operands += list(state)
        in_specs += state_specs
    if last:
        tail = -(-rows // (LANES * 16)) * 16
        out_shape = [jax.ShapeDtypeStruct((rows + tail, DC), jnp.bfloat16)]
        out_specs = [pl.BlockSpec((rows + tail, DC), lambda i: (0, 0))]
    else:
        out_shape = [
            jax.ShapeDtypeStruct((rows, LANES), jnp.float32),
            jax.ShapeDtypeStruct((rows, LANES), jnp.float32),
            jax.ShapeDtypeStruct((rows, DC), jnp.float32),
        ]
        out_specs = list(state_specs)
    out = pl.pallas_call(
        functools.partial(attend_kernel, spec, new is not None, state is None, last),
        grid=(rows // tile,),
        in_specs=in_specs,
        out_specs=out_specs,
        out_shape=out_shape,
        compiler_params=pltpu.CompilerParams(vmem_limit_bytes=40 * 1024 * 1024),
        cost_estimate=pl.CostEstimate(
            flops=0, bytes_accessed=0, transcendentals=0
        ),
        name="attend",
    )(*operands)
    return out[0] if last else out


def after_kernel(x_ref, token_ref, out_ref):
    pass


def after(x, token):
    return pl.pallas_call(
        after_kernel,
        in_specs=[pl.BlockSpec(memory_space=pl.ANY)] * 2,
        out_specs=pl.BlockSpec(memory_space=pl.ANY),
        out_shape=jax.ShapeDtypeStruct(x.shape, x.dtype),
        input_output_aliases={0: 0},
        compiler_params=pltpu.CompilerParams(vmem_limit_bytes=VMEM),
        name="after",
    )(x, token)


def pack_kernel(query_ref, dec_ref, span_kv_ref, dec_kv_ref, out_ref):
    n, per, _ = out_ref.shape
    row = span_kv_ref.shape[1]
    per_dec = dec_ref.shape[0]
    part = query_ref.shape[1] // n
    cut = part // per
    pad = -(-row // LANES) * LANES - row

    def padded(ref):
        x = ref[...].astype(jnp.float32)
        return jnp.concatenate([x, jnp.zeros((x.shape[0], pad), jnp.float32)], axis=1)

    fresh = padded(span_kv_ref)
    dec_kv = padded(dec_kv_ref)
    tail = [fresh]
    for e in range(per_dec):
        for j in range(0, row + pad, per * LANES):
            strips = [dec_kv[e : e + 1, k : k + LANES] for k in range(j, min(j + per * LANES, row + pad), LANES)]
            strips += [jnp.zeros((1, LANES), jnp.float32)] * (per - len(strips))
            tail.append(jnp.concatenate(strips, axis=0))
    tail = jnp.concatenate(tail, axis=1).astype(jnp.bfloat16)
    for d in range(n):
        out_ref[d, :, :part] = query_ref[:, d * part : (d + 1) * part]
        for e in range(per_dec):
            strips = dec_ref[e : e + 1, d * part : (d + 1) * part].astype(jnp.float32)
            strips = [strips[:, i * cut : (i + 1) * cut] for i in range(per)]
            at = part + e * cut
            out_ref[d, :, at : at + cut] = jnp.concatenate(strips, axis=0).astype(jnp.bfloat16)
        out_ref[d, :, part + per_dec * cut :] = tail


def pack(n, query, dec_query, span_kv, dec_kv):
    per, row = span_kv.shape
    per_dec = dec_kv.shape[0]
    part = query.shape[1] // n
    wide = -(-row // LANES) * LANES
    fold = -(-wide // (per * LANES)) * LANES
    total = part + per_dec * (part // per) + wide + per_dec * fold
    operands = (query, dec_query, span_kv, dec_kv)
    return pl.pallas_call(
        pack_kernel,
        grid=(1,),
        in_specs=[pl.BlockSpec(x.shape, lambda i: (0, 0)) for x in operands],
        out_specs=pl.BlockSpec((n, per, total), lambda i: (0, 0, 0)),
        out_shape=jax.ShapeDtypeStruct((n, per, total), jnp.bfloat16),
        compiler_params=pltpu.CompilerParams(vmem_limit_bytes=VMEM),
        name="pack",
    )(*operands)


def absorb_kernel(per_dec, got_ref, w_ref, absorbed_ref, extra_ref):
    heads = w_ref.shape[0]
    n, per, _ = got_ref.shape
    row = extra_ref.shape[1]
    count = absorbed_ref.shape[0] // heads
    wide = -(-row // LANES) * LANES
    fold = -(-wide // (per * LANES)) * LANES
    part = (got_ref.shape[2] - wide - per_dec * fold) * per // (per + per_dec)
    width = part // heads
    cut = part // per
    at = part + per_dec * cut

    def unfold(x, length):
        strips = []
        for j in range(0, x.shape[1], length):
            strips += [x[i : i + 1, j : j + length] for i in range(per)]
        return jnp.concatenate(strips, axis=1)

    blocks = [got_ref[d].astype(jnp.float32) for d in range(n)]
    queries = [x[:, :part] for x in blocks]
    fresh = [x[:, at : at + wide] for x in blocks]
    for x in blocks:
        for e in range(per_dec):
            queries.append(unfold(x[:, part + e * cut : part + (e + 1) * cut], cut))
            begin = at + wide + e * fold
            fresh.append(unfold(x[:, begin : begin + fold], LANES)[:, :wide])
    q = jnp.concatenate(queries, axis=0).astype(jnp.bfloat16)
    new = jnp.concatenate(fresh, axis=0)
    blank = jnp.zeros((count, absorbed_ref.shape[1] - row), jnp.float32)
    for h in range(0, heads, 2):
        parts = []
        for g in (h, h + 1):
            mine = q[:, g * width : (g + 1) * width]
            latent = jnp.dot(mine[:, :DN], w_ref[g], preferred_element_type=jnp.float32)
            rope = mine[:, DN:].astype(jnp.float32)
            parts.append(jnp.concatenate([latent, rope, blank], axis=1))
        pair = jnp.concatenate(parts, axis=0).astype(jnp.bfloat16)
        absorbed_ref[h * count : (h + 2) * count, :] = pair
    blank = jnp.zeros((extra_ref.shape[0] - count, row), jnp.float32)
    extra_ref[...] = jnp.concatenate([new[:, :row], blank], axis=0).astype(jnp.bfloat16)


def absorb(count, per_dec, got, w_uk, row):
    heads = w_uk.shape[0]
    return pl.pallas_call(
        functools.partial(absorb_kernel, per_dec),
        out_shape=(
            jax.ShapeDtypeStruct((heads * count, -(-row // LANES) * LANES), jnp.bfloat16),
            jax.ShapeDtypeStruct((LANES, row), jnp.bfloat16),
        ),
        compiler_params=pltpu.CompilerParams(vmem_limit_bytes=40 * 1024 * 1024),
        cost_estimate=pl.CostEstimate(
            flops=2 * count * heads * DN * DC,
            bytes_accessed=2 * w_uk.size + 2 * got.size,
            transcendentals=0,
        ),
        name="absorb",
    )(got, w_uk)


def split_kernel(spans, x_ref, after_ref, *out_refs):
    for (a, b), ref in zip(spans, out_refs):
        ref[...] = x_ref[:, a:b]


def split(x, spans, after):
    return pl.pallas_call(
        functools.partial(split_kernel, spans),
        grid=(1,),
        in_specs=[
            pl.BlockSpec(x.shape, lambda i: (0, 0)),
            pl.BlockSpec(memory_space=pl.ANY),
        ],
        out_specs=[pl.BlockSpec((x.shape[0], b - a), lambda i: (0, 0)) for a, b in spans],
        out_shape=[jax.ShapeDtypeStruct((x.shape[0], b - a), x.dtype) for a, b in spans],
        compiler_params=pltpu.CompilerParams(vmem_limit_bytes=VMEM),
        name="split",
    )(x, after)


def finish_kernel(count, m_ref, l_ref, acc_ref, far_ref, w_ref, span_ref, dec_ref):
    rows = m_ref.shape[0]
    heads = w_ref.shape[0]
    scale = score_scale * LOG2E
    parts = far_ref[rows:, :].astype(jnp.float32)
    packed = parts[:, :LANES] + parts[:, LANES : 2 * LANES] + parts[:, 2 * LANES : 3 * LANES]
    columns = []
    for g in range(rows // LANES):
        row = jnp.broadcast_to(packed[g : g + 1, :], (LANES, LANES))
        columns.append(jnp.transpose(row))
    far = jnp.concatenate(columns, axis=0)
    near = m_ref[...] * scale
    top = jnp.maximum(near, far)
    w_near = jnp.exp2(near - top)
    w_far = jnp.exp2(far - top)
    total = l_ref[...] * w_near + w_far
    inverse = 1.0 / total
    w_near = lanes(w_near * inverse, DC)
    w_far = lanes(w_far * inverse, DC)
    for h in range(heads):
        a, b = h * count, (h + 1) * count
        near_part = acc_ref[a:b, :] * w_near[a:b, :]
        far_part = far_ref[:rows, :].astype(jnp.float32)[a:b, :] * w_far[a:b, :]
        latent = (near_part + far_part).astype(jnp.bfloat16)
        done = jnp.dot(latent, w_ref[h], preferred_element_type=jnp.float32)
        span = span_ref.shape[0]
        span_ref[:, h * LANES : (h + 1) * LANES] = done[:span].astype(jnp.bfloat16)
        dec_ref[:, h * LANES : (h + 1) * LANES] = done[span:].astype(jnp.bfloat16)


def finish(count, span, state, far, w_uv):
    heads = w_uv.shape[0]
    wide = heads * w_uv.shape[2]
    return pl.pallas_call(
        functools.partial(finish_kernel, count),
        out_shape=(
            jax.ShapeDtypeStruct((span, wide), jnp.bfloat16),
            jax.ShapeDtypeStruct((count - span, wide), jnp.bfloat16),
        ),
        compiler_params=pltpu.CompilerParams(vmem_limit_bytes=40 * 1024 * 1024),
        cost_estimate=pl.CostEstimate(
            flops=2 * count * heads * DC * w_uv.shape[2],
            bytes_accessed=2 * w_uv.size + 6 * state[2].size,
            transcendentals=0,
        ),
        name="finish",
    )(*state, far, w_uv)


def body(query, dec_query, cache_kv, span_kv, dec_kv, cache_fill, owner, slot, dec_len, w_uk, w_uv):
    me = lax.axis_index("seq")
    n = lax.axis_size("seq")
    pos_dev = cache_kv.shape[0]
    span = owner.shape[0]
    rows_dec = dec_len.shape[0]
    count = span + rows_dec
    heads = w_uk.shape[0]
    row = cache_kv.shape[1]

    def swap(x, stride):
        return lax.ppermute(x, "seq", [(i, i ^ stride) for i in range(n)])

    far, pair = n // 2, n // 4
    near = [1 << b for b in range(pair.bit_length() - 1)]
    keys = cache_kv.T
    eighth = pos_dev // 8
    edges = [0, 2 * eighth, 5 * eighth, 7 * eighth, pos_dev]

    mine = pack(n, query, dec_query, span_kv, dec_kv)
    got = lax.all_to_all(mine, "seq", split_axis=0, concat_axis=0, tiled=True)
    absorbed, extra = absorb(count, rows_dec // n, got, w_uk, row)
    new_rows = extra[:span]
    other = swap(absorbed, pair)

    lead = keys[:, : edges[1]]
    *pieces, rest = split(
        keys, [*zip(edges[1:], edges[2:]), (edges[1], pos_dev)], extra
    )
    blocks = [(0, [lead, rest])]
    for stride in near:
        blocks += [(offset ^ stride, [swap(x, stride) for x in held]) for offset, held in blocks]
    pieces = [swap(x, far) for x in [lead, *pieces]]

    def spread(x):
        part = [(far, x)]
        for stride in near:
            part += [(offset ^ stride, swap(y, stride)) for offset, y in part]
        return part

    target = jnp.where(owner == me, slot, -1)
    onehot = jnp.arange(pos_dev, dtype=jnp.int32)[None, :] == target[:, None]
    placed = lax.dot_general(
        new_rows,
        onehot.astype(jnp.bfloat16),
        (((0,), (0,)), ((), ())),
        preferred_element_type=jnp.float32,
    ).astype(jnp.bfloat16)
    new_cache = jnp.where(jnp.any(onehot, axis=0)[None, :], placed, keys).T

    limits = jnp.concatenate([jnp.arange(1, span + 1, dtype=jnp.int32), dec_len])
    index = jnp.arange(LANES, dtype=jnp.int32)
    queries = jnp.arange(count, dtype=jnp.int32)
    seen = (index[None, :] < span) & (index[None, :] < limits[:, None])
    seen |= (index[None, :] >= span) & (index[None, :] == queries[:, None])
    bias = jnp.where(seen, 0.0, HIDDEN).astype(jnp.float32)
    held = [offset for offset, _ in blocks]
    offsets = held + [offset ^ far for offset in held]
    which = jnp.stack([me ^ offset for offset in offsets])
    fills = jnp.sum(
        jnp.where(which[:, None] == jnp.arange(n, dtype=jnp.int32)[None, :], cache_fill[None, :], 0),
        axis=1,
    )
    base = len(blocks)
    tile = heads // 2 * count

    def stage_of(c, part):
        return [(edges[c], base + i, x) for i, (_, x) in enumerate(part)]

    home = [(0, 0, keys)]
    for i, (_, (x, y)) in enumerate(blocks[1:], 1):
        home += [(0, i, x), (edges[1], i, y)]
    state = attend(fills, absorbed, home, new=(extra, bias), tile=tile)
    first = stage_of(0, spread(pieces[0]))
    first += stage_of(1, spread(after(pieces[1], state[0])))
    guest = attend(fills, other, home, tile=tile)
    second = stage_of(2, spread(after(pieces[2], guest[0])))
    guest = attend(fills, other, first, state=guest, tile=tile)
    state = attend(fills, absorbed, first, state=state, tile=tile)
    third = stage_of(3, spread(after(after(pieces[3], guest[0]), state[0])))
    second, third = second + third[:1], third[1:]
    guest = attend(fills, other, second, state=guest, tile=tile)
    sent = attend(fills, other, third, state=guest, last=True)
    back = swap(sent, pair)
    state = attend(fills, absorbed, second, state=state, tile=tile)
    state = attend(fills, absorbed, third, state=state, tile=tile)
    span_out, dec_out = finish(count, span, state, back, w_uv)
    return (span_out, dec_out, new_cache)


def solution(mesh):
    in_specs = (
        P(("grp", "seq"), None),
        P(("grp", "seq"), None),
        P(("grp", "seq"), None),
        P(("grp", "seq"), None),
        P(("grp", "seq"), None),
        P("grp"),
        P("grp"),
        P("grp"),
        P("grp"),
        P("seq", None, None),
        P("seq", None, None),
    )
    out_specs = (P("grp", "seq"), P("grp", "seq"), P(("grp", "seq"), None))
    return jax.shard_map(body, mesh=mesh, in_specs=in_specs, out_specs=out_specs, check_vma=False)
```

```python
import functools

import jax
import jax.numpy as jnp
from jax import lax
from jax.experimental import pallas as pl
from jax.experimental.pallas import tpu as pltpu
from jax.sharding import PartitionSpec as P

DN = 128
DC = 512
LANES = 128
ANY = pl.BlockSpec(memory_space=pl.ANY)
WHOLE = pl.BlockSpec(memory_space=pltpu.VMEM)


def room(mebibytes):
    return pltpu.CompilerParams(vmem_limit_bytes=mebibytes * 1024 * 1024)

score_scale = 0.1353
LOG2E = 1.4426950408889634
HIDDEN = -1e30
FLOOR = -1e25


def lanes(x, width):
    return jnp.concatenate([x] * (width // LANES), axis=1) if width > LANES else x


def attend_kernel(pieces, extra, first, last, tile, *refs):
    refs = list(refs)
    fills = refs.pop(0)
    q_ref = refs.pop(0)
    keys = [refs.pop(0) for _ in pieces]
    if extra:
        new_ref = refs.pop(0)
        bias_ref = refs.pop(0)
    if not first:
        m_in, l_in, acc_in = refs.pop(0), refs.pop(0), refs.pop(0)
    scale = score_scale * LOG2E
    weights = []
    for at in range(0, q_ref.shape[0], tile):
        rows = slice(at, at + tile)
        q = q_ref[rows, : keys[0].shape[0]]
        scores = []
        for (start, width, which), ref in zip(pieces, keys):
            s = jnp.dot(q, ref[...], preferred_element_type=jnp.float32)
            slot = start + lax.broadcasted_iota(jnp.int32, (1, width), 1)
            scores.append(jnp.where(slot < fills[which], s, HIDDEN))
        if extra:
            s = lax.dot_general(
                q, new_ref[...], (((1,), (1,)), ((), ())), preferred_element_type=jnp.float32
            )
            bias = bias_ref[...]
            scores.append(s + jnp.concatenate([bias] * (tile // bias.shape[0]), axis=0))
        peak = functools.reduce(jnp.maximum, [jnp.max(s, axis=1, keepdims=True) for s in scores])
        peak = jnp.maximum(peak, FLOOR)
        if not first:
            old = m_in[rows, :1]
            peak = jnp.maximum(peak, old)
        total = 0.0
        acc = 0.0
        for i, s in enumerate(scores):
            e = jnp.exp2((s - peak) * scale)
            total = total + jnp.sum(e, axis=1, keepdims=True)
            w = e.astype(jnp.bfloat16)
            if i < len(pieces):
                acc = acc + lax.dot_general(
                    w, keys[i][:DC, :], (((1,), (1,)), ((), ())), preferred_element_type=jnp.float32
                )
            else:
                acc = acc + jnp.dot(w, new_ref[:, :DC], preferred_element_type=jnp.float32)
        if not first:
            keep = jnp.exp2((old - peak) * scale)
            total = total + l_in[rows, :1] * keep
            acc = acc + acc_in[rows, :] * keep
        if last:
            refs[0][rows, :] = (acc * (1.0 / total)).astype(jnp.bfloat16)
            weights.append(jnp.broadcast_to(peak * scale + jnp.log2(total), (tile, LANES)))
        else:
            m_out, l_out, acc_out = refs
            m_out[rows, :] = jnp.broadcast_to(peak, (tile, LANES))
            l_out[rows, :] = jnp.broadcast_to(total, (tile, LANES))
            acc_out[rows, :] = acc
    if not last:
        return
    out = refs[0]
    count = q_ref.shape[0]
    weight = jnp.concatenate(weights, axis=0)
    tail = out.shape[0] - count
    place = lax.broadcasted_iota(jnp.int32, (tail, LANES), 0)
    packed = jnp.zeros((tail, LANES), jnp.float32)
    for g in range(count // LANES):
        turned = jnp.transpose(weight[g * LANES : (g + 1) * LANES, :])
        packed = jnp.where(place == g, turned[:tail, :], packed)
    high = packed.astype(jnp.bfloat16)
    rest = packed - high.astype(jnp.float32)
    mid = rest.astype(jnp.bfloat16)
    low = (rest - mid.astype(jnp.float32)).astype(jnp.bfloat16)
    out[count:, :] = jnp.concatenate([high, mid, low, jnp.zeros_like(low)], axis=1)


def attend(fills, q, pieces, tile, new=None, state=None, last=False):
    rows = q.shape[0]
    spec = tuple((start, keys.shape[1], which) for start, which, keys in pieces)
    operands = [fills, q] + [keys for _, _, keys in pieces]
    if new is not None:
        operands += list(new)
    aliases = {}
    if state is not None:
        if not last:
            aliases = {len(operands) + i: i for i in range(3)}
        operands += list(state)
    if last:
        tail = -(-rows // (LANES * 16)) * 16
        out_shape = [jax.ShapeDtypeStruct((rows + tail, DC), jnp.bfloat16)]
    else:
        out_shape = [
            jax.ShapeDtypeStruct((rows, LANES), jnp.float32),
            jax.ShapeDtypeStruct((rows, LANES), jnp.float32),
            jax.ShapeDtypeStruct((rows, DC), jnp.float32),
        ]
    out = pl.pallas_call(
        functools.partial(attend_kernel, spec, new is not None, state is None, last, tile),
        in_specs=[pl.BlockSpec(memory_space=pltpu.SMEM)] + [WHOLE] * (len(operands) - 1),
        out_specs=[WHOLE] * len(out_shape),
        out_shape=out_shape,
        input_output_aliases=aliases,
        compiler_params=room(24),
        cost_estimate=pl.CostEstimate(flops=0, bytes_accessed=0, transcendentals=0),
        name="attend",
    )(*operands)
    return out[0] if last else out


def after_kernel(x_ref, *refs):
    pass


def after(x, *tokens):
    return pl.pallas_call(
        after_kernel,
        in_specs=[ANY] * (1 + len(tokens)),
        out_specs=ANY,
        out_shape=jax.ShapeDtypeStruct(x.shape, x.dtype),
        input_output_aliases={0: 0},
        compiler_params=room(1),
        name="after",
    )(x, *tokens)


def pack_kernel(n, me_ref, query_ref, dec_ref, span_kv_ref, dec_kv_ref, *out_refs):
    per, row = span_kv_ref.shape
    per_dec = dec_ref.shape[0]
    part = query_ref.shape[1] // n
    cut = part // per
    pad = -(-row // LANES) * LANES - row

    def padded(ref):
        x = ref[...].astype(jnp.float32)
        return jnp.concatenate([x, jnp.zeros((x.shape[0], pad), jnp.float32)], axis=1)

    dec_kv = padded(dec_kv_ref)
    tail = [padded(span_kv_ref)]
    for e in range(per_dec):
        for j in range(0, row + pad, per * LANES):
            ends = range(j, min(j + per * LANES, row + pad), LANES)
            strips = [dec_kv[e : e + 1, k : k + LANES] for k in ends]
            strips += [jnp.zeros((1, LANES), jnp.float32)] * (per - len(strips))
            tail.append(jnp.concatenate(strips, axis=0))
    tail = jnp.concatenate(tail, axis=1).astype(jnp.bfloat16)
    for r, out_ref in enumerate(out_refs):
        begin = (me_ref[0] ^ r) * part
        out_ref[:, :part] = query_ref[:, pl.ds(pl.multiple_of(begin, LANES), part)]
        for e in range(per_dec):
            strips = []
            for i in range(per):
                at = pl.multiple_of(begin + i * cut, LANES)
                strips.append(dec_ref[e : e + 1, pl.ds(at, cut)].astype(jnp.float32))
            at = part + e * cut
            out_ref[:, at : at + cut] = jnp.concatenate(strips, axis=0).astype(jnp.bfloat16)
        out_ref[:, part + per_dec * cut :] = tail


def pack(n, me, query, dec_query, span_kv, dec_kv):
    per, row = span_kv.shape
    per_dec = dec_kv.shape[0]
    part = query.shape[1] // n
    wide = -(-row // LANES) * LANES
    fold = -(-wide // (per * LANES)) * LANES
    total = part + per_dec * (part // per) + wide + per_dec * fold
    operands = (query, dec_query, span_kv, dec_kv)
    return pl.pallas_call(
        functools.partial(pack_kernel, n),
        grid=(1,),
        in_specs=[pl.BlockSpec(memory_space=pltpu.SMEM)]
        + [pl.BlockSpec(x.shape, lambda i: (0, 0)) for x in operands],
        out_specs=[pl.BlockSpec((per, total), lambda i: (0, 0))] * n,
        out_shape=[jax.ShapeDtypeStruct((per, total), jnp.bfloat16)] * n,
        compiler_params=room(60),
        name="pack",
    )(me, *operands)


def absorb_kernel(per_dec, n, me_ref, w_ref, *refs):
    got_refs, absorbed_ref, extra_ref, placed = refs[:n], refs[n], refs[n + 1], refs[n + 2]
    heads = w_ref.shape[0]
    per = got_refs[0].shape[0]
    row = extra_ref.shape[1]
    count = absorbed_ref.shape[0] // heads
    wide = -(-row // LANES) * LANES
    fold = -(-wide // (per * LANES)) * LANES
    part = (got_refs[0].shape[1] - wide - per_dec * fold) * per // (per + per_dec)
    width = part // heads
    cut = part // per
    at = part + per_dec * cut
    for r, ref in enumerate(got_refs):
        placed[me_ref[0] ^ r] = ref[...].astype(jnp.float32)

    def unfold(x, length):
        strips = []
        for j in range(0, x.shape[1], length):
            strips += [x[i : i + 1, j : j + length] for i in range(per)]
        return jnp.concatenate(strips, axis=1)

    blocks = [placed[d] for d in range(n)]
    queries = [x[:, :part] for x in blocks]
    fresh = [x[:, at : at + wide] for x in blocks]
    for x in blocks:
        for e in range(per_dec):
            queries.append(unfold(x[:, part + e * cut : part + (e + 1) * cut], cut))
            begin = at + wide + e * fold
            fresh.append(unfold(x[:, begin : begin + fold], LANES)[:, :wide])
    q = jnp.concatenate(queries, axis=0).astype(jnp.bfloat16)
    new = jnp.concatenate(fresh, axis=0)
    blank = jnp.zeros((count, absorbed_ref.shape[1] - row), jnp.float32)
    for h in range(0, heads, 2):
        parts = []
        for g in (h, h + 1):
            mine = q[:, g * width : (g + 1) * width]
            latent = jnp.dot(mine[:, :DN], w_ref[g], preferred_element_type=jnp.float32)
            rope = mine[:, DN:].astype(jnp.float32)
            parts.append(jnp.concatenate([latent, rope, blank], axis=1))
        pair = jnp.concatenate(parts, axis=0).astype(jnp.bfloat16)
        absorbed_ref[h * count : (h + 2) * count, :] = pair
    blank = jnp.zeros((extra_ref.shape[0] - count, row), jnp.float32)
    extra_ref[...] = jnp.concatenate([new[:, :row], blank], axis=0).astype(jnp.bfloat16)


def absorb(count, per_dec, me, got, w_uk, row):
    heads = w_uk.shape[0]
    return pl.pallas_call(
        functools.partial(absorb_kernel, per_dec, len(got)),
        in_specs=[pl.BlockSpec(memory_space=pltpu.SMEM)] + [WHOLE] * (1 + len(got)),
        out_shape=(
            jax.ShapeDtypeStruct((heads * count, -(-row // LANES) * LANES), jnp.bfloat16),
            jax.ShapeDtypeStruct((LANES, row), jnp.bfloat16),
        ),
        scratch_shapes=[pltpu.VMEM((len(got), *got[0].shape), jnp.float32)],
        compiler_params=room(24),
        cost_estimate=pl.CostEstimate(
            flops=2 * count * heads * DN * DC,
            bytes_accessed=2 * w_uk.size,
            transcendentals=0,
        ),
        name="absorb",
    )(me, w_uk, *got)


def split_kernel(spans, x_ref, *refs):
    for (a, b), ref in zip(spans, refs[-len(spans) :]):
        ref[...] = x_ref[:, a:b]


def split(x, spans, tokens):
    return pl.pallas_call(
        functools.partial(split_kernel, spans),
        grid=(1,),
        in_specs=[pl.BlockSpec(x.shape, lambda i: (0, 0))] + [ANY] * len(tokens),
        out_specs=[pl.BlockSpec((x.shape[0], b - a), lambda i: (0, 0)) for a, b in spans],
        out_shape=[jax.ShapeDtypeStruct((x.shape[0], b - a), x.dtype) for a, b in spans],
        compiler_params=room(16),
        name="split",
    )(x, *tokens)


def finish_kernel(count, m_ref, l_ref, acc_ref, far_ref, w_ref, span_ref, dec_ref):
    rows = m_ref.shape[0]
    heads = w_ref.shape[0]
    scale = score_scale * LOG2E
    parts = far_ref[rows:, :].astype(jnp.float32)
    packed = parts[:, :LANES] + parts[:, LANES : 2 * LANES] + parts[:, 2 * LANES : 3 * LANES]
    columns = []
    for g in range(rows // LANES):
        row = jnp.broadcast_to(packed[g : g + 1, :], (LANES, LANES))
        columns.append(jnp.transpose(row))
    far = jnp.concatenate(columns, axis=0)
    near = m_ref[...] * scale
    top = jnp.maximum(near, far)
    w_near = jnp.exp2(near - top)
    w_far = jnp.exp2(far - top)
    total = l_ref[...] * w_near + w_far
    inverse = 1.0 / total
    w_near = lanes(w_near * inverse, DC)
    w_far = lanes(w_far * inverse, DC)
    for h in range(heads):
        a, b = h * count, (h + 1) * count
        near_part = acc_ref[a:b, :] * w_near[a:b, :]
        far_part = far_ref[:rows, :].astype(jnp.float32)[a:b, :] * w_far[a:b, :]
        latent = (near_part + far_part).astype(jnp.bfloat16)
        done = jnp.dot(latent, w_ref[h], preferred_element_type=jnp.float32)
        span = span_ref.shape[0]
        span_ref[:, h * LANES : (h + 1) * LANES] = done[:span].astype(jnp.bfloat16)
        dec_ref[:, h * LANES : (h + 1) * LANES] = done[span:].astype(jnp.bfloat16)


def finish(count, span, state, far, w_uv):
    heads = w_uv.shape[0]
    wide = heads * w_uv.shape[2]
    return pl.pallas_call(
        functools.partial(finish_kernel, count),
        out_shape=(
            jax.ShapeDtypeStruct((span, wide), jnp.bfloat16),
            jax.ShapeDtypeStruct((count - span, wide), jnp.bfloat16),
        ),
        compiler_params=room(24),
        cost_estimate=pl.CostEstimate(
            flops=2 * count * heads * DC * w_uv.shape[2],
            bytes_accessed=2 * w_uv.size + 6 * state[2].size,
            transcendentals=0,
        ),
        name="finish",
    )(*state, far, w_uv)


def body(query, dec_query, cache_kv, span_kv, dec_kv, cache_fill, owner, slot, dec_len, w_uk, w_uv):
    me = lax.axis_index("seq")
    n = lax.axis_size("seq")
    pos_dev = cache_kv.shape[0]
    span = owner.shape[0]
    rows_dec = dec_len.shape[0]
    count = span + rows_dec
    heads = w_uk.shape[0]
    row = cache_kv.shape[1]

    def swap(x, stride):
        return lax.ppermute(x, "seq", [(i, i ^ stride) for i in range(n)])

    far, pair = n // 2, n // 4
    near = [1 << b for b in range(pair.bit_length() - 1)]
    keys = cache_kv.T
    edges = [0, pos_dev // 2, pos_dev // 8 * 7, pos_dev]

    place = me[None].astype(jnp.int32)
    mine = pack(n, place, query, dec_query, span_kv, dec_kv)
    got = [mine[0]] + [swap(x, r) for r, x in enumerate(mine) if r]
    absorbed, extra = absorb(count, rows_dec // n, place, got, w_uk, row)
    new_rows = extra[:span]
    other = swap(absorbed, pair)

    *cuts, copy = split(keys, [*zip(edges, edges[1:]), (0, pos_dev)], got[1:])
    blocks = [(0, copy)]
    for stride in near:
        blocks += [(offset ^ stride, swap(x, stride)) for offset, x in blocks]
    pieces = [swap(cuts[0], far)]

    def spread(x):
        part = [(far, x)]
        for stride in near:
            part += [(offset ^ stride, swap(y, stride)) for offset, y in part]
        return part

    target = jnp.where(owner == me, slot, -1)
    onehot = jnp.arange(pos_dev, dtype=jnp.int32)[None, :] == target[:, None]
    placed = lax.dot_general(
        new_rows,
        onehot.astype(jnp.bfloat16),
        (((0,), (0,)), ((), ())),
        preferred_element_type=jnp.float32,
    ).astype(jnp.bfloat16)
    new_cache = jnp.where(jnp.any(onehot, axis=0)[None, :], placed, keys).T

    limits = jnp.concatenate([jnp.arange(1, span + 1, dtype=jnp.int32), dec_len])
    index = jnp.arange(LANES, dtype=jnp.int32)
    queries = jnp.arange(count, dtype=jnp.int32)
    seen = (index[None, :] < span) & (index[None, :] < limits[:, None])
    seen |= (index[None, :] >= span) & (index[None, :] == queries[:, None])
    bias = jnp.where(seen, 0.0, HIDDEN).astype(jnp.float32)
    held = [offset for offset, _ in blocks]
    offsets = held + [offset ^ far for offset in held]
    which = jnp.stack([me ^ offset for offset in offsets])
    fills = jnp.sum(
        jnp.where(which[:, None] == jnp.arange(n, dtype=jnp.int32)[None, :], cache_fill[None, :], 0),
        axis=1,
    )
    base = len(blocks)
    tile = heads // 2 * count

    def stage_of(c, part):
        return [(edges[c], base + i, x) for i, (_, x) in enumerate(part)]

    home = [(0, 0, keys)]
    side = [(0, i, x) for i, (_, x) in enumerate(blocks) if i]
    state = attend(fills, absorbed, home, tile, new=(extra, bias))
    pieces.append(swap(after(cuts[1], state[0], pieces[0]), far))
    first = stage_of(0, spread(after(pieces[0], state[0])))
    state = attend(fills, absorbed, side, tile, state=state)
    other = after(other, state[0])
    guest = attend(fills, other, home + side, tile)
    pieces.append(swap(after(cuts[2], guest[0], pieces[1]), far))
    second = stage_of(1, spread(after(pieces[1], guest[0])))
    guest = attend(fills, other, first, tile, state=guest)
    state = attend(fills, absorbed, first, tile, state=state)
    third = stage_of(2, spread(after(pieces[2], guest[0], state[0])))
    second, third = second + third[:1], third[1:]
    guest = attend(fills, other, second, tile, state=guest)
    sent = attend(fills, other, third, tile, state=guest, last=True)
    back = swap(sent, pair)
    state = attend(fills, absorbed, second + third, tile, state=state)
    span_out, dec_out = finish(count, span, state, back, w_uv)
    return (span_out, dec_out, new_cache)


def solution(mesh):
    in_specs = (
        P(("grp", "seq"), None),
        P(("grp", "seq"), None),
        P(("grp", "seq"), None),
        P(("grp", "seq"), None),
        P(("grp", "seq"), None),
        P("grp"),
        P("grp"),
        P("grp"),
        P("grp"),
        P("seq", None, None),
        P("seq", None, None),
    )
    out_specs = (P("grp", "seq"), P("grp", "seq"), P(("grp", "seq"), None))
    return jax.shard_map(body, mesh=mesh, in_specs=in_specs, out_specs=out_specs, check_vma=False)
```

```python
import functools

import jax
import jax.numpy as jnp
from jax import lax
from jax.experimental import pallas as pl
from jax.experimental.pallas import tpu as pltpu
from jax.sharding import PartitionSpec as P

DN = 128
DC = 512
LANES = 128
ANY = pl.BlockSpec(memory_space=pl.ANY)
WHOLE = pl.BlockSpec(memory_space=pltpu.VMEM)


def room(mebibytes):
    return pltpu.CompilerParams(vmem_limit_bytes=mebibytes * 1024 * 1024)

score_scale = 0.1353
LOG2E = 1.4426950408889634
HIDDEN = -1e30
FLOOR = -1e25


def lanes(x, width):
    return jnp.concatenate([x] * (width // LANES), axis=1) if width > LANES else x


def attend_kernel(pieces, extra, first, last, tile, *refs):
    refs = list(refs)
    fills = refs.pop(0)
    q_ref = refs.pop(0)
    keys = [refs.pop(0) for _ in pieces]
    if extra:
        new_ref = refs.pop(0)
        bias_ref = refs.pop(0)
    if not first:
        m_in, l_in, acc_in = refs.pop(0), refs.pop(0), refs.pop(0)
    scale = score_scale * LOG2E
    weights = []
    for at in range(0, q_ref.shape[0], tile):
        rows = slice(at, at + tile)
        q = q_ref[rows, : keys[0].shape[0]]
        scores = []
        for (start, width, which), ref in zip(pieces, keys):
            s = jnp.dot(q, ref[...], preferred_element_type=jnp.float32)
            slot = start + lax.broadcasted_iota(jnp.int32, (1, width), 1)
            scores.append(jnp.where(slot < fills[which], s, HIDDEN))
        if extra:
            s = lax.dot_general(
                q, new_ref[...], (((1,), (1,)), ((), ())), preferred_element_type=jnp.float32
            )
            bias = bias_ref[...]
            scores.append(s + jnp.concatenate([bias] * (tile // bias.shape[0]), axis=0))
        peak = functools.reduce(jnp.maximum, [jnp.max(s, axis=1, keepdims=True) for s in scores])
        peak = jnp.maximum(peak, FLOOR)
        if not first:
            old = m_in[rows, :1]
            peak = jnp.maximum(peak, old)
        total = 0.0
        acc = 0.0
        for i, s in enumerate(scores):
            e = jnp.exp2((s - peak) * scale)
            total = total + jnp.sum(e, axis=1, keepdims=True)
            w = e.astype(jnp.bfloat16)
            if i < len(pieces):
                acc = acc + lax.dot_general(
                    w, keys[i][:DC, :], (((1,), (1,)), ((), ())), preferred_element_type=jnp.float32
                )
            else:
                acc = acc + jnp.dot(w, new_ref[:, :DC], preferred_element_type=jnp.float32)
        if not first:
            keep = jnp.exp2((old - peak) * scale)
            total = total + l_in[rows, :1] * keep
            acc = acc + acc_in[rows, :] * keep
        if last:
            refs[0][rows, :] = (acc * (1.0 / total)).astype(jnp.bfloat16)
            weights.append(jnp.broadcast_to(peak * scale + jnp.log2(total), (tile, LANES)))
        else:
            m_out, l_out, acc_out = refs
            m_out[rows, :] = jnp.broadcast_to(peak, (tile, LANES))
            l_out[rows, :] = jnp.broadcast_to(total, (tile, LANES))
            acc_out[rows, :] = acc
    if not last:
        return
    out = refs[0]
    count = q_ref.shape[0]
    weight = jnp.concatenate(weights, axis=0)
    tail = out.shape[0] - count
    place = lax.broadcasted_iota(jnp.int32, (tail, LANES), 0)
    packed = jnp.zeros((tail, LANES), jnp.float32)
    for g in range(count // LANES):
        turned = jnp.transpose(weight[g * LANES : (g + 1) * LANES, :])
        packed = jnp.where(place == g, turned[:tail, :], packed)
    high = packed.astype(jnp.bfloat16)
    rest = packed - high.astype(jnp.float32)
    mid = rest.astype(jnp.bfloat16)
    low = (rest - mid.astype(jnp.float32)).astype(jnp.bfloat16)
    out[count:, :] = jnp.concatenate([high, mid, low, jnp.zeros_like(low)], axis=1)


def attend(fills, q, pieces, tile, new=None, state=None, last=False):
    rows = q.shape[0]
    spec = tuple((start, keys.shape[1], which) for start, which, keys in pieces)
    operands = [fills, q] + [keys for _, _, keys in pieces]
    if new is not None:
        operands += list(new)
    aliases = {}
    if state is not None:
        if not last:
            aliases = {len(operands) + i: i for i in range(3)}
        operands += list(state)
    if last:
        tail = -(-rows // (LANES * 16)) * 16
        out_shape = [jax.ShapeDtypeStruct((rows + tail, DC), jnp.bfloat16)]
    else:
        out_shape = [
            jax.ShapeDtypeStruct((rows, LANES), jnp.float32),
            jax.ShapeDtypeStruct((rows, LANES), jnp.float32),
            jax.ShapeDtypeStruct((rows, DC), jnp.float32),
        ]
    out = pl.pallas_call(
        functools.partial(attend_kernel, spec, new is not None, state is None, last, tile),
        in_specs=[pl.BlockSpec(memory_space=pltpu.SMEM)] + [WHOLE] * (len(operands) - 1),
        out_specs=[WHOLE] * len(out_shape),
        out_shape=out_shape,
        input_output_aliases=aliases,
        compiler_params=room(24),
        cost_estimate=pl.CostEstimate(flops=0, bytes_accessed=0, transcendentals=0),
        name="attend",
    )(*operands)
    return out[0] if last else out


def after_kernel(x_ref, *refs):
    pass


def after(x, *tokens):
    return pl.pallas_call(
        after_kernel,
        in_specs=[ANY] * (1 + len(tokens)),
        out_specs=ANY,
        out_shape=jax.ShapeDtypeStruct(x.shape, x.dtype),
        input_output_aliases={0: 0},
        compiler_params=room(1),
        name="after",
    )(x, *tokens)


def pack_kernel(n, me_ref, query_ref, dec_ref, span_kv_ref, dec_kv_ref, *out_refs):
    per, row = span_kv_ref.shape
    per_dec = dec_ref.shape[0]
    part = query_ref.shape[1] // n
    cut = part // per
    pad = -(-row // LANES) * LANES - row

    def padded(ref):
        x = ref[...].astype(jnp.float32)
        return jnp.concatenate([x, jnp.zeros((x.shape[0], pad), jnp.float32)], axis=1)

    dec_kv = padded(dec_kv_ref)
    tail = [padded(span_kv_ref)]
    for e in range(per_dec):
        for j in range(0, row + pad, per * LANES):
            ends = range(j, min(j + per * LANES, row + pad), LANES)
            strips = [dec_kv[e : e + 1, k : k + LANES] for k in ends]
            strips += [jnp.zeros((1, LANES), jnp.float32)] * (per - len(strips))
            tail.append(jnp.concatenate(strips, axis=0))
    tail = jnp.concatenate(tail, axis=1).astype(jnp.bfloat16)
    for r, out_ref in enumerate(out_refs):
        begin = (me_ref[0] ^ r) * part
        out_ref[:, :part] = query_ref[:, pl.ds(pl.multiple_of(begin, LANES), part)]
        for e in range(per_dec):
            strips = []
            for i in range(per):
                at = pl.multiple_of(begin + i * cut, LANES)
                strips.append(dec_ref[e : e + 1, pl.ds(at, cut)].astype(jnp.float32))
            at = part + e * cut
            out_ref[:, at : at + cut] = jnp.concatenate(strips, axis=0).astype(jnp.bfloat16)
        out_ref[:, part + per_dec * cut :] = tail


def pack(n, me, query, dec_query, span_kv, dec_kv):
    per, row = span_kv.shape
    per_dec = dec_kv.shape[0]
    part = query.shape[1] // n
    wide = -(-row // LANES) * LANES
    fold = -(-wide // (per * LANES)) * LANES
    total = part + per_dec * (part // per) + wide + per_dec * fold
    operands = (query, dec_query, span_kv, dec_kv)
    return pl.pallas_call(
        functools.partial(pack_kernel, n),
        grid=(1,),
        in_specs=[pl.BlockSpec(memory_space=pltpu.SMEM)]
        + [pl.BlockSpec(x.shape, lambda i: (0, 0)) for x in operands],
        out_specs=[pl.BlockSpec((per, total), lambda i: (0, 0))] * n,
        out_shape=[jax.ShapeDtypeStruct((per, total), jnp.bfloat16)] * n,
        compiler_params=room(60),
        name="pack",
    )(me, *operands)


def absorb_kernel(per_dec, n, me_ref, w_hbm, *refs):
    got_refs, refs = refs[:n], refs[-6:]
    absorbed_ref, extra_ref, w_ref, placed, w_sem, sems = refs
    heads = w_ref.shape[0]
    _, per, total = placed.shape
    row = extra_ref.shape[1]
    count = absorbed_ref.shape[0] // heads
    wide = -(-row // LANES) * LANES
    fold = -(-wide // (per * LANES)) * LANES
    part = (total - wide - per_dec * fold) * per // (per + per_dec)
    width = part // heads
    cut = part // per
    at = part + per_dec * cut
    weights = pltpu.make_async_copy(w_hbm, w_ref, w_sem)
    weights.start()
    copies = [
        pltpu.make_async_copy(ref, placed.at[me_ref[0] ^ r], sems.at[r])
        for r, ref in enumerate(got_refs)
    ]
    for copy in copies:
        copy.start()
    for copy in copies:
        copy.wait()

    def unfold(x, length):
        strips = []
        for j in range(0, x.shape[1], length):
            strips += [x[i : i + 1, j : j + length] for i in range(per)]
        return jnp.concatenate(strips, axis=1)

    blocks = [placed[d].astype(jnp.float32) for d in range(n)]
    queries = [x[:, :part] for x in blocks]
    fresh = [x[:, at : at + wide] for x in blocks]
    for x in blocks:
        for e in range(per_dec):
            queries.append(unfold(x[:, part + e * cut : part + (e + 1) * cut], cut))
            begin = at + wide + e * fold
            fresh.append(unfold(x[:, begin : begin + fold], LANES)[:, :wide])
    q = jnp.concatenate(queries, axis=0).astype(jnp.bfloat16)
    new = jnp.concatenate(fresh, axis=0)
    blank = jnp.zeros((count, absorbed_ref.shape[1] - row), jnp.float32)
    weights.wait()
    for h in range(0, heads, 2):
        parts = []
        for g in (h, h + 1):
            mine = q[:, g * width : (g + 1) * width]
            latent = jnp.dot(mine[:, :DN], w_ref[g], preferred_element_type=jnp.float32)
            rope = mine[:, DN:].astype(jnp.float32)
            parts.append(jnp.concatenate([latent, rope, blank], axis=1))
        pair = jnp.concatenate(parts, axis=0).astype(jnp.bfloat16)
        absorbed_ref[h * count : (h + 2) * count, :] = pair
    blank = jnp.zeros((extra_ref.shape[0] - count, row), jnp.float32)
    extra_ref[...] = jnp.concatenate([new[:, :row], blank], axis=0).astype(jnp.bfloat16)


def absorb(count, per_dec, me, got, w_uk, row, tokens):
    heads = w_uk.shape[0]
    n = len(got)
    return pl.pallas_call(
        functools.partial(absorb_kernel, per_dec, n),
        in_specs=[pl.BlockSpec(memory_space=pltpu.SMEM)] + [ANY] * (1 + n + len(tokens)),
        out_shape=[
            jax.ShapeDtypeStruct((heads * count, -(-row // LANES) * LANES), jnp.bfloat16),
            jax.ShapeDtypeStruct((LANES, row), jnp.bfloat16),
        ],
        scratch_shapes=[
            pltpu.VMEM(w_uk.shape, w_uk.dtype),
            pltpu.VMEM((n, *got[0].shape), got[0].dtype),
            pltpu.SemaphoreType.DMA(()),
            pltpu.SemaphoreType.DMA((n,)),
        ],
        compiler_params=room(16),
        name="absorb",
    )(me, w_uk, *got, *tokens)


def split_kernel(spans, x_ref, *refs):
    for (a, b), ref in zip(spans, refs[-len(spans) :]):
        ref[...] = x_ref[:, a:b]


def split(x, spans, tokens):
    return pl.pallas_call(
        functools.partial(split_kernel, spans),
        grid=(1,),
        in_specs=[pl.BlockSpec(x.shape, lambda i: (0, 0))] + [ANY] * len(tokens),
        out_specs=[pl.BlockSpec((x.shape[0], b - a), lambda i: (0, 0)) for a, b in spans],
        out_shape=[jax.ShapeDtypeStruct((x.shape[0], b - a), x.dtype) for a, b in spans],
        compiler_params=room(16),
        name="split",
    )(x, *tokens)


def finish_kernel(count, m_ref, l_ref, acc_ref, far_ref, w_ref, span_ref, dec_ref):
    rows = m_ref.shape[0]
    heads = w_ref.shape[0]
    scale = score_scale * LOG2E
    parts = far_ref[rows:, :].astype(jnp.float32)
    packed = parts[:, :LANES] + parts[:, LANES : 2 * LANES] + parts[:, 2 * LANES : 3 * LANES]
    columns = []
    for g in range(rows // LANES):
        row = jnp.broadcast_to(packed[g : g + 1, :], (LANES, LANES))
        columns.append(jnp.transpose(row))
    far = jnp.concatenate(columns, axis=0)
    near = m_ref[...] * scale
    top = jnp.maximum(near, far)
    w_near = jnp.exp2(near - top)
    w_far = jnp.exp2(far - top)
    total = l_ref[...] * w_near + w_far
    inverse = 1.0 / total
    w_near = lanes(w_near * inverse, DC)
    w_far = lanes(w_far * inverse, DC)
    for h in range(heads):
        a, b = h * count, (h + 1) * count
        near_part = acc_ref[a:b, :] * w_near[a:b, :]
        far_part = far_ref[:rows, :].astype(jnp.float32)[a:b, :] * w_far[a:b, :]
        latent = (near_part + far_part).astype(jnp.bfloat16)
        done = jnp.dot(latent, w_ref[h], preferred_element_type=jnp.float32)
        span = span_ref.shape[0]
        span_ref[:, h * LANES : (h + 1) * LANES] = done[:span].astype(jnp.bfloat16)
        dec_ref[:, h * LANES : (h + 1) * LANES] = done[span:].astype(jnp.bfloat16)


def finish(count, span, state, far, w_uv):
    heads = w_uv.shape[0]
    wide = heads * w_uv.shape[2]
    return pl.pallas_call(
        functools.partial(finish_kernel, count),
        out_shape=(
            jax.ShapeDtypeStruct((span, wide), jnp.bfloat16),
            jax.ShapeDtypeStruct((count - span, wide), jnp.bfloat16),
        ),
        compiler_params=room(24),
        cost_estimate=pl.CostEstimate(
            flops=2 * count * heads * DC * w_uv.shape[2],
            bytes_accessed=2 * w_uv.size + 6 * state[2].size,
            transcendentals=0,
        ),
        name="finish",
    )(*state, far, w_uv)


def body(query, dec_query, cache_kv, span_kv, dec_kv, cache_fill, owner, slot, dec_len, w_uk, w_uv):
    me = lax.axis_index("seq")
    n = lax.axis_size("seq")
    pos_dev = cache_kv.shape[0]
    span = owner.shape[0]
    rows_dec = dec_len.shape[0]
    count = span + rows_dec
    heads = w_uk.shape[0]
    row = cache_kv.shape[1]

    def swap(x, stride):
        return lax.ppermute(x, "seq", [(i, i ^ stride) for i in range(n)])

    far, pair = n // 2, n // 4
    near = [1 << b for b in range(pair.bit_length() - 1)]
    keys = cache_kv.T
    edges = [0, pos_dev // 4, pos_dev // 4 * 3, pos_dev]

    place = me[None].astype(jnp.int32)
    mine = pack(n, place, query, dec_query, span_kv, dec_kv)
    got = [mine[0]] + [swap(x, r) for r, x in enumerate(mine) if r]

    pieces = [swap(keys[:, : edges[1]], far)]
    absorbed, extra = absorb(count, rows_dec // n, place, got, w_uk, row, pieces)
    new_rows = extra[:span]
    other = swap(absorbed, pair)
    *cuts, copy = split(keys, [*zip(edges[1:], edges[2:]), (0, pos_dev)], got[1:] + pieces)
    blocks = [(0, copy)]
    for stride in near:
        blocks += [(offset ^ stride, swap(x, stride)) for offset, x in blocks]
    pieces.append(swap(cuts[0], far))

    def spread(x):
        part = [(far, x)]
        for stride in near:
            part += [(offset ^ stride, swap(y, stride)) for offset, y in part]
        return part

    target = jnp.where(owner == me, slot, -1)
    onehot = jnp.arange(pos_dev, dtype=jnp.int32)[None, :] == target[:, None]
    placed = lax.dot_general(
        new_rows,
        onehot.astype(jnp.bfloat16),
        (((0,), (0,)), ((), ())),
        preferred_element_type=jnp.float32,
    ).astype(jnp.bfloat16)
    new_cache = jnp.where(jnp.any(onehot, axis=0)[None, :], placed, keys).T

    limits = jnp.concatenate([jnp.arange(1, span + 1, dtype=jnp.int32), dec_len])
    index = jnp.arange(LANES, dtype=jnp.int32)
    queries = jnp.arange(count, dtype=jnp.int32)
    seen = (index[None, :] < span) & (index[None, :] < limits[:, None])
    seen |= (index[None, :] >= span) & (index[None, :] == queries[:, None])
    bias = jnp.where(seen, 0.0, HIDDEN).astype(jnp.float32)
    held = [offset for offset, _ in blocks]
    offsets = held + [offset ^ far for offset in held]
    which = jnp.stack([me ^ offset for offset in offsets])
    fills = jnp.sum(
        jnp.where(which[:, None] == jnp.arange(n, dtype=jnp.int32)[None, :], cache_fill[None, :], 0),
        axis=1,
    )
    base = len(blocks)
    tile = heads // 2 * count

    def stage_of(c, part):
        return [(edges[c], base + i, x) for i, (_, x) in enumerate(part)]

    home = [(0, 0, keys)]
    side = [(0, i, x) for i, (_, x) in enumerate(blocks) if i]
    state = attend(fills, absorbed, home, tile, new=(extra, bias))
    first = stage_of(0, spread(pieces[0]))
    pieces.append(swap(after(cuts[1], state[0], pieces[1]), far))
    first += stage_of(1, spread(after(pieces[1], state[0])))
    state = attend(fills, absorbed, side, tile, state=state)
    other = after(other, state[0])
    guest = attend(fills, other, home + side, tile)
    second = stage_of(2, spread(after(pieces[2], guest[0])))
    guest = attend(fills, other, first, tile, state=guest)
    sent = attend(fills, other, second, tile, state=guest, last=True)
    back = swap(sent, pair)
    state = attend(fills, absorbed, first + second, tile, state=state)
    span_out, dec_out = finish(count, span, state, back, w_uv)
    return (span_out, dec_out, new_cache)


def solution(mesh):
    in_specs = (
        P(("grp", "seq"), None),
        P(("grp", "seq"), None),
        P(("grp", "seq"), None),
        P(("grp", "seq"), None),
        P(("grp", "seq"), None),
        P("grp"),
        P("grp"),
        P("grp"),
        P("grp"),
        P("seq", None, None),
        P("seq", None, None),
    )
    out_specs = (P("grp", "seq"), P("grp", "seq"), P(("grp", "seq"), None))
    return jax.shard_map(body, mesh=mesh, in_specs=in_specs, out_specs=out_specs, check_vma=False)
```

```python
import functools

import jax
import jax.numpy as jnp
from jax import lax
from jax.experimental import pallas as pl
from jax.experimental.pallas import tpu as pltpu
from jax.sharding import PartitionSpec as P

DN = 128
DC = 512
LANES = 128
ANY = pl.BlockSpec(memory_space=pl.ANY)
WHOLE = pl.BlockSpec(memory_space=pltpu.VMEM)


def room(mebibytes):
    return pltpu.CompilerParams(vmem_limit_bytes=mebibytes * 1024 * 1024)

score_scale = 0.1353
LOG2E = 1.4426950408889634
HIDDEN = -1e30
FLOOR = -1e25


def lanes(x, width):
    return jnp.concatenate([x] * (width // LANES), axis=1) if width > LANES else x


def attend_kernel(pieces, extra, first, last, tile, *refs):
    refs = list(refs)
    fills = refs.pop(0)
    q_ref = refs.pop(0)
    keys = [refs.pop(0) for _ in pieces]
    if extra:
        new_ref = refs.pop(0)
        bias_ref = refs.pop(0)
    if not first:
        m_in, l_in, acc_in = refs.pop(0), refs.pop(0), refs.pop(0)
    scale = score_scale * LOG2E
    weights = []
    for at in range(0, q_ref.shape[0], tile):
        rows = slice(at, at + tile)
        q = q_ref[rows, : keys[0].shape[0]]
        scores = []
        for (start, width, which), ref in zip(pieces, keys):
            s = jnp.dot(q, ref[...], preferred_element_type=jnp.float32)
            slot = start + lax.broadcasted_iota(jnp.int32, (1, width), 1)
            scores.append(jnp.where(slot < fills[which], s, HIDDEN))
        if extra:
            s = lax.dot_general(
                q, new_ref[...], (((1,), (1,)), ((), ())), preferred_element_type=jnp.float32
            )
            bias = bias_ref[...]
            scores.append(s + jnp.concatenate([bias] * (tile // bias.shape[0]), axis=0))
        peak = functools.reduce(jnp.maximum, [jnp.max(s, axis=1, keepdims=True) for s in scores])
        peak = jnp.maximum(peak, FLOOR)
        if not first:
            old = m_in[rows, :1]
            peak = jnp.maximum(peak, old)
        total = 0.0
        acc = 0.0
        for i, s in enumerate(scores):
            e = jnp.exp2((s - peak) * scale)
            total = total + jnp.sum(e, axis=1, keepdims=True)
            w = e.astype(jnp.bfloat16)
            if i < len(pieces):
                acc = acc + lax.dot_general(
                    w, keys[i][:DC, :], (((1,), (1,)), ((), ())), preferred_element_type=jnp.float32
                )
            else:
                acc = acc + jnp.dot(w, new_ref[:, :DC], preferred_element_type=jnp.float32)
        if not first:
            keep = jnp.exp2((old - peak) * scale)
            total = total + l_in[rows, :1] * keep
            acc = acc + acc_in[rows, :] * keep
        if last:
            refs[0][rows, :] = (acc * (1.0 / total)).astype(jnp.bfloat16)
            weights.append(jnp.broadcast_to(peak * scale + jnp.log2(total), (tile, LANES)))
        else:
            m_out, l_out, acc_out = refs
            m_out[rows, :] = jnp.broadcast_to(peak, (tile, LANES))
            l_out[rows, :] = jnp.broadcast_to(total, (tile, LANES))
            acc_out[rows, :] = acc
    if not last:
        return
    out = refs[0]
    count = q_ref.shape[0]
    weight = jnp.concatenate(weights, axis=0)
    tail = out.shape[0] - count
    place = lax.broadcasted_iota(jnp.int32, (tail, LANES), 0)
    packed = jnp.zeros((tail, LANES), jnp.float32)
    for g in range(count // LANES):
        turned = jnp.transpose(weight[g * LANES : (g + 1) * LANES, :])
        packed = jnp.where(place == g, turned[:tail, :], packed)
    high = packed.astype(jnp.bfloat16)
    rest = packed - high.astype(jnp.float32)
    mid = rest.astype(jnp.bfloat16)
    low = (rest - mid.astype(jnp.float32)).astype(jnp.bfloat16)
    out[count:, :] = jnp.concatenate([high, mid, low, jnp.zeros_like(low)], axis=1)


def attend(fills, q, pieces, tile, new=None, state=None, last=False):
    rows = q.shape[0]
    spec = tuple((start, keys.shape[1], which) for start, which, keys in pieces)
    operands = [fills, q] + [keys for _, _, keys in pieces]
    if new is not None:
        operands += list(new)
    aliases = {}
    if state is not None:
        if not last:
            aliases = {len(operands) + i: i for i in range(3)}
        operands += list(state)
    if last:
        tail = -(-rows // (LANES * 16)) * 16
        out_shape = [jax.ShapeDtypeStruct((rows + tail, DC), jnp.bfloat16)]
    else:
        out_shape = [
            jax.ShapeDtypeStruct((rows, LANES), jnp.float32),
            jax.ShapeDtypeStruct((rows, LANES), jnp.float32),
            jax.ShapeDtypeStruct((rows, DC), jnp.float32),
        ]
    out = pl.pallas_call(
        functools.partial(attend_kernel, spec, new is not None, state is None, last, tile),
        in_specs=[pl.BlockSpec(memory_space=pltpu.SMEM)] + [WHOLE] * (len(operands) - 1),
        out_specs=[WHOLE] * len(out_shape),
        out_shape=out_shape,
        input_output_aliases=aliases,
        compiler_params=room(24),
        cost_estimate=pl.CostEstimate(flops=0, bytes_accessed=0, transcendentals=0),
        name="attend",
    )(*operands)
    return out[0] if last else out


def after_kernel(x_ref, *refs):
    pass


def after(x, *tokens):
    return pl.pallas_call(
        after_kernel,
        in_specs=[ANY] * (1 + len(tokens)),
        out_specs=ANY,
        out_shape=jax.ShapeDtypeStruct(x.shape, x.dtype),
        input_output_aliases={0: 0},
        compiler_params=room(1),
        name="after",
    )(x, *tokens)


def pack_kernel(order, me_ref, query_ref, dec_ref, span_kv_ref, dec_kv_ref, *out_refs):
    per, row = span_kv_ref.shape
    per_dec = dec_ref.shape[0]
    n = sum(len(x) for x in order)
    part = query_ref.shape[1] // n
    cut = part // per
    pad = -(-row // LANES) * LANES - row

    def padded(ref):
        x = ref[...].astype(jnp.float32)
        return jnp.concatenate([x, jnp.zeros((x.shape[0], pad), jnp.float32)], axis=1)

    dec_kv = padded(dec_kv_ref)
    tail = [padded(span_kv_ref)]
    for e in range(per_dec):
        for j in range(0, row + pad, per * LANES):
            ends = range(j, min(j + per * LANES, row + pad), LANES)
            strips = [dec_kv[e : e + 1, k : k + LANES] for k in ends]
            strips += [jnp.zeros((1, LANES), jnp.float32)] * (per - len(strips))
            tail.append(jnp.concatenate(strips, axis=0))
    tail = jnp.concatenate(tail, axis=1).astype(jnp.bfloat16)
    places = [(ref, i, r) for ref, rs in zip(out_refs, order) for i, r in enumerate(rs)]
    for out_ref, j, r in places:
        begin = (me_ref[0] ^ r) * part
        out_ref[j, :, :part] = query_ref[:, pl.ds(pl.multiple_of(begin, LANES), part)]
        for e in range(per_dec):
            strips = []
            for i in range(per):
                at = pl.multiple_of(begin + i * cut, LANES)
                strips.append(dec_ref[e : e + 1, pl.ds(at, cut)].astype(jnp.float32))
            at = part + e * cut
            out_ref[j, :, at : at + cut] = jnp.concatenate(strips, axis=0).astype(jnp.bfloat16)
        out_ref[j, :, part + per_dec * cut :] = tail


def pack(order, me, query, dec_query, span_kv, dec_kv):
    n = sum(len(x) for x in order)
    per, row = span_kv.shape
    per_dec = dec_kv.shape[0]
    part = query.shape[1] // n
    wide = -(-row // LANES) * LANES
    fold = -(-wide // (per * LANES)) * LANES
    total = part + per_dec * (part // per) + wide + per_dec * fold
    operands = (query, dec_query, span_kv, dec_kv)
    return pl.pallas_call(
        functools.partial(pack_kernel, order),
        grid=(1,),
        in_specs=[pl.BlockSpec(memory_space=pltpu.SMEM)]
        + [pl.BlockSpec(x.shape, lambda i: (0, 0)) for x in operands],
        out_specs=[pl.BlockSpec((len(x), per, total), lambda i: (0, 0, 0)) for x in order],
        out_shape=[jax.ShapeDtypeStruct((len(x), per, total), jnp.bfloat16) for x in order],
        compiler_params=room(60),
        name="pack",
    )(me, *operands)


def absorb_kernel(per_dec, order, me_ref, w_hbm, *refs):
    got_refs, refs = refs[: len(order)], refs[-6:]
    absorbed_ref, extra_ref, w_ref, placed, w_sem, sems = refs
    heads = w_ref.shape[0]
    n, per, total = placed.shape
    row = extra_ref.shape[1]
    count = absorbed_ref.shape[0] // heads
    wide = -(-row // LANES) * LANES
    fold = -(-wide // (per * LANES)) * LANES
    part = (total - wide - per_dec * fold) * per // (per + per_dec)
    width = part // heads
    cut = part // per
    at = part + per_dec * cut
    weights = pltpu.make_async_copy(w_hbm, w_ref, w_sem)
    weights.start()
    copies = [
        pltpu.make_async_copy(ref.at[i], placed.at[me_ref[0] ^ r], sems.at[r])
        for ref, rs in zip(got_refs, order)
        for i, r in enumerate(rs)
    ]
    for copy in copies:
        copy.start()
    for copy in copies:
        copy.wait()

    def unfold(x, length):
        strips = []
        for j in range(0, x.shape[1], length):
            strips += [x[i : i + 1, j : j + length] for i in range(per)]
        return jnp.concatenate(strips, axis=1)

    blocks = [placed[d].astype(jnp.float32) for d in range(n)]
    queries = [x[:, :part] for x in blocks]
    fresh = [x[:, at : at + wide] for x in blocks]
    for x in blocks:
        for e in range(per_dec):
            queries.append(unfold(x[:, part + e * cut : part + (e + 1) * cut], cut))
            begin = at + wide + e * fold
            fresh.append(unfold(x[:, begin : begin + fold], LANES)[:, :wide])
    q = jnp.concatenate(queries, axis=0).astype(jnp.bfloat16)
    new = jnp.concatenate(fresh, axis=0)
    blank = jnp.zeros((count, absorbed_ref.shape[1] - row), jnp.float32)
    weights.wait()
    for h in range(0, heads, 2):
        parts = []
        for g in (h, h + 1):
            mine = q[:, g * width : (g + 1) * width]
            latent = jnp.dot(mine[:, :DN], w_ref[g], preferred_element_type=jnp.float32)
            rope = mine[:, DN:].astype(jnp.float32)
            parts.append(jnp.concatenate([latent, rope, blank], axis=1))
        pair = jnp.concatenate(parts, axis=0).astype(jnp.bfloat16)
        absorbed_ref[h * count : (h + 2) * count, :] = pair
    blank = jnp.zeros((extra_ref.shape[0] - count, row), jnp.float32)
    extra_ref[...] = jnp.concatenate([new[:, :row], blank], axis=0).astype(jnp.bfloat16)


def absorb(count, per_dec, me, order, got, w_uk, row):
    heads = w_uk.shape[0]
    n = sum(len(x) for x in order)
    return pl.pallas_call(
        functools.partial(absorb_kernel, per_dec, order),
        in_specs=[pl.BlockSpec(memory_space=pltpu.SMEM)] + [ANY] * (1 + len(got)),
        out_shape=[
            jax.ShapeDtypeStruct((heads * count, -(-row // LANES) * LANES), jnp.bfloat16),
            jax.ShapeDtypeStruct((LANES, row), jnp.bfloat16),
        ],
        scratch_shapes=[
            pltpu.VMEM(w_uk.shape, w_uk.dtype),
            pltpu.VMEM((n, *got[0].shape[1:]), got[0].dtype),
            pltpu.SemaphoreType.DMA(()),
            pltpu.SemaphoreType.DMA((n,)),
        ],
        compiler_params=room(16),
        name="absorb",
    )(me, w_uk, *got)


def split_kernel(spans, x_ref, *refs):
    for (a, b), ref in zip(spans, refs[-len(spans) :]):
        ref[...] = x_ref[:, a:b]


def split(x, spans, tokens):
    return pl.pallas_call(
        functools.partial(split_kernel, spans),
        grid=(1,),
        in_specs=[pl.BlockSpec(x.shape, lambda i: (0, 0))] + [ANY] * len(tokens),
        out_specs=[pl.BlockSpec((x.shape[0], b - a), lambda i: (0, 0)) for a, b in spans],
        out_shape=[jax.ShapeDtypeStruct((x.shape[0], b - a), x.dtype) for a, b in spans],
        compiler_params=room(16),
        name="split",
    )(x, *tokens)


def finish_kernel(count, m_ref, l_ref, acc_ref, far_ref, w_ref, span_ref, dec_ref):
    rows = m_ref.shape[0]
    heads = w_ref.shape[0]
    scale = score_scale * LOG2E
    parts = far_ref[rows:, :].astype(jnp.float32)
    packed = parts[:, :LANES] + parts[:, LANES : 2 * LANES] + parts[:, 2 * LANES : 3 * LANES]
    columns = []
    for g in range(rows // LANES):
        row = jnp.broadcast_to(packed[g : g + 1, :], (LANES, LANES))
        columns.append(jnp.transpose(row))
    far = jnp.concatenate(columns, axis=0)
    near = m_ref[...] * scale
    top = jnp.maximum(near, far)
    w_near = jnp.exp2(near - top)
    w_far = jnp.exp2(far - top)
    total = l_ref[...] * w_near + w_far
    inverse = 1.0 / total
    w_near = lanes(w_near * inverse, DC)
    w_far = lanes(w_far * inverse, DC)
    for h in range(heads):
        a, b = h * count, (h + 1) * count
        near_part = acc_ref[a:b, :] * w_near[a:b, :]
        far_part = far_ref[:rows, :].astype(jnp.float32)[a:b, :] * w_far[a:b, :]
        latent = (near_part + far_part).astype(jnp.bfloat16)
        done = jnp.dot(latent, w_ref[h], preferred_element_type=jnp.float32)
        span = span_ref.shape[0]
        span_ref[:, h * LANES : (h + 1) * LANES] = done[:span].astype(jnp.bfloat16)
        dec_ref[:, h * LANES : (h + 1) * LANES] = done[span:].astype(jnp.bfloat16)


def finish(count, span, state, far, w_uv):
    heads = w_uv.shape[0]
    wide = heads * w_uv.shape[2]
    return pl.pallas_call(
        functools.partial(finish_kernel, count),
        out_shape=(
            jax.ShapeDtypeStruct((span, wide), jnp.bfloat16),
            jax.ShapeDtypeStruct((count - span, wide), jnp.bfloat16),
        ),
        compiler_params=room(24),
        cost_estimate=pl.CostEstimate(
            flops=2 * count * heads * DC * w_uv.shape[2],
            bytes_accessed=2 * w_uv.size + 6 * state[2].size,
            transcendentals=0,
        ),
        name="finish",
    )(*state, far, w_uv)


def body(query, dec_query, cache_kv, span_kv, dec_kv, cache_fill, owner, slot, dec_len, w_uk, w_uv):
    me = lax.axis_index("seq")
    n = lax.axis_size("seq")
    pos_dev = cache_kv.shape[0]
    span = owner.shape[0]
    rows_dec = dec_len.shape[0]
    count = span + rows_dec
    heads = w_uk.shape[0]
    row = cache_kv.shape[1]

    def swap(x, stride):
        return lax.ppermute(x, "seq", [(i, i ^ stride) for i in range(n)])

    far, pair = n // 2, n // 4
    near = [1 << b for b in range(pair.bit_length() - 1)]
    keys = cache_kv.T
    edges = [0, pos_dev // 8 * 3, pos_dev // 4 * 3, pos_dev]

    lead = keys[:, : edges[1]]
    pieces = [swap(lead, far)]

    place = me[None].astype(jnp.int32)
    order = [[r for r in range(n) if not r & 1], [r for r in range(n) if r & 1]]
    stay, go = pack(order, place, query, dec_query, span_kv, dec_kv)
    come = swap(go, 1)
    groups = {r: [(0, stay[i]), (1, come[i])] for i, r in enumerate(order[0])}
    for stride in near[1:]:
        away = [r for r in groups if r & stride]
        moved = swap(jnp.stack([x for r in away for _, x in groups[r]]), stride)
        held = len(groups[away[0]])
        for i, r in enumerate(away):
            kept = groups[r ^ stride]
            kept += [(o ^ stride, moved[i * held + j]) for j, (o, _) in enumerate(groups.pop(r))]
    got, order = [], []
    for r in sorted(groups):
        got.append(jnp.stack([x for _, x in groups[r]]))
        order.append([r ^ o for o, _ in groups[r]])
    got = got[:1] + [swap(x, r) for r, x in zip(sorted(groups)[1:], got[1:])]

    middle = edges[1]
    *cuts, early, late = split(
        keys, [*zip(edges[1:], edges[2:]), (0, middle), (middle, pos_dev)], [come]
    )
    halves = [(0, early, after(late, *got[1:]))]
    for stride in near:
        halves += [(o ^ stride, swap(x, stride), swap(y, stride)) for o, x, y in halves]
    absorbed, extra = absorb(count, rows_dec // n, place, order, got, w_uk, row)
    new_rows = extra[:span]
    other = swap(absorbed, pair)
    pieces.append(swap(after(cuts[0], pieces[0], halves[-1][1], *got[1:]), far))

    def spread(x):
        part = [(far, x)]
        for stride in near:
            part += [(offset ^ stride, swap(y, stride)) for offset, y in part]
        return part

    target = jnp.where(owner == me, slot, -1)
    onehot = jnp.arange(pos_dev, dtype=jnp.int32)[None, :] == target[:, None]
    placed = lax.dot_general(
        new_rows,
        onehot.astype(jnp.bfloat16),
        (((0,), (0,)), ((), ())),
        preferred_element_type=jnp.float32,
    ).astype(jnp.bfloat16)
    new_cache = jnp.where(jnp.any(onehot, axis=0)[None, :], placed, keys).T

    limits = jnp.concatenate([jnp.arange(1, span + 1, dtype=jnp.int32), dec_len])
    index = jnp.arange(LANES, dtype=jnp.int32)
    queries = jnp.arange(count, dtype=jnp.int32)
    seen = (index[None, :] < span) & (index[None, :] < limits[:, None])
    seen |= (index[None, :] >= span) & (index[None, :] == queries[:, None])
    bias = jnp.where(seen, 0.0, HIDDEN).astype(jnp.float32)
    held = [offset for offset, _, _ in halves]
    offsets = held + [offset ^ far for offset in held]
    which = jnp.stack([me ^ offset for offset in offsets])
    fills = jnp.sum(
        jnp.where(which[:, None] == jnp.arange(n, dtype=jnp.int32)[None, :], cache_fill[None, :], 0),
        axis=1,
    )
    base = len(halves)
    tile = heads // 2 * count

    def stage_of(c, part):
        return [(edges[c], base + i, x) for i, (_, x) in enumerate(part)]

    home = [(0, 0, keys)]
    side = [(a, i, z) for i, (_, x, y) in enumerate(halves) if i for a, z in ((0, x), (middle, y))]
    state = attend(fills, absorbed, home, tile, new=(extra, bias))
    part = spread(pieces[0])
    side += stage_of(0, part)
    pieces.append(swap(after(cuts[1], state[0], pieces[1], part[-1][1]), far))
    first = stage_of(1, spread(after(pieces[1], state[0])))
    state = attend(fills, absorbed, side, tile, state=state)
    other = after(other, state[0])
    guest = attend(fills, other, home + side, tile)
    second = stage_of(2, spread(after(pieces[2], guest[0])))
    guest = attend(fills, other, first, tile, state=guest)
    sent = attend(fills, other, second, tile, state=guest, last=True)
    back = swap(sent, pair)
    state = attend(fills, absorbed, first + second, tile, state=state)
    span_out, dec_out = finish(count, span, state, back, w_uv)
    return (span_out, dec_out, new_cache)


def solution(mesh):
    in_specs = (
        P(("grp", "seq"), None),
        P(("grp", "seq"), None),
        P(("grp", "seq"), None),
        P(("grp", "seq"), None),
        P(("grp", "seq"), None),
        P("grp"),
        P("grp"),
        P("grp"),
        P("grp"),
        P("seq", None, None),
        P("seq", None, None),
    )
    out_specs = (P("grp", "seq"), P("grp", "seq"), P(("grp", "seq"), None))
    return jax.shard_map(body, mesh=mesh, in_specs=in_specs, out_specs=out_specs, check_vma=False)
```

```python
import functools

import jax
import jax.numpy as jnp
from jax import lax
from jax.experimental import pallas as pl
from jax.experimental.pallas import tpu as pltpu
from jax.sharding import PartitionSpec as P

DN = 128
DC = 512
LANES = 128
ANY = pl.BlockSpec(memory_space=pl.ANY)
WHOLE = pl.BlockSpec(memory_space=pltpu.VMEM)


def room(mebibytes):
    return pltpu.CompilerParams(vmem_limit_bytes=mebibytes * 1024 * 1024)

score_scale = 0.1353
LOG2E = 1.4426950408889634
HIDDEN = -1e30
FLOOR = -1e25


def lanes(x, width):
    return jnp.concatenate([x] * (width // LANES), axis=1) if width > LANES else x


def attend_kernel(pieces, extra, first, last, tile, *refs):
    refs = list(refs)
    fills = refs.pop(0)
    q_ref = refs.pop(0)
    keys = [refs.pop(0) for _ in pieces]
    if extra:
        new_ref = refs.pop(0)
        bias_ref = refs.pop(0)
    if not first:
        m_in, l_in, acc_in = refs.pop(0), refs.pop(0), refs.pop(0)
    scale = score_scale * LOG2E
    weights = []
    for at in range(0, q_ref.shape[0], tile):
        rows = slice(at, at + tile)
        q = q_ref[rows, : keys[0].shape[0]]
        scores = []
        for (start, width, which), ref in zip(pieces, keys):
            s = jnp.dot(q, ref[...], preferred_element_type=jnp.float32)
            slot = start + lax.broadcasted_iota(jnp.int32, (1, width), 1)
            scores.append(jnp.where(slot < fills[which], s, HIDDEN))
        if extra:
            s = lax.dot_general(
                q, new_ref[...], (((1,), (1,)), ((), ())), preferred_element_type=jnp.float32
            )
            bias = bias_ref[...]
            scores.append(s + jnp.concatenate([bias] * (tile // bias.shape[0]), axis=0))
        peak = functools.reduce(jnp.maximum, [jnp.max(s, axis=1, keepdims=True) for s in scores])
        peak = jnp.maximum(peak, FLOOR)
        if not first:
            old = m_in[rows, :1]
            peak = jnp.maximum(peak, old)
        total = 0.0
        acc = 0.0
        for i, s in enumerate(scores):
            e = jnp.exp2((s - peak) * scale)
            total = total + jnp.sum(e, axis=1, keepdims=True)
            w = e.astype(jnp.bfloat16)
            if i < len(pieces):
                acc = acc + lax.dot_general(
                    w, keys[i][:DC, :], (((1,), (1,)), ((), ())), preferred_element_type=jnp.float32
                )
            else:
                acc = acc + jnp.dot(w, new_ref[:, :DC], preferred_element_type=jnp.float32)
        if not first:
            keep = jnp.exp2((old - peak) * scale)
            total = total + l_in[rows, :1] * keep
            acc = acc + acc_in[rows, :] * keep
        if last:
            refs[0][rows, :] = (acc * (1.0 / total)).astype(jnp.bfloat16)
            weights.append(jnp.broadcast_to(peak * scale + jnp.log2(total), (tile, LANES)))
        else:
            m_out, l_out, acc_out = refs
            m_out[rows, :] = jnp.broadcast_to(peak, (tile, LANES))
            l_out[rows, :] = jnp.broadcast_to(total, (tile, LANES))
            acc_out[rows, :] = acc
    if not last:
        return
    out = refs[0]
    count = q_ref.shape[0]
    weight = jnp.concatenate(weights, axis=0)
    tail = out.shape[0] - count
    place = lax.broadcasted_iota(jnp.int32, (tail, LANES), 0)
    packed = jnp.zeros((tail, LANES), jnp.float32)
    for g in range(count // LANES):
        turned = jnp.transpose(weight[g * LANES : (g + 1) * LANES, :])
        packed = jnp.where(place == g, turned[:tail, :], packed)
    high = packed.astype(jnp.bfloat16)
    rest = packed - high.astype(jnp.float32)
    mid = rest.astype(jnp.bfloat16)
    low = (rest - mid.astype(jnp.float32)).astype(jnp.bfloat16)
    out[count:, :] = jnp.concatenate([high, mid, low, jnp.zeros_like(low)], axis=1)


def attend(fills, q, pieces, tile, new=None, state=None, last=False):
    rows = q.shape[0]
    spec = tuple((start, keys.shape[1], which) for start, which, keys in pieces)
    operands = [fills, q] + [keys for _, _, keys in pieces]
    if new is not None:
        operands += list(new)
    aliases = {}
    if state is not None:
        if not last:
            aliases = {len(operands) + i: i for i in range(3)}
        operands += list(state)
    if last:
        tail = -(-rows // (LANES * 16)) * 16
        out_shape = [jax.ShapeDtypeStruct((rows + tail, DC), jnp.bfloat16)]
    else:
        out_shape = [
            jax.ShapeDtypeStruct((rows, LANES), jnp.float32),
            jax.ShapeDtypeStruct((rows, LANES), jnp.float32),
            jax.ShapeDtypeStruct((rows, DC), jnp.float32),
        ]
    out = pl.pallas_call(
        functools.partial(attend_kernel, spec, new is not None, state is None, last, tile),
        in_specs=[pl.BlockSpec(memory_space=pltpu.SMEM)] + [WHOLE] * (len(operands) - 1),
        out_specs=[WHOLE] * len(out_shape),
        out_shape=out_shape,
        input_output_aliases=aliases,
        compiler_params=room(24),
        cost_estimate=pl.CostEstimate(flops=0, bytes_accessed=0, transcendentals=0),
        name="attend",
    )(*operands)
    return out[0] if last else out


def after_kernel(x_ref, *refs):
    pass


def after(x, *tokens):
    return pl.pallas_call(
        after_kernel,
        in_specs=[ANY] * (1 + len(tokens)),
        out_specs=ANY,
        out_shape=jax.ShapeDtypeStruct(x.shape, x.dtype),
        input_output_aliases={0: 0},
        compiler_params=room(1),
        name="after",
    )(x, *tokens)


def pack_kernel(order, me_ref, query_ref, dec_ref, span_kv_ref, dec_kv_ref, *out_refs):
    per, row = span_kv_ref.shape
    per_dec = dec_ref.shape[0]
    n = sum(len(x) for x in order)
    part = query_ref.shape[1] // n
    cut = part // per
    pad = -(-row // LANES) * LANES - row

    def padded(ref):
        x = ref[...].astype(jnp.float32)
        return jnp.concatenate([x, jnp.zeros((x.shape[0], pad), jnp.float32)], axis=1)

    dec_kv = padded(dec_kv_ref)
    tail = [padded(span_kv_ref)]
    for e in range(per_dec):
        for j in range(0, row + pad, per * LANES):
            ends = range(j, min(j + per * LANES, row + pad), LANES)
            strips = [dec_kv[e : e + 1, k : k + LANES] for k in ends]
            strips += [jnp.zeros((1, LANES), jnp.float32)] * (per - len(strips))
            tail.append(jnp.concatenate(strips, axis=0))
    tail = jnp.concatenate(tail, axis=1).astype(jnp.bfloat16)
    places = [(ref, i, r) for ref, rs in zip(out_refs, order) for i, r in enumerate(rs)]
    for out_ref, j, r in places:
        begin = (me_ref[0] ^ r) * part
        out_ref[j, :, :part] = query_ref[:, pl.ds(pl.multiple_of(begin, LANES), part)]
        for e in range(per_dec):
            strips = []
            for i in range(per):
                at = pl.multiple_of(begin + i * cut, LANES)
                strips.append(dec_ref[e : e + 1, pl.ds(at, cut)].astype(jnp.float32))
            at = part + e * cut
            out_ref[j, :, at : at + cut] = jnp.concatenate(strips, axis=0).astype(jnp.bfloat16)
        out_ref[j, :, part + per_dec * cut :] = tail


def pack(order, me, query, dec_query, span_kv, dec_kv):
    n = sum(len(x) for x in order)
    per, row = span_kv.shape
    per_dec = dec_kv.shape[0]
    part = query.shape[1] // n
    wide = -(-row // LANES) * LANES
    fold = -(-wide // (per * LANES)) * LANES
    total = part + per_dec * (part // per) + wide + per_dec * fold
    operands = (query, dec_query, span_kv, dec_kv)
    return pl.pallas_call(
        functools.partial(pack_kernel, order),
        grid=(1,),
        in_specs=[pl.BlockSpec(memory_space=pltpu.SMEM)]
        + [pl.BlockSpec(x.shape, lambda i: (0, 0)) for x in operands],
        out_specs=[pl.BlockSpec((len(x), per, total), lambda i: (0, 0, 0)) for x in order],
        out_shape=[jax.ShapeDtypeStruct((len(x), per, total), jnp.bfloat16) for x in order],
        compiler_params=room(60),
        name="pack",
    )(me, *operands)


def absorb_kernel(per_dec, order, me_ref, w_hbm, *refs):
    got_refs, refs = refs[: len(order)], refs[-6:]
    absorbed_ref, extra_ref, w_ref, placed, w_sem, sems = refs
    heads = w_ref.shape[0]
    n, per, total = placed.shape
    row = extra_ref.shape[1]
    count = absorbed_ref.shape[0] // heads
    wide = -(-row // LANES) * LANES
    fold = -(-wide // (per * LANES)) * LANES
    part = (total - wide - per_dec * fold) * per // (per + per_dec)
    width = part // heads
    cut = part // per
    at = part + per_dec * cut
    weights = pltpu.make_async_copy(w_hbm, w_ref, w_sem)
    weights.start()
    copies = [
        pltpu.make_async_copy(ref.at[i], placed.at[me_ref[0] ^ r], sems.at[r])
        for ref, rs in zip(got_refs, order)
        for i, r in enumerate(rs)
    ]
    for copy in copies:
        copy.start()
    for copy in copies:
        copy.wait()

    def unfold(x, length):
        strips = []
        for j in range(0, x.shape[1], length):
            strips += [x[i : i + 1, j : j + length] for i in range(per)]
        return jnp.concatenate(strips, axis=1)

    blocks = [placed[d].astype(jnp.float32) for d in range(n)]
    queries = [x[:, :part] for x in blocks]
    fresh = [x[:, at : at + wide] for x in blocks]
    for x in blocks:
        for e in range(per_dec):
            queries.append(unfold(x[:, part + e * cut : part + (e + 1) * cut], cut))
            begin = at + wide + e * fold
            fresh.append(unfold(x[:, begin : begin + fold], LANES)[:, :wide])
    q = jnp.concatenate(queries, axis=0).astype(jnp.bfloat16)
    new = jnp.concatenate(fresh, axis=0)
    blank = jnp.zeros((count, absorbed_ref.shape[1] - row), jnp.float32)
    weights.wait()
    for h in range(0, heads, 2):
        parts = []
        for g in (h, h + 1):
            mine = q[:, g * width : (g + 1) * width]
            latent = jnp.dot(mine[:, :DN], w_ref[g], preferred_element_type=jnp.float32)
            rope = mine[:, DN:].astype(jnp.float32)
            parts.append(jnp.concatenate([latent, rope, blank], axis=1))
        pair = jnp.concatenate(parts, axis=0).astype(jnp.bfloat16)
        absorbed_ref[h * count : (h + 2) * count, :] = pair
    blank = jnp.zeros((extra_ref.shape[0] - count, row), jnp.float32)
    extra_ref[...] = jnp.concatenate([new[:, :row], blank], axis=0).astype(jnp.bfloat16)


def absorb(count, per_dec, me, order, got, w_uk, row, tokens):
    heads = w_uk.shape[0]
    n = sum(len(x) for x in order)
    return pl.pallas_call(
        functools.partial(absorb_kernel, per_dec, order),
        in_specs=[pl.BlockSpec(memory_space=pltpu.SMEM)] + [ANY] * (1 + len(got) + len(tokens)),
        out_shape=[
            jax.ShapeDtypeStruct((heads * count, -(-row // LANES) * LANES), jnp.bfloat16),
            jax.ShapeDtypeStruct((LANES, row), jnp.bfloat16),
        ],
        scratch_shapes=[
            pltpu.VMEM(w_uk.shape, w_uk.dtype),
            pltpu.VMEM((n, *got[0].shape[1:]), got[0].dtype),
            pltpu.SemaphoreType.DMA(()),
            pltpu.SemaphoreType.DMA((n,)),
        ],
        compiler_params=room(16),
        name="absorb",
    )(me, w_uk, *got, *tokens)


def split_kernel(spans, x_ref, *refs):
    for (a, b), ref in zip(spans, refs[-len(spans) :]):
        ref[...] = x_ref[:, a:b]


def split(x, spans, tokens):
    return pl.pallas_call(
        functools.partial(split_kernel, spans),
        grid=(1,),
        in_specs=[pl.BlockSpec(x.shape, lambda i: (0, 0))] + [ANY] * len(tokens),
        out_specs=[pl.BlockSpec((x.shape[0], b - a), lambda i: (0, 0)) for a, b in spans],
        out_shape=[jax.ShapeDtypeStruct((x.shape[0], b - a), x.dtype) for a, b in spans],
        compiler_params=room(16),
        name="split",
    )(x, *tokens)


def finish_kernel(count, m_ref, l_ref, acc_ref, far_ref, w_ref, span_ref, dec_ref):
    rows = m_ref.shape[0]
    heads = w_ref.shape[0]
    scale = score_scale * LOG2E
    parts = far_ref[rows:, :].astype(jnp.float32)
    packed = parts[:, :LANES] + parts[:, LANES : 2 * LANES] + parts[:, 2 * LANES : 3 * LANES]
    columns = []
    for g in range(rows // LANES):
        row = jnp.broadcast_to(packed[g : g + 1, :], (LANES, LANES))
        columns.append(jnp.transpose(row))
    far = jnp.concatenate(columns, axis=0)
    near = m_ref[...] * scale
    top = jnp.maximum(near, far)
    w_near = jnp.exp2(near - top)
    w_far = jnp.exp2(far - top)
    total = l_ref[...] * w_near + w_far
    inverse = 1.0 / total
    w_near = lanes(w_near * inverse, DC)
    w_far = lanes(w_far * inverse, DC)
    for h in range(heads):
        a, b = h * count, (h + 1) * count
        near_part = acc_ref[a:b, :] * w_near[a:b, :]
        far_part = far_ref[:rows, :].astype(jnp.float32)[a:b, :] * w_far[a:b, :]
        latent = (near_part + far_part).astype(jnp.bfloat16)
        done = jnp.dot(latent, w_ref[h], preferred_element_type=jnp.float32)
        span = span_ref.shape[0]
        span_ref[:, h * LANES : (h + 1) * LANES] = done[:span].astype(jnp.bfloat16)
        dec_ref[:, h * LANES : (h + 1) * LANES] = done[span:].astype(jnp.bfloat16)


def finish(count, span, state, far, w_uv):
    heads = w_uv.shape[0]
    wide = heads * w_uv.shape[2]
    return pl.pallas_call(
        functools.partial(finish_kernel, count),
        out_shape=(
            jax.ShapeDtypeStruct((span, wide), jnp.bfloat16),
            jax.ShapeDtypeStruct((count - span, wide), jnp.bfloat16),
        ),
        compiler_params=room(24),
        cost_estimate=pl.CostEstimate(
            flops=2 * count * heads * DC * w_uv.shape[2],
            bytes_accessed=2 * w_uv.size + 6 * state[2].size,
            transcendentals=0,
        ),
        name="finish",
    )(*state, far, w_uv)


def body(query, dec_query, cache_kv, span_kv, dec_kv, cache_fill, owner, slot, dec_len, w_uk, w_uv):
    me = lax.axis_index("seq")
    n = lax.axis_size("seq")
    pos_dev = cache_kv.shape[0]
    span = owner.shape[0]
    rows_dec = dec_len.shape[0]
    count = span + rows_dec
    heads = w_uk.shape[0]
    row = cache_kv.shape[1]

    def swap(x, stride):
        return lax.ppermute(x, "seq", [(i, i ^ stride) for i in range(n)])

    far, pair = n // 2, n // 4
    near = [1 << b for b in range(pair.bit_length() - 1)]
    keys = cache_kv.T
    edges = [0, pos_dev // 4, pos_dev // 8 * 5, pos_dev]

    lead = keys[:, : edges[1]]
    pieces = [swap(lead, far)]

    place = me[None].astype(jnp.int32)
    order = [[r for r in range(n) if not r & 1], [r for r in range(n) if r & 1]]
    stay, go = pack(order, place, query, dec_query, span_kv, dec_kv)
    come = swap(go, 1)
    groups = {r: [(0, stay[i]), (1, come[i])] for i, r in enumerate(order[0])}
    for stride in near[1:]:
        away = [r for r in groups if r & stride]
        moved = swap(jnp.stack([x for r in away for _, x in groups[r]]), stride)
        held = len(groups[away[0]])
        for i, r in enumerate(away):
            kept = groups[r ^ stride]
            kept += [(o ^ stride, moved[i * held + j]) for j, (o, _) in enumerate(groups.pop(r))]
    got, order = [], []
    for r in sorted(groups):
        got.append(jnp.stack([x for _, x in groups[r]]))
        order.append([r ^ o for o, _ in groups[r]])
    got = got[:1] + [swap(x, r) for r, x in zip(sorted(groups)[1:], got[1:])]

    middle = pos_dev // 2
    *cuts, early, late = split(
        keys, [*zip(edges[1:], edges[2:]), (0, middle), (middle, pos_dev)], [come]
    )
    early, late = [(0, early)], [(0, late)]
    for stride in near:
        early += [(o ^ stride, swap(x, stride)) for o, x in early]
    absorbed, extra = absorb(
        count, rows_dec // n, place, order, got, w_uk, row, pieces + [x for _, x in early[1:]]
    )
    new_rows = extra[:span]
    other = swap(absorbed, pair)
    late[0] = (0, after(late[0][1], absorbed))
    for stride in near:
        late += [(o ^ stride, swap(x, stride)) for o, x in late]
    halves = [(o, x, y) for (o, x), (_, y) in zip(early, late)]
    pieces += [swap(after(x, absorbed), far) for x in cuts]

    def spread(x):
        part = [(far, x)]
        for stride in near:
            part += [(offset ^ stride, swap(y, stride)) for offset, y in part]
        return part

    target = jnp.where(owner == me, slot, -1)
    onehot = jnp.arange(pos_dev, dtype=jnp.int32)[None, :] == target[:, None]
    placed = lax.dot_general(
        new_rows,
        onehot.astype(jnp.bfloat16),
        (((0,), (0,)), ((), ())),
        preferred_element_type=jnp.float32,
    ).astype(jnp.bfloat16)
    new_cache = jnp.where(jnp.any(onehot, axis=0)[None, :], placed, keys).T

    limits = jnp.concatenate([jnp.arange(1, span + 1, dtype=jnp.int32), dec_len])
    index = jnp.arange(LANES, dtype=jnp.int32)
    queries = jnp.arange(count, dtype=jnp.int32)
    seen = (index[None, :] < span) & (index[None, :] < limits[:, None])
    seen |= (index[None, :] >= span) & (index[None, :] == queries[:, None])
    bias = jnp.where(seen, 0.0, HIDDEN).astype(jnp.float32)
    held = [offset for offset, _, _ in halves]
    offsets = held + [offset ^ far for offset in held]
    which = jnp.stack([me ^ offset for offset in offsets])
    fills = jnp.sum(
        jnp.where(which[:, None] == jnp.arange(n, dtype=jnp.int32)[None, :], cache_fill[None, :], 0),
        axis=1,
    )
    base = len(halves)
    tile = heads // 2 * count

    def stage_of(c, part):
        return [(edges[c], base + i, x) for i, (_, x) in enumerate(part)]

    home = [(0, 0, keys)]
    side = [(a, i, z) for i, (_, x, y) in enumerate(halves) if i for a, z in ((0, x), (middle, y))]
    state = attend(fills, absorbed, home, tile, new=(extra, bias))
    side += stage_of(0, spread(pieces[0]))
    state = attend(fills, absorbed, side, tile, state=state)
    first = stage_of(1, spread(after(pieces[1], state[0])))
    other = after(other, state[0], pieces[1])
    guest = attend(fills, other, home + side, tile)
    second = stage_of(2, spread(after(pieces[2], guest[0])))
    first, second = first + second[:1], second[1:]
    other = after(other, pieces[2])
    guest = attend(fills, other, first, tile, state=guest)
    sent = attend(fills, other, second, tile, state=guest, last=True)
    back = swap(sent, pair)
    state = attend(fills, absorbed, first + second, tile, state=state)
    span_out, dec_out = finish(count, span, state, back, w_uv)
    return (span_out, dec_out, new_cache)


def solution(mesh):
    in_specs = (
        P(("grp", "seq"), None),
        P(("grp", "seq"), None),
        P(("grp", "seq"), None),
        P(("grp", "seq"), None),
        P(("grp", "seq"), None),
        P("grp"),
        P("grp"),
        P("grp"),
        P("grp"),
        P("seq", None, None),
        P("seq", None, None),
    )
    out_specs = (P("grp", "seq"), P("grp", "seq"), P(("grp", "seq"), None))
    return jax.shard_map(body, mesh=mesh, in_specs=in_specs, out_specs=out_specs, check_vma=False)
```

```python
import functools

import jax
import jax.numpy as jnp
from jax import lax
from jax.experimental import pallas as pl
from jax.experimental.pallas import tpu as pltpu
from jax.sharding import PartitionSpec as P

DN = 128
DC = 512
LANES = 128
ANY = pl.BlockSpec(memory_space=pl.ANY)
WHOLE = pl.BlockSpec(memory_space=pltpu.VMEM)


def room(mebibytes):
    return pltpu.CompilerParams(vmem_limit_bytes=mebibytes * 1024 * 1024)

score_scale = 0.1353
LOG2E = 1.4426950408889634
HIDDEN = -1e30
FLOOR = -1e25


def lanes(x, width):
    return jnp.concatenate([x] * (width // LANES), axis=1) if width > LANES else x


def attend_kernel(pieces, extra, first, last, tile, *refs):
    refs = list(refs)
    fills = refs.pop(0)
    q_ref = refs.pop(0)
    keys = [refs.pop(0) for _ in pieces]
    if extra:
        new_ref = refs.pop(0)
        bias_ref = refs.pop(0)
    if not first:
        m_in, l_in, acc_in = refs.pop(0), refs.pop(0), refs.pop(0)
    scale = score_scale * LOG2E
    weights = []
    for at in range(0, q_ref.shape[0], tile):
        rows = slice(at, at + tile)
        q = q_ref[rows, : keys[0].shape[0]]
        scores = []
        for (start, width, which), ref in zip(pieces, keys):
            s = jnp.dot(q, ref[...], preferred_element_type=jnp.float32)
            slot = start + lax.broadcasted_iota(jnp.int32, (1, width), 1)
            scores.append(jnp.where(slot < fills[which], s, HIDDEN))
        if extra:
            s = lax.dot_general(
                q, new_ref[...], (((1,), (1,)), ((), ())), preferred_element_type=jnp.float32
            )
            bias = bias_ref[...]
            scores.append(s + jnp.concatenate([bias] * (tile // bias.shape[0]), axis=0))
        peak = functools.reduce(jnp.maximum, [jnp.max(s, axis=1, keepdims=True) for s in scores])
        peak = jnp.maximum(peak, FLOOR)
        if not first:
            old = m_in[rows, :1]
            peak = jnp.maximum(peak, old)
        total = 0.0
        acc = 0.0
        for i, s in enumerate(scores):
            e = jnp.exp2((s - peak) * scale)
            total = total + jnp.sum(e, axis=1, keepdims=True)
            w = e.astype(jnp.bfloat16)
            if i < len(pieces):
                acc = acc + lax.dot_general(
                    w, keys[i][:DC, :], (((1,), (1,)), ((), ())), preferred_element_type=jnp.float32
                )
            else:
                acc = acc + jnp.dot(w, new_ref[:, :DC], preferred_element_type=jnp.float32)
        if not first:
            keep = jnp.exp2((old - peak) * scale)
            total = total + l_in[rows, :1] * keep
            acc = acc + acc_in[rows, :] * keep
        if last:
            refs[0][rows, :] = (acc * (1.0 / total)).astype(jnp.bfloat16)
            weights.append(jnp.broadcast_to(peak * scale + jnp.log2(total), (tile, LANES)))
        else:
            m_out, l_out, acc_out = refs
            m_out[rows, :] = jnp.broadcast_to(peak, (tile, LANES))
            l_out[rows, :] = jnp.broadcast_to(total, (tile, LANES))
            acc_out[rows, :] = acc
    if not last:
        return
    out = refs[0]
    count = q_ref.shape[0]
    weight = jnp.concatenate(weights, axis=0)
    tail = out.shape[0] - count
    place = lax.broadcasted_iota(jnp.int32, (tail, LANES), 0)
    packed = jnp.zeros((tail, LANES), jnp.float32)
    for g in range(count // LANES):
        turned = jnp.transpose(weight[g * LANES : (g + 1) * LANES, :])
        packed = jnp.where(place == g, turned[:tail, :], packed)
    high = packed.astype(jnp.bfloat16)
    rest = packed - high.astype(jnp.float32)
    mid = rest.astype(jnp.bfloat16)
    low = (rest - mid.astype(jnp.float32)).astype(jnp.bfloat16)
    out[count:, :] = jnp.concatenate([high, mid, low, jnp.zeros_like(low)], axis=1)


def attend(fills, q, pieces, tile, new=None, state=None, last=False):
    rows = q.shape[0]
    spec = tuple((start, keys.shape[1], which) for start, which, keys in pieces)
    operands = [fills, q] + [keys for _, _, keys in pieces]
    if new is not None:
        operands += list(new)
    aliases = {}
    if state is not None:
        if not last:
            aliases = {len(operands) + i: i for i in range(3)}
        operands += list(state)
    if last:
        tail = -(-rows // (LANES * 16)) * 16
        out_shape = [jax.ShapeDtypeStruct((rows + tail, DC), jnp.bfloat16)]
    else:
        out_shape = [
            jax.ShapeDtypeStruct((rows, LANES), jnp.float32),
            jax.ShapeDtypeStruct((rows, LANES), jnp.float32),
            jax.ShapeDtypeStruct((rows, DC), jnp.float32),
        ]
    out = pl.pallas_call(
        functools.partial(attend_kernel, spec, new is not None, state is None, last, tile),
        in_specs=[pl.BlockSpec(memory_space=pltpu.SMEM)] + [WHOLE] * (len(operands) - 1),
        out_specs=[WHOLE] * len(out_shape),
        out_shape=out_shape,
        input_output_aliases=aliases,
        compiler_params=room(24),
        cost_estimate=pl.CostEstimate(flops=0, bytes_accessed=0, transcendentals=0),
        name="attend",
    )(*operands)
    return out[0] if last else out


def after_kernel(x_ref, *refs):
    pass


def after(x, *tokens):
    return pl.pallas_call(
        after_kernel,
        in_specs=[ANY] * (1 + len(tokens)),
        out_specs=ANY,
        out_shape=jax.ShapeDtypeStruct(x.shape, x.dtype),
        input_output_aliases={0: 0},
        compiler_params=room(1),
        name="after",
    )(x, *tokens)


def pack_kernel(order, me_ref, query_ref, dec_ref, span_kv_ref, dec_kv_ref, *out_refs):
    per, row = span_kv_ref.shape
    per_dec = dec_ref.shape[0]
    n = sum(len(x) for x in order)
    part = query_ref.shape[1] // n
    cut = part // per
    pad = -(-row // LANES) * LANES - row

    def padded(ref):
        x = ref[...].astype(jnp.float32)
        return jnp.concatenate([x, jnp.zeros((x.shape[0], pad), jnp.float32)], axis=1)

    dec_kv = padded(dec_kv_ref)
    tail = [padded(span_kv_ref)]
    for e in range(per_dec):
        for j in range(0, row + pad, per * LANES):
            ends = range(j, min(j + per * LANES, row + pad), LANES)
            strips = [dec_kv[e : e + 1, k : k + LANES] for k in ends]
            strips += [jnp.zeros((1, LANES), jnp.float32)] * (per - len(strips))
            tail.append(jnp.concatenate(strips, axis=0))
    tail = jnp.concatenate(tail, axis=1).astype(jnp.bfloat16)
    places = [(ref, i, r) for ref, rs in zip(out_refs, order) for i, r in enumerate(rs)]
    for out_ref, j, r in places:
        begin = (me_ref[0] ^ r) * part
        out_ref[j, :, :part] = query_ref[:, pl.ds(pl.multiple_of(begin, LANES), part)]
        for e in range(per_dec):
            strips = []
            for i in range(per):
                at = pl.multiple_of(begin + i * cut, LANES)
                strips.append(dec_ref[e : e + 1, pl.ds(at, cut)].astype(jnp.float32))
            at = part + e * cut
            out_ref[j, :, at : at + cut] = jnp.concatenate(strips, axis=0).astype(jnp.bfloat16)
        out_ref[j, :, part + per_dec * cut :] = tail


def pack(order, me, query, dec_query, span_kv, dec_kv):
    n = sum(len(x) for x in order)
    per, row = span_kv.shape
    per_dec = dec_kv.shape[0]
    part = query.shape[1] // n
    wide = -(-row // LANES) * LANES
    fold = -(-wide // (per * LANES)) * LANES
    total = part + per_dec * (part // per) + wide + per_dec * fold
    operands = (query, dec_query, span_kv, dec_kv)
    return pl.pallas_call(
        functools.partial(pack_kernel, order),
        grid=(1,),
        in_specs=[pl.BlockSpec(memory_space=pltpu.SMEM)]
        + [pl.BlockSpec(x.shape, lambda i: (0, 0)) for x in operands],
        out_specs=[pl.BlockSpec((len(x), per, total), lambda i: (0, 0, 0)) for x in order],
        out_shape=[jax.ShapeDtypeStruct((len(x), per, total), jnp.bfloat16) for x in order],
        compiler_params=room(60),
        name="pack",
    )(me, *operands)


def absorb_kernel(per_dec, order, me_ref, w_hbm, *refs):
    got_refs, refs = refs[: len(order)], refs[-6:]
    absorbed_ref, extra_ref, w_ref, placed, w_sem, sems = refs
    heads = w_ref.shape[0]
    n, per, total = placed.shape
    row = extra_ref.shape[1]
    count = absorbed_ref.shape[0] // heads
    wide = -(-row // LANES) * LANES
    fold = -(-wide // (per * LANES)) * LANES
    part = (total - wide - per_dec * fold) * per // (per + per_dec)
    width = part // heads
    cut = part // per
    at = part + per_dec * cut
    weights = pltpu.make_async_copy(w_hbm, w_ref, w_sem)
    weights.start()
    copies = [
        pltpu.make_async_copy(ref.at[i], placed.at[me_ref[0] ^ r], sems.at[r])
        for ref, rs in zip(got_refs, order)
        for i, r in enumerate(rs)
    ]
    for copy in copies:
        copy.start()
    for copy in copies:
        copy.wait()

    def unfold(x, length):
        strips = []
        for j in range(0, x.shape[1], length):
            strips += [x[i : i + 1, j : j + length] for i in range(per)]
        return jnp.concatenate(strips, axis=1)

    blocks = [placed[d].astype(jnp.float32) for d in range(n)]
    queries = [x[:, :part] for x in blocks]
    fresh = [x[:, at : at + wide] for x in blocks]
    for x in blocks:
        for e in range(per_dec):
            queries.append(unfold(x[:, part + e * cut : part + (e + 1) * cut], cut))
            begin = at + wide + e * fold
            fresh.append(unfold(x[:, begin : begin + fold], LANES)[:, :wide])
    q = jnp.concatenate(queries, axis=0).astype(jnp.bfloat16)
    new = jnp.concatenate(fresh, axis=0)
    blank = jnp.zeros((count, absorbed_ref.shape[1] - row), jnp.float32)
    weights.wait()
    for h in range(0, heads, 2):
        parts = []
        for g in (h, h + 1):
            mine = q[:, g * width : (g + 1) * width]
            latent = jnp.dot(mine[:, :DN], w_ref[g], preferred_element_type=jnp.float32)
            rope = mine[:, DN:].astype(jnp.float32)
            parts.append(jnp.concatenate([latent, rope, blank], axis=1))
        pair = jnp.concatenate(parts, axis=0).astype(jnp.bfloat16)
        absorbed_ref[h * count : (h + 2) * count, :] = pair
    blank = jnp.zeros((extra_ref.shape[0] - count, row), jnp.float32)
    extra_ref[...] = jnp.concatenate([new[:, :row], blank], axis=0).astype(jnp.bfloat16)


def absorb(count, per_dec, me, order, got, w_uk, row):
    heads = w_uk.shape[0]
    n = sum(len(x) for x in order)
    return pl.pallas_call(
        functools.partial(absorb_kernel, per_dec, order),
        in_specs=[pl.BlockSpec(memory_space=pltpu.SMEM)] + [ANY] * (1 + len(got)),
        out_shape=[
            jax.ShapeDtypeStruct((heads * count, -(-row // LANES) * LANES), jnp.bfloat16),
            jax.ShapeDtypeStruct((LANES, row), jnp.bfloat16),
        ],
        scratch_shapes=[
            pltpu.VMEM(w_uk.shape, w_uk.dtype),
            pltpu.VMEM((n, *got[0].shape[1:]), got[0].dtype),
            pltpu.SemaphoreType.DMA(()),
            pltpu.SemaphoreType.DMA((n,)),
        ],
        compiler_params=room(16),
        name="absorb",
    )(me, w_uk, *got)


def cut_kernel(spans, x_ref, *refs):
    for (a, b), ref in zip(spans, refs[-len(spans) :]):
        ref[...] = x_ref[:, a:b]


def cut(x, spans, tokens):
    return pl.pallas_call(
        functools.partial(cut_kernel, spans),
        in_specs=[WHOLE] + [ANY] * len(tokens),
        out_specs=[WHOLE] * len(spans),
        out_shape=[jax.ShapeDtypeStruct((x.shape[0], b - a), x.dtype) for a, b in spans],
        compiler_params=room(4),
        name="cut",
    )(x, *tokens)


def finish_kernel(count, m_ref, l_ref, acc_ref, far_ref, w_ref, span_ref, dec_ref):
    rows = m_ref.shape[0]
    heads = w_ref.shape[0]
    scale = score_scale * LOG2E
    parts = far_ref[rows:, :].astype(jnp.float32)
    packed = parts[:, :LANES] + parts[:, LANES : 2 * LANES] + parts[:, 2 * LANES : 3 * LANES]
    columns = []
    for g in range(rows // LANES):
        row = jnp.broadcast_to(packed[g : g + 1, :], (LANES, LANES))
        columns.append(jnp.transpose(row))
    far = jnp.concatenate(columns, axis=0)
    near = m_ref[...] * scale
    top = jnp.maximum(near, far)
    w_near = jnp.exp2(near - top)
    w_far = jnp.exp2(far - top)
    total = l_ref[...] * w_near + w_far
    inverse = 1.0 / total
    w_near = lanes(w_near * inverse, DC)
    w_far = lanes(w_far * inverse, DC)
    for h in range(heads):
        a, b = h * count, (h + 1) * count
        near_part = acc_ref[a:b, :] * w_near[a:b, :]
        far_part = far_ref[:rows, :].astype(jnp.float32)[a:b, :] * w_far[a:b, :]
        latent = (near_part + far_part).astype(jnp.bfloat16)
        done = jnp.dot(latent, w_ref[h], preferred_element_type=jnp.float32)
        span = span_ref.shape[0]
        span_ref[:, h * LANES : (h + 1) * LANES] = done[:span].astype(jnp.bfloat16)
        dec_ref[:, h * LANES : (h + 1) * LANES] = done[span:].astype(jnp.bfloat16)


def finish(count, span, state, far, w_uv):
    heads = w_uv.shape[0]
    wide = heads * w_uv.shape[2]
    return pl.pallas_call(
        functools.partial(finish_kernel, count),
        out_shape=(
            jax.ShapeDtypeStruct((span, wide), jnp.bfloat16),
            jax.ShapeDtypeStruct((count - span, wide), jnp.bfloat16),
        ),
        compiler_params=room(24),
        cost_estimate=pl.CostEstimate(
            flops=2 * count * heads * DC * w_uv.shape[2],
            bytes_accessed=2 * w_uv.size + 6 * state[2].size,
            transcendentals=0,
        ),
        name="finish",
    )(*state, far, w_uv)


def body(query, dec_query, cache_kv, span_kv, dec_kv, cache_fill, owner, slot, dec_len, w_uk, w_uv):
    me = lax.axis_index("seq")
    n = lax.axis_size("seq")
    pos_dev = cache_kv.shape[0]
    span = owner.shape[0]
    rows_dec = dec_len.shape[0]
    count = span + rows_dec
    heads = w_uk.shape[0]
    row = cache_kv.shape[1]

    def swap(x, stride):
        return lax.ppermute(x, "seq", [(i, i ^ stride) for i in range(n)])

    far, pair = n // 2, n // 4
    near = [1 << b for b in range(pair.bit_length() - 1)]
    keys = cache_kv.T
    edges = [i * (pos_dev // 8) for i in (0, 3, 6, 8)]

    place = me[None].astype(jnp.int32)
    order = [[r for r in range(n) if not r & 1], [r for r in range(n) if r & 1]]
    stay, go = pack(order, place, query, dec_query, span_kv, dec_kv)
    come = swap(go, 1)
    groups = {r: [(0, stay[i]), (1, come[i])] for i, r in enumerate(order[0])}
    for stride in near[1:]:
        away = [r for r in groups if r & stride]
        moved = swap(jnp.stack([x for r in away for _, x in groups[r]]), stride)
        held = len(groups[away[0]])
        for i, r in enumerate(away):
            kept = groups[r ^ stride]
            kept += [(o ^ stride, moved[i * held + j]) for j, (o, _) in enumerate(groups.pop(r))]
    got, order = [], []
    for r in sorted(groups):
        got.append(jnp.stack([x for _, x in groups[r]]))
        order.append([r ^ o for o, _ in groups[r]])
    got = got[:1] + [swap(x, r) for r, x in zip(sorted(groups)[1:], got[1:])]

    absorbed, extra = absorb(count, rows_dec // n, place, order, got, w_uk, row)
    other = swap(absorbed, pair)
    spans = [*zip(edges, edges[1:])]
    cuts = cut(keys, spans[:1], got[1:]) + cut(keys, spans[1:], [absorbed])
    pieces = [swap(x, far) for x in cuts]
    extra = after(extra, pieces[0])
    new_rows = extra[:span]
    blocks = [(0, cut(keys, [(0, pos_dev)], got[1:])[0])]
    for stride in near:
        blocks += [(offset ^ stride, swap(x, stride)) for offset, x in blocks]

    def spread(x):
        part = [(far, x)]
        for stride in near:
            part += [(offset ^ stride, swap(y, stride)) for offset, y in part]
        return part

    target = jnp.where(owner == me, slot, -1)
    onehot = jnp.arange(pos_dev, dtype=jnp.int32)[None, :] == target[:, None]
    placed = lax.dot_general(
        new_rows,
        onehot.astype(jnp.bfloat16),
        (((0,), (0,)), ((), ())),
        preferred_element_type=jnp.float32,
    ).astype(jnp.bfloat16)
    new_cache = jnp.where(jnp.any(onehot, axis=0)[None, :], placed, keys).T

    limits = jnp.concatenate([jnp.arange(1, span + 1, dtype=jnp.int32), dec_len])
    index = jnp.arange(LANES, dtype=jnp.int32)
    queries = jnp.arange(count, dtype=jnp.int32)
    seen = (index[None, :] < span) & (index[None, :] < limits[:, None])
    seen |= (index[None, :] >= span) & (index[None, :] == queries[:, None])
    bias = jnp.where(seen, 0.0, HIDDEN).astype(jnp.float32)
    held = [offset for offset, _ in blocks]
    offsets = held + [offset ^ far for offset in held]
    which = jnp.stack([me ^ offset for offset in offsets])
    fills = jnp.sum(
        jnp.where(which[:, None] == jnp.arange(n, dtype=jnp.int32)[None, :], cache_fill[None, :], 0),
        axis=1,
    )
    base = len(blocks)
    tile = heads // 2 * count

    def stage_of(c, part):
        return [(edges[c], base + i, x) for i, (_, x) in enumerate(part)]

    home = [(0, 0, keys)]
    side = [(0, i, x) for i, (_, x) in enumerate(blocks) if i]
    side += stage_of(0, spread(pieces[0]))
    state = attend(fills, absorbed, home, tile, new=(extra, bias))
    first = stage_of(1, spread(after(pieces[1], state[0])))
    state = attend(fills, absorbed, side, tile, state=state)
    other = after(other, state[0], pieces[1])
    guest = attend(fills, other, home + side, tile)
    second = stage_of(2, spread(after(pieces[2], guest[0])))
    first, second = first + second[:1], second[1:]
    other = after(other, pieces[2])
    guest = attend(fills, other, first, tile, state=guest)
    sent = attend(fills, other, second, tile, state=guest, last=True)
    back = swap(sent, pair)
    state = attend(fills, absorbed, first + second, tile, state=state)
    span_out, dec_out = finish(count, span, state, back, w_uv)
    return (span_out, dec_out, new_cache)


def solution(mesh):
    in_specs = (
        P(("grp", "seq"), None),
        P(("grp", "seq"), None),
        P(("grp", "seq"), None),
        P(("grp", "seq"), None),
        P(("grp", "seq"), None),
        P("grp"),
        P("grp"),
        P("grp"),
        P("grp"),
        P("seq", None, None),
        P("seq", None, None),
    )
    out_specs = (P("grp", "seq"), P("grp", "seq"), P(("grp", "seq"), None))
    return jax.shard_map(body, mesh=mesh, in_specs=in_specs, out_specs=out_specs, check_vma=False)
```

```python
import functools

import jax
import jax.numpy as jnp
from jax import lax
from jax.experimental import pallas as pl
from jax.experimental.pallas import tpu as pltpu
from jax.sharding import PartitionSpec as P

DN = 128
DC = 512
LANES = 128
ANY = pl.BlockSpec(memory_space=pl.ANY)
WHOLE = pl.BlockSpec(memory_space=pltpu.VMEM)


def room(mebibytes):
    return pltpu.CompilerParams(vmem_limit_bytes=mebibytes * 1024 * 1024)

score_scale = 0.1353
LOG2E = 1.4426950408889634
HIDDEN = -1e30
FLOOR = -1e25


def lanes(x, width):
    return jnp.concatenate([x] * (width // LANES), axis=1) if width > LANES else x


def attend_kernel(pieces, extra, first, last, tile, *refs):
    refs = list(refs)
    fills = refs.pop(0)
    q_ref = refs.pop(0)
    keys = [refs.pop(0) for _ in pieces]
    if extra:
        new_ref = refs.pop(0)
        bias_ref = refs.pop(0)
    if not first:
        m_in, l_in, acc_in = refs.pop(0), refs.pop(0), refs.pop(0)
    scale = score_scale * LOG2E
    weights = []
    for at in range(0, q_ref.shape[0], tile):
        rows = slice(at, at + tile)
        q = q_ref[rows, : keys[0].shape[0]]
        scores = []
        for (start, width, which), ref in zip(pieces, keys):
            s = jnp.dot(q, ref[...], preferred_element_type=jnp.float32)
            slot = start + lax.broadcasted_iota(jnp.int32, (1, width), 1)
            scores.append(jnp.where(slot < fills[which], s, HIDDEN))
        if extra:
            s = lax.dot_general(
                q, new_ref[...], (((1,), (1,)), ((), ())), preferred_element_type=jnp.float32
            )
            bias = bias_ref[...]
            scores.append(s + jnp.concatenate([bias] * (tile // bias.shape[0]), axis=0))
        peak = functools.reduce(jnp.maximum, [jnp.max(s, axis=1, keepdims=True) for s in scores])
        peak = jnp.maximum(peak, FLOOR)
        if not first:
            old = m_in[rows, :1]
            peak = jnp.maximum(peak, old)
        total = 0.0
        acc = 0.0
        for i, s in enumerate(scores):
            e = jnp.exp2((s - peak) * scale)
            total = total + jnp.sum(e, axis=1, keepdims=True)
            w = e.astype(jnp.bfloat16)
            if i < len(pieces):
                acc = acc + lax.dot_general(
                    w, keys[i][:DC, :], (((1,), (1,)), ((), ())), preferred_element_type=jnp.float32
                )
            else:
                acc = acc + jnp.dot(w, new_ref[:, :DC], preferred_element_type=jnp.float32)
        if not first:
            keep = jnp.exp2((old - peak) * scale)
            total = total + l_in[rows, :1] * keep
            acc = acc + acc_in[rows, :] * keep
        if last:
            refs[0][rows, :] = (acc * (1.0 / total)).astype(jnp.bfloat16)
            weights.append(jnp.broadcast_to(peak * scale + jnp.log2(total), (tile, LANES)))
        else:
            m_out, l_out, acc_out = refs
            m_out[rows, :] = jnp.broadcast_to(peak, (tile, LANES))
            l_out[rows, :] = jnp.broadcast_to(total, (tile, LANES))
            acc_out[rows, :] = acc
    if not last:
        return
    out = refs[0]
    count = q_ref.shape[0]
    weight = jnp.concatenate(weights, axis=0)
    tail = out.shape[0] - count
    place = lax.broadcasted_iota(jnp.int32, (tail, LANES), 0)
    packed = jnp.zeros((tail, LANES), jnp.float32)
    for g in range(count // LANES):
        turned = jnp.transpose(weight[g * LANES : (g + 1) * LANES, :])
        packed = jnp.where(place == g, turned[:tail, :], packed)
    high = packed.astype(jnp.bfloat16)
    rest = packed - high.astype(jnp.float32)
    mid = rest.astype(jnp.bfloat16)
    low = (rest - mid.astype(jnp.float32)).astype(jnp.bfloat16)
    out[count:, :] = jnp.concatenate([high, mid, low, jnp.zeros_like(low)], axis=1)


def attend(fills, q, pieces, tile, new=None, state=None, last=False):
    rows = q.shape[0]
    spec = tuple((start, keys.shape[1], which) for start, which, keys in pieces)
    operands = [fills, q] + [keys for _, _, keys in pieces]
    if new is not None:
        operands += list(new)
    aliases = {}
    if state is not None:
        if not last:
            aliases = {len(operands) + i: i for i in range(3)}
        operands += list(state)
    if last:
        tail = -(-rows // (LANES * 16)) * 16
        out_shape = [jax.ShapeDtypeStruct((rows + tail, DC), jnp.bfloat16)]
    else:
        out_shape = [
            jax.ShapeDtypeStruct((rows, LANES), jnp.float32),
            jax.ShapeDtypeStruct((rows, LANES), jnp.float32),
            jax.ShapeDtypeStruct((rows, DC), jnp.float32),
        ]
    out = pl.pallas_call(
        functools.partial(attend_kernel, spec, new is not None, state is None, last, tile),
        in_specs=[pl.BlockSpec(memory_space=pltpu.SMEM)] + [WHOLE] * (len(operands) - 1),
        out_specs=[WHOLE] * len(out_shape),
        out_shape=out_shape,
        input_output_aliases=aliases,
        compiler_params=room(24),
        cost_estimate=pl.CostEstimate(flops=0, bytes_accessed=0, transcendentals=0),
        name="attend",
    )(*operands)
    return out[0] if last else out


def after_kernel(x_ref, *refs):
    pass


def after(x, *tokens):
    return pl.pallas_call(
        after_kernel,
        in_specs=[ANY] * (1 + len(tokens)),
        out_specs=ANY,
        out_shape=jax.ShapeDtypeStruct(x.shape, x.dtype),
        input_output_aliases={0: 0},
        compiler_params=room(1),
        name="after",
    )(x, *tokens)


def pack_kernel(order, me_ref, query_ref, dec_ref, span_kv_ref, dec_kv_ref, *out_refs):
    per, row = span_kv_ref.shape
    per_dec = dec_ref.shape[0]
    n = sum(len(x) for x in order)
    part = query_ref.shape[1] // n
    cut = part // per
    pad = -(-row // LANES) * LANES - row

    def padded(ref):
        x = ref[...].astype(jnp.float32)
        return jnp.concatenate([x, jnp.zeros((x.shape[0], pad), jnp.float32)], axis=1)

    dec_kv = padded(dec_kv_ref)
    tail = [padded(span_kv_ref)]
    for e in range(per_dec):
        for j in range(0, row + pad, per * LANES):
            ends = range(j, min(j + per * LANES, row + pad), LANES)
            strips = [dec_kv[e : e + 1, k : k + LANES] for k in ends]
            strips += [jnp.zeros((1, LANES), jnp.float32)] * (per - len(strips))
            tail.append(jnp.concatenate(strips, axis=0))
    tail = jnp.concatenate(tail, axis=1).astype(jnp.bfloat16)
    places = [(ref, i, r) for ref, rs in zip(out_refs, order) for i, r in enumerate(rs)]
    for out_ref, j, r in places:
        begin = (me_ref[0] ^ r) * part
        out_ref[j, :, :part] = query_ref[:, pl.ds(pl.multiple_of(begin, LANES), part)]
        for e in range(per_dec):
            strips = []
            for i in range(per):
                at = pl.multiple_of(begin + i * cut, LANES)
                strips.append(dec_ref[e : e + 1, pl.ds(at, cut)].astype(jnp.float32))
            at = part + e * cut
            out_ref[j, :, at : at + cut] = jnp.concatenate(strips, axis=0).astype(jnp.bfloat16)
        out_ref[j, :, part + per_dec * cut :] = tail


def pack(order, me, query, dec_query, span_kv, dec_kv):
    n = sum(len(x) for x in order)
    per, row = span_kv.shape
    per_dec = dec_kv.shape[0]
    part = query.shape[1] // n
    wide = -(-row // LANES) * LANES
    fold = -(-wide // (per * LANES)) * LANES
    total = part + per_dec * (part // per) + wide + per_dec * fold
    operands = (query, dec_query, span_kv, dec_kv)
    return pl.pallas_call(
        functools.partial(pack_kernel, order),
        grid=(1,),
        in_specs=[pl.BlockSpec(memory_space=pltpu.SMEM)]
        + [pl.BlockSpec(x.shape, lambda i: (0, 0)) for x in operands],
        out_specs=[pl.BlockSpec((len(x), per, total), lambda i: (0, 0, 0)) for x in order],
        out_shape=[jax.ShapeDtypeStruct((len(x), per, total), jnp.bfloat16) for x in order],
        compiler_params=room(60),
        name="pack",
    )(me, *operands)


def absorb_kernel(per_dec, order, me_ref, w_hbm, *refs):
    got_refs, refs = refs[: len(order)], refs[-6:]
    absorbed_ref, extra_ref, w_ref, placed, w_sem, sems = refs
    heads = w_ref.shape[0]
    n, per, total = placed.shape
    row = extra_ref.shape[1]
    count = absorbed_ref.shape[0] // heads
    wide = -(-row // LANES) * LANES
    fold = -(-wide // (per * LANES)) * LANES
    part = (total - wide - per_dec * fold) * per // (per + per_dec)
    width = part // heads
    cut = part // per
    at = part + per_dec * cut
    weights = pltpu.make_async_copy(w_hbm, w_ref, w_sem)
    weights.start()
    copies = [
        pltpu.make_async_copy(ref.at[i], placed.at[me_ref[0] ^ r], sems.at[r])
        for ref, rs in zip(got_refs, order)
        for i, r in enumerate(rs)
    ]
    for copy in copies:
        copy.start()
    for copy in copies:
        copy.wait()

    def unfold(x, length):
        strips = []
        for j in range(0, x.shape[1], length):
            strips += [x[i : i + 1, j : j + length] for i in range(per)]
        return jnp.concatenate(strips, axis=1)

    blocks = [placed[d].astype(jnp.float32) for d in range(n)]
    queries = [x[:, :part] for x in blocks]
    fresh = [x[:, at : at + wide] for x in blocks]
    for x in blocks:
        for e in range(per_dec):
            queries.append(unfold(x[:, part + e * cut : part + (e + 1) * cut], cut))
            begin = at + wide + e * fold
            fresh.append(unfold(x[:, begin : begin + fold], LANES)[:, :wide])
    q = jnp.concatenate(queries, axis=0).astype(jnp.bfloat16)
    new = jnp.concatenate(fresh, axis=0)
    blank = jnp.zeros((count, absorbed_ref.shape[1] - row), jnp.float32)
    weights.wait()
    for h in range(0, heads, 2):
        parts = []
        for g in (h, h + 1):
            mine = q[:, g * width : (g + 1) * width]
            latent = jnp.dot(mine[:, :DN], w_ref[g], preferred_element_type=jnp.float32)
            rope = mine[:, DN:].astype(jnp.float32)
            parts.append(jnp.concatenate([latent, rope, blank], axis=1))
        pair = jnp.concatenate(parts, axis=0).astype(jnp.bfloat16)
        absorbed_ref[h * count : (h + 2) * count, :] = pair
    blank = jnp.zeros((extra_ref.shape[0] - count, row), jnp.float32)
    extra_ref[...] = jnp.concatenate([new[:, :row], blank], axis=0).astype(jnp.bfloat16)


def absorb(count, per_dec, me, order, got, w_uk, row):
    heads = w_uk.shape[0]
    n = sum(len(x) for x in order)
    return pl.pallas_call(
        functools.partial(absorb_kernel, per_dec, order),
        in_specs=[pl.BlockSpec(memory_space=pltpu.SMEM)] + [ANY] * (1 + len(got)),
        out_shape=[
            jax.ShapeDtypeStruct((heads * count, -(-row // LANES) * LANES), jnp.bfloat16),
            jax.ShapeDtypeStruct((LANES, row), jnp.bfloat16),
        ],
        scratch_shapes=[
            pltpu.VMEM(w_uk.shape, w_uk.dtype),
            pltpu.VMEM((n, *got[0].shape[1:]), got[0].dtype),
            pltpu.SemaphoreType.DMA(()),
            pltpu.SemaphoreType.DMA((n,)),
        ],
        compiler_params=room(16),
        name="absorb",
    )(me, w_uk, *got)


def cut_kernel(spans, x_ref, *refs):
    for (a, b), ref in zip(spans, refs[-len(spans) :]):
        ref[...] = x_ref[:, a:b]


def cut(x, spans, tokens):
    return pl.pallas_call(
        functools.partial(cut_kernel, spans),
        in_specs=[WHOLE] + [ANY] * len(tokens),
        out_specs=[WHOLE] * len(spans),
        out_shape=[jax.ShapeDtypeStruct((x.shape[0], b - a), x.dtype) for a, b in spans],
        compiler_params=room(4),
        name="cut",
    )(x, *tokens)


def finish_kernel(count, m_ref, l_ref, acc_ref, far_ref, w_ref, span_ref, dec_ref):
    rows = m_ref.shape[0]
    heads = w_ref.shape[0]
    scale = score_scale * LOG2E
    parts = far_ref[rows:, :].astype(jnp.float32)
    packed = parts[:, :LANES] + parts[:, LANES : 2 * LANES] + parts[:, 2 * LANES : 3 * LANES]
    columns = []
    for g in range(rows // LANES):
        row = jnp.broadcast_to(packed[g : g + 1, :], (LANES, LANES))
        columns.append(jnp.transpose(row))
    far = jnp.concatenate(columns, axis=0)
    near = m_ref[...] * scale
    top = jnp.maximum(near, far)
    w_near = jnp.exp2(near - top)
    w_far = jnp.exp2(far - top)
    total = l_ref[...] * w_near + w_far
    inverse = 1.0 / total
    w_near = lanes(w_near * inverse, DC)
    w_far = lanes(w_far * inverse, DC)
    for h in range(heads):
        a, b = h * count, (h + 1) * count
        near_part = acc_ref[a:b, :] * w_near[a:b, :]
        far_part = far_ref[:rows, :].astype(jnp.float32)[a:b, :] * w_far[a:b, :]
        latent = (near_part + far_part).astype(jnp.bfloat16)
        done = jnp.dot(latent, w_ref[h], preferred_element_type=jnp.float32)
        span = span_ref.shape[0]
        span_ref[:, h * LANES : (h + 1) * LANES] = done[:span].astype(jnp.bfloat16)
        dec_ref[:, h * LANES : (h + 1) * LANES] = done[span:].astype(jnp.bfloat16)


def finish(count, span, state, far, w_uv):
    heads = w_uv.shape[0]
    wide = heads * w_uv.shape[2]
    return pl.pallas_call(
        functools.partial(finish_kernel, count),
        out_shape=(
            jax.ShapeDtypeStruct((span, wide), jnp.bfloat16),
            jax.ShapeDtypeStruct((count - span, wide), jnp.bfloat16),
        ),
        compiler_params=room(24),
        cost_estimate=pl.CostEstimate(
            flops=2 * count * heads * DC * w_uv.shape[2],
            bytes_accessed=2 * w_uv.size + 6 * state[2].size,
            transcendentals=0,
        ),
        name="finish",
    )(*state, far, w_uv)


def body(query, dec_query, cache_kv, span_kv, dec_kv, cache_fill, owner, slot, dec_len, w_uk, w_uv):
    me = lax.axis_index("seq")
    n = lax.axis_size("seq")
    pos_dev = cache_kv.shape[0]
    span = owner.shape[0]
    rows_dec = dec_len.shape[0]
    count = span + rows_dec
    heads = w_uk.shape[0]
    row = cache_kv.shape[1]

    def swap(x, stride):
        return lax.ppermute(x, "seq", [(i, i ^ stride) for i in range(n)])

    far, pair = n // 2, n // 4
    near = [1 << b for b in range(pair.bit_length() - 1)]
    keys = cache_kv.T
    edges = [i * (pos_dev // 8) for i in (0, 3, 5, 7, 8)]

    place = me[None].astype(jnp.int32)
    order = [[r for r in range(n) if not r & 1], [r for r in range(n) if r & 1]]
    stay, go = pack(order, place, query, dec_query, span_kv, dec_kv)
    come = swap(go, 1)
    groups = {r: [(0, stay[i]), (1, come[i])] for i, r in enumerate(order[0])}
    for stride in near[1:]:
        away = [r for r in groups if r & stride]
        moved = swap(jnp.stack([x for r in away for _, x in groups[r]]), stride)
        held = len(groups[away[0]])
        for i, r in enumerate(away):
            kept = groups[r ^ stride]
            kept += [(o ^ stride, moved[i * held + j]) for j, (o, _) in enumerate(groups.pop(r))]
    got, order = [], []
    for r in sorted(groups):
        got.append(jnp.stack([x for _, x in groups[r]]))
        order.append([r ^ o for o, _ in groups[r]])
    got = got[:1] + [swap(x, r) for r, x in zip(sorted(groups)[1:], got[1:])]

    absorbed, extra = absorb(count, rows_dec // n, place, order, got, w_uk, row)
    other = swap(absorbed, pair)
    spans = [*zip(edges, edges[1:])]
    cuts = cut(keys, spans[:1], got[1:]) + cut(keys, spans[1:], [absorbed])
    pieces = [swap(x, far) for x in cuts]
    extra = after(extra, pieces[0])
    new_rows = extra[:span]
    blocks = [(0, cut(keys, [(0, pos_dev)], got[1:])[0])]
    for stride in near:
        blocks += [(offset ^ stride, swap(x, stride)) for offset, x in blocks]

    def spread(x):
        part = [(far, x)]
        for stride in near:
            part += [(offset ^ stride, swap(y, stride)) for offset, y in part]
        return part

    target = jnp.where(owner == me, slot, -1)
    onehot = jnp.arange(pos_dev, dtype=jnp.int32)[None, :] == target[:, None]
    placed = lax.dot_general(
        new_rows,
        onehot.astype(jnp.bfloat16),
        (((0,), (0,)), ((), ())),
        preferred_element_type=jnp.float32,
    ).astype(jnp.bfloat16)
    new_cache = jnp.where(jnp.any(onehot, axis=0)[None, :], placed, keys).T

    limits = jnp.concatenate([jnp.arange(1, span + 1, dtype=jnp.int32), dec_len])
    index = jnp.arange(LANES, dtype=jnp.int32)
    queries = jnp.arange(count, dtype=jnp.int32)
    seen = (index[None, :] < span) & (index[None, :] < limits[:, None])
    seen |= (index[None, :] >= span) & (index[None, :] == queries[:, None])
    bias = jnp.where(seen, 0.0, HIDDEN).astype(jnp.float32)
    held = [offset for offset, _ in blocks]
    offsets = held + [offset ^ far for offset in held]
    which = jnp.stack([me ^ offset for offset in offsets])
    fills = jnp.sum(
        jnp.where(which[:, None] == jnp.arange(n, dtype=jnp.int32)[None, :], cache_fill[None, :], 0),
        axis=1,
    )
    base = len(blocks)
    tile = heads // 2 * count

    def stage_of(c, part):
        return [(edges[c], base + i, x) for i, (_, x) in enumerate(part)]

    home = [(0, 0, keys)]
    side = [(0, i, x) for i, (_, x) in enumerate(blocks) if i]
    state = attend(fills, absorbed, home, tile, new=(extra, bias))
    first = stage_of(0, spread(pieces[0]))
    state = attend(fills, absorbed, side, tile, state=state)
    first += stage_of(1, spread(after(pieces[1], state[0])))
    other = after(other, state[0], pieces[1])
    guest = attend(fills, other, home + side, tile)
    second = stage_of(2, spread(after(pieces[2], guest[0])))
    other = after(other, pieces[2])
    guest = attend(fills, other, first, tile, state=guest)
    third = stage_of(3, spread(after(pieces[3], guest[0])))
    second, third = second + third[:1], third[1:]
    guest = attend(fills, other, second, tile, state=guest)
    sent = attend(fills, other, third, tile, state=guest, last=True)
    back = swap(sent, pair)
    state = attend(fills, absorbed, first + second + third, tile, state=state)
    span_out, dec_out = finish(count, span, state, back, w_uv)
    return (span_out, dec_out, new_cache)


def solution(mesh):
    in_specs = (
        P(("grp", "seq"), None),
        P(("grp", "seq"), None),
        P(("grp", "seq"), None),
        P(("grp", "seq"), None),
        P(("grp", "seq"), None),
        P("grp"),
        P("grp"),
        P("grp"),
        P("grp"),
        P("seq", None, None),
        P("seq", None, None),
    )
    out_specs = (P("grp", "seq"), P("grp", "seq"), P(("grp", "seq"), None))
    return jax.shard_map(body, mesh=mesh, in_specs=in_specs, out_specs=out_specs, check_vma=False)
```

```python
import functools

import jax
import jax.numpy as jnp
from jax import lax
from jax.experimental import pallas as pl
from jax.experimental.pallas import tpu as pltpu
from jax.sharding import PartitionSpec as P

DN = 128
DC = 512
LANES = 128
ANY = pl.BlockSpec(memory_space=pl.ANY)
WHOLE = pl.BlockSpec(memory_space=pltpu.VMEM)


def room(mebibytes):
    return pltpu.CompilerParams(vmem_limit_bytes=mebibytes * 1024 * 1024)

score_scale = 0.1353
LOG2E = 1.4426950408889634
HIDDEN = -1e30
FLOOR = -1e25


def lanes(x, width):
    return jnp.concatenate([x] * (width // LANES), axis=1) if width > LANES else x


def attend_kernel(pieces, extra, first, last, tile, *refs):
    refs = list(refs)
    fills = refs.pop(0)
    q_ref = refs.pop(0)
    keys = [refs.pop(0) for _ in pieces]
    if extra:
        new_ref = refs.pop(0)
        bias_ref = refs.pop(0)
    if not first:
        m_in, l_in, acc_in = refs.pop(0), refs.pop(0), refs.pop(0)
    scale = score_scale * LOG2E
    weights = []
    for at in range(0, q_ref.shape[0], tile):
        rows = slice(at, at + tile)
        q = q_ref[rows, : keys[0].shape[0]]
        scores = []
        for (start, width, which), ref in zip(pieces, keys):
            s = jnp.dot(q, ref[...], preferred_element_type=jnp.float32)
            slot = start + lax.broadcasted_iota(jnp.int32, (1, width), 1)
            scores.append(jnp.where(slot < fills[which], s, HIDDEN))
        if extra:
            s = lax.dot_general(
                q, new_ref[...], (((1,), (1,)), ((), ())), preferred_element_type=jnp.float32
            )
            bias = bias_ref[...]
            scores.append(s + jnp.concatenate([bias] * (tile // bias.shape[0]), axis=0))
        peak = functools.reduce(jnp.maximum, [jnp.max(s, axis=1, keepdims=True) for s in scores])
        peak = jnp.maximum(peak, FLOOR)
        if not first:
            old = m_in[rows, :1]
            peak = jnp.maximum(peak, old)
        total = 0.0
        acc = 0.0
        for i, s in enumerate(scores):
            e = jnp.exp2((s - peak) * scale)
            total = total + jnp.sum(e, axis=1, keepdims=True)
            w = e.astype(jnp.bfloat16)
            if i < len(pieces):
                acc = acc + lax.dot_general(
                    w, keys[i][:DC, :], (((1,), (1,)), ((), ())), preferred_element_type=jnp.float32
                )
            else:
                acc = acc + jnp.dot(w, new_ref[:, :DC], preferred_element_type=jnp.float32)
        if not first:
            keep = jnp.exp2((old - peak) * scale)
            total = total + l_in[rows, :1] * keep
            acc = acc + acc_in[rows, :] * keep
        if last:
            refs[0][rows, :] = (acc * (1.0 / total)).astype(jnp.bfloat16)
            weights.append(jnp.broadcast_to(peak * scale + jnp.log2(total), (tile, LANES)))
        else:
            m_out, l_out, acc_out = refs
            m_out[rows, :] = jnp.broadcast_to(peak, (tile, LANES))
            l_out[rows, :] = jnp.broadcast_to(total, (tile, LANES))
            acc_out[rows, :] = acc
    if not last:
        return
    out = refs[0]
    count = q_ref.shape[0]
    weight = jnp.concatenate(weights, axis=0)
    tail = out.shape[0] - count
    place = lax.broadcasted_iota(jnp.int32, (tail, LANES), 0)
    packed = jnp.zeros((tail, LANES), jnp.float32)
    for g in range(count // LANES):
        turned = jnp.transpose(weight[g * LANES : (g + 1) * LANES, :])
        packed = jnp.where(place == g, turned[:tail, :], packed)
    high = packed.astype(jnp.bfloat16)
    rest = packed - high.astype(jnp.float32)
    mid = rest.astype(jnp.bfloat16)
    low = (rest - mid.astype(jnp.float32)).astype(jnp.bfloat16)
    out[count:, :] = jnp.concatenate([high, mid, low, jnp.zeros_like(low)], axis=1)


def attend(fills, q, pieces, tile, new=None, state=None, last=False):
    rows = q.shape[0]
    spec = tuple((start, keys.shape[1], which) for start, which, keys in pieces)
    operands = [fills, q] + [keys for _, _, keys in pieces]
    if new is not None:
        operands += list(new)
    aliases = {}
    if state is not None:
        if not last:
            aliases = {len(operands) + i: i for i in range(3)}
        operands += list(state)
    if last:
        tail = -(-rows // (LANES * 16)) * 16
        out_shape = [jax.ShapeDtypeStruct((rows + tail, DC), jnp.bfloat16)]
    else:
        out_shape = [
            jax.ShapeDtypeStruct((rows, LANES), jnp.float32),
            jax.ShapeDtypeStruct((rows, LANES), jnp.float32),
            jax.ShapeDtypeStruct((rows, DC), jnp.float32),
        ]
    out = pl.pallas_call(
        functools.partial(attend_kernel, spec, new is not None, state is None, last, tile),
        in_specs=[pl.BlockSpec(memory_space=pltpu.SMEM)] + [WHOLE] * (len(operands) - 1),
        out_specs=[WHOLE] * len(out_shape),
        out_shape=out_shape,
        input_output_aliases=aliases,
        compiler_params=room(24),
        cost_estimate=pl.CostEstimate(flops=0, bytes_accessed=0, transcendentals=0),
        name="attend",
    )(*operands)
    return out[0] if last else out


def after_kernel(x_ref, *refs):
    pass


def after(x, *tokens):
    return pl.pallas_call(
        after_kernel,
        in_specs=[ANY] * (1 + len(tokens)),
        out_specs=ANY,
        out_shape=jax.ShapeDtypeStruct(x.shape, x.dtype),
        input_output_aliases={0: 0},
        compiler_params=room(1),
        name="after",
    )(x, *tokens)


def pack_kernel(order, me_ref, query_ref, dec_ref, span_kv_ref, dec_kv_ref, *out_refs):
    per, row = span_kv_ref.shape
    per_dec = dec_ref.shape[0]
    n = sum(len(x) for x in order)
    part = query_ref.shape[1] // n
    cut = part // per
    pad = -(-row // LANES) * LANES - row

    def padded(ref):
        x = ref[...].astype(jnp.float32)
        return jnp.concatenate([x, jnp.zeros((x.shape[0], pad), jnp.float32)], axis=1)

    dec_kv = padded(dec_kv_ref)
    tail = [padded(span_kv_ref)]
    for e in range(per_dec):
        for j in range(0, row + pad, per * LANES):
            ends = range(j, min(j + per * LANES, row + pad), LANES)
            strips = [dec_kv[e : e + 1, k : k + LANES] for k in ends]
            strips += [jnp.zeros((1, LANES), jnp.float32)] * (per - len(strips))
            tail.append(jnp.concatenate(strips, axis=0))
    tail = jnp.concatenate(tail, axis=1).astype(jnp.bfloat16)
    places = [(ref, i, r) for ref, rs in zip(out_refs, order) for i, r in enumerate(rs)]
    for out_ref, j, r in places:
        begin = (me_ref[0] ^ r) * part
        out_ref[j, :, :part] = query_ref[:, pl.ds(pl.multiple_of(begin, LANES), part)]
        for e in range(per_dec):
            strips = []
            for i in range(per):
                at = pl.multiple_of(begin + i * cut, LANES)
                strips.append(dec_ref[e : e + 1, pl.ds(at, cut)].astype(jnp.float32))
            at = part + e * cut
            out_ref[j, :, at : at + cut] = jnp.concatenate(strips, axis=0).astype(jnp.bfloat16)
        out_ref[j, :, part + per_dec * cut :] = tail


def pack(order, me, query, dec_query, span_kv, dec_kv):
    n = sum(len(x) for x in order)
    per, row = span_kv.shape
    per_dec = dec_kv.shape[0]
    part = query.shape[1] // n
    wide = -(-row // LANES) * LANES
    fold = -(-wide // (per * LANES)) * LANES
    total = part + per_dec * (part // per) + wide + per_dec * fold
    operands = (query, dec_query, span_kv, dec_kv)
    return pl.pallas_call(
        functools.partial(pack_kernel, order),
        grid=(1,),
        in_specs=[pl.BlockSpec(memory_space=pltpu.SMEM)]
        + [pl.BlockSpec(x.shape, lambda i: (0, 0)) for x in operands],
        out_specs=[pl.BlockSpec((len(x), per, total), lambda i: (0, 0, 0)) for x in order],
        out_shape=[jax.ShapeDtypeStruct((len(x), per, total), jnp.bfloat16) for x in order],
        compiler_params=room(60),
        name="pack",
    )(me, *operands)


def absorb_kernel(per_dec, order, me_ref, w_hbm, *refs):
    got_refs, refs = refs[: len(order)], refs[-6:]
    absorbed_ref, extra_ref, w_ref, placed, w_sem, sems = refs
    heads = w_ref.shape[0]
    n, per, total = placed.shape
    row = extra_ref.shape[1]
    count = absorbed_ref.shape[0] // heads
    wide = -(-row // LANES) * LANES
    fold = -(-wide // (per * LANES)) * LANES
    part = (total - wide - per_dec * fold) * per // (per + per_dec)
    width = part // heads
    cut = part // per
    at = part + per_dec * cut
    weights = pltpu.make_async_copy(w_hbm, w_ref, w_sem)
    weights.start()
    copies = [
        pltpu.make_async_copy(ref.at[i], placed.at[me_ref[0] ^ r], sems.at[r])
        for ref, rs in zip(got_refs, order)
        for i, r in enumerate(rs)
    ]
    for copy in copies:
        copy.start()
    for copy in copies:
        copy.wait()

    def unfold(x, length):
        strips = []
        for j in range(0, x.shape[1], length):
            strips += [x[i : i + 1, j : j + length] for i in range(per)]
        return jnp.concatenate(strips, axis=1)

    blocks = [placed[d].astype(jnp.float32) for d in range(n)]
    queries = [x[:, :part] for x in blocks]
    fresh = [x[:, at : at + wide] for x in blocks]
    for x in blocks:
        for e in range(per_dec):
            queries.append(unfold(x[:, part + e * cut : part + (e + 1) * cut], cut))
            begin = at + wide + e * fold
            fresh.append(unfold(x[:, begin : begin + fold], LANES)[:, :wide])
    q = jnp.concatenate(queries, axis=0).astype(jnp.bfloat16)
    new = jnp.concatenate(fresh, axis=0)
    blank = jnp.zeros((count, absorbed_ref.shape[1] - row), jnp.float32)
    weights.wait()
    for h in range(0, heads, 2):
        parts = []
        for g in (h, h + 1):
            mine = q[:, g * width : (g + 1) * width]
            latent = jnp.dot(mine[:, :DN], w_ref[g], preferred_element_type=jnp.float32)
            rope = mine[:, DN:].astype(jnp.float32)
            parts.append(jnp.concatenate([latent, rope, blank], axis=1))
        pair = jnp.concatenate(parts, axis=0).astype(jnp.bfloat16)
        absorbed_ref[h * count : (h + 2) * count, :] = pair
    blank = jnp.zeros((extra_ref.shape[0] - count, row), jnp.float32)
    extra_ref[...] = jnp.concatenate([new[:, :row], blank], axis=0).astype(jnp.bfloat16)


def absorb(count, per_dec, me, order, got, w_uk, row, tokens):
    heads = w_uk.shape[0]
    n = sum(len(x) for x in order)
    return pl.pallas_call(
        functools.partial(absorb_kernel, per_dec, order),
        in_specs=[pl.BlockSpec(memory_space=pltpu.SMEM)] + [ANY] * (1 + len(got) + len(tokens)),
        out_shape=[
            jax.ShapeDtypeStruct((heads * count, -(-row // LANES) * LANES), jnp.bfloat16),
            jax.ShapeDtypeStruct((LANES, row), jnp.bfloat16),
        ],
        scratch_shapes=[
            pltpu.VMEM(w_uk.shape, w_uk.dtype),
            pltpu.VMEM((n, *got[0].shape[1:]), got[0].dtype),
            pltpu.SemaphoreType.DMA(()),
            pltpu.SemaphoreType.DMA((n,)),
        ],
        compiler_params=room(16),
        name="absorb",
    )(me, w_uk, *got, *tokens)


def cut_kernel(spans, x_ref, *refs):
    for (a, b), ref in zip(spans, refs[-len(spans) :]):
        ref[...] = x_ref[:, a:b]


def cut(x, spans, tokens):
    return pl.pallas_call(
        functools.partial(cut_kernel, spans),
        in_specs=[WHOLE] + [ANY] * len(tokens),
        out_specs=[WHOLE] * len(spans),
        out_shape=[jax.ShapeDtypeStruct((x.shape[0], b - a), x.dtype) for a, b in spans],
        compiler_params=room(4),
        name="cut",
    )(x, *tokens)


def finish_kernel(count, m_ref, l_ref, acc_ref, far_ref, w_ref, span_ref, dec_ref):
    rows = m_ref.shape[0]
    heads = w_ref.shape[0]
    scale = score_scale * LOG2E
    parts = far_ref[rows:, :].astype(jnp.float32)
    packed = parts[:, :LANES] + parts[:, LANES : 2 * LANES] + parts[:, 2 * LANES : 3 * LANES]
    columns = []
    for g in range(rows // LANES):
        row = jnp.broadcast_to(packed[g : g + 1, :], (LANES, LANES))
        columns.append(jnp.transpose(row))
    far = jnp.concatenate(columns, axis=0)
    near = m_ref[...] * scale
    top = jnp.maximum(near, far)
    w_near = jnp.exp2(near - top)
    w_far = jnp.exp2(far - top)
    total = l_ref[...] * w_near + w_far
    inverse = 1.0 / total
    w_near = lanes(w_near * inverse, DC)
    w_far = lanes(w_far * inverse, DC)
    for h in range(heads):
        a, b = h * count, (h + 1) * count
        near_part = acc_ref[a:b, :] * w_near[a:b, :]
        far_part = far_ref[:rows, :].astype(jnp.float32)[a:b, :] * w_far[a:b, :]
        latent = (near_part + far_part).astype(jnp.bfloat16)
        done = jnp.dot(latent, w_ref[h], preferred_element_type=jnp.float32)
        span = span_ref.shape[0]
        span_ref[:, h * LANES : (h + 1) * LANES] = done[:span].astype(jnp.bfloat16)
        dec_ref[:, h * LANES : (h + 1) * LANES] = done[span:].astype(jnp.bfloat16)


def finish(count, span, state, far, w_uv):
    heads = w_uv.shape[0]
    wide = heads * w_uv.shape[2]
    return pl.pallas_call(
        functools.partial(finish_kernel, count),
        out_shape=(
            jax.ShapeDtypeStruct((span, wide), jnp.bfloat16),
            jax.ShapeDtypeStruct((count - span, wide), jnp.bfloat16),
        ),
        compiler_params=room(24),
        cost_estimate=pl.CostEstimate(
            flops=2 * count * heads * DC * w_uv.shape[2],
            bytes_accessed=2 * w_uv.size + 6 * state[2].size,
            transcendentals=0,
        ),
        name="finish",
    )(*state, far, w_uv)


def body(query, dec_query, cache_kv, span_kv, dec_kv, cache_fill, owner, slot, dec_len, w_uk, w_uv):
    me = lax.axis_index("seq")
    n = lax.axis_size("seq")
    pos_dev = cache_kv.shape[0]
    span = owner.shape[0]
    rows_dec = dec_len.shape[0]
    count = span + rows_dec
    heads = w_uk.shape[0]
    row = cache_kv.shape[1]

    def swap(x, stride):
        return lax.ppermute(x, "seq", [(i, i ^ stride) for i in range(n)])

    far, pair = n // 2, n // 4
    near = [1 << b for b in range(pair.bit_length() - 1)]
    keys = cache_kv.T
    edges = [i * (pos_dev // 8) for i in (0, 1, 5, 7, 8)]

    pieces = [swap(keys[:, : edges[1]], far)]

    place = me[None].astype(jnp.int32)
    order = [[r for r in range(n) if not r & 1], [r for r in range(n) if r & 1]]
    stay, go = pack(order, place, query, dec_query, span_kv, dec_kv)
    come = swap(go, 1)
    groups = {r: [(0, stay[i]), (1, come[i])] for i, r in enumerate(order[0])}
    for stride in near[1:]:
        away = [r for r in groups if r & stride]
        moved = swap(jnp.stack([x for r in away for _, x in groups[r]]), stride)
        held = len(groups[away[0]])
        for i, r in enumerate(away):
            kept = groups[r ^ stride]
            kept += [(o ^ stride, moved[i * held + j]) for j, (o, _) in enumerate(groups.pop(r))]
    got, order = [], []
    for r in sorted(groups):
        got.append(jnp.stack([x for _, x in groups[r]]))
        order.append([r ^ o for o, _ in groups[r]])
    got = got[:1] + [swap(x, r) for r, x in zip(sorted(groups)[1:], got[1:])]

    absorbed, extra = absorb(count, rows_dec // n, place, order, got, w_uk, row, pieces)
    new_rows = extra[:span]
    other = swap(absorbed, pair)
    spans = [*zip(edges, edges[1:])]
    cuts = cut(keys, spans[1:2], got[1:]) + cut(keys, spans[2:], [absorbed])
    pieces += [swap(x, far) for x in cuts]
    blocks = [(0, cut(keys, [(0, pos_dev)], got[1:])[0])]
    for stride in near:
        blocks += [(offset ^ stride, swap(x, stride)) for offset, x in blocks]

    def spread(x):
        part = [(far, x)]
        for stride in near:
            part += [(offset ^ stride, swap(y, stride)) for offset, y in part]
        return part

    target = jnp.where(owner == me, slot, -1)
    onehot = jnp.arange(pos_dev, dtype=jnp.int32)[None, :] == target[:, None]
    placed = lax.dot_general(
        new_rows,
        onehot.astype(jnp.bfloat16),
        (((0,), (0,)), ((), ())),
        preferred_element_type=jnp.float32,
    ).astype(jnp.bfloat16)
    new_cache = jnp.where(jnp.any(onehot, axis=0)[None, :], placed, keys).T

    limits = jnp.concatenate([jnp.arange(1, span + 1, dtype=jnp.int32), dec_len])
    index = jnp.arange(LANES, dtype=jnp.int32)
    queries = jnp.arange(count, dtype=jnp.int32)
    seen = (index[None, :] < span) & (index[None, :] < limits[:, None])
    seen |= (index[None, :] >= span) & (index[None, :] == queries[:, None])
    bias = jnp.where(seen, 0.0, HIDDEN).astype(jnp.float32)
    held = [offset for offset, _ in blocks]
    offsets = held + [offset ^ far for offset in held]
    which = jnp.stack([me ^ offset for offset in offsets])
    fills = jnp.sum(
        jnp.where(which[:, None] == jnp.arange(n, dtype=jnp.int32)[None, :], cache_fill[None, :], 0),
        axis=1,
    )
    base = len(blocks)
    tile = heads // 2 * count

    def stage_of(c, part):
        return [(edges[c], base + i, x) for i, (_, x) in enumerate(part)]

    home = [(0, 0, keys)]
    side = [(0, i, x) for i, (_, x) in enumerate(blocks) if i]
    state = attend(fills, absorbed, home, tile, new=(extra, bias))
    lead = stage_of(0, spread(pieces[0]))
    lead += stage_of(1, spread(after(pieces[1], state[0])))
    state = attend(fills, absorbed, side, tile, state=state)
    first = stage_of(2, spread(after(pieces[2], state[0])))
    other = after(other, state[0], pieces[2])
    guest = attend(fills, other, home + side + lead, tile)
    second = stage_of(3, spread(after(pieces[3], guest[0])))
    first, second = first + second[:1], second[1:]
    guest = attend(fills, other, first, tile, state=guest)
    sent = attend(fills, other, second, tile, state=guest, last=True)
    back = swap(sent, pair)
    state = attend(fills, absorbed, lead + first + second, tile, state=state)
    span_out, dec_out = finish(count, span, state, back, w_uv)
    return (span_out, dec_out, new_cache)


def solution(mesh):
    in_specs = (
        P(("grp", "seq"), None),
        P(("grp", "seq"), None),
        P(("grp", "seq"), None),
        P(("grp", "seq"), None),
        P(("grp", "seq"), None),
        P("grp"),
        P("grp"),
        P("grp"),
        P("grp"),
        P("seq", None, None),
        P("seq", None, None),
    )
    out_specs = (P("grp", "seq"), P("grp", "seq"), P(("grp", "seq"), None))
    return jax.shard_map(body, mesh=mesh, in_specs=in_specs, out_specs=out_specs, check_vma=False)
```

```python
import functools

import jax
import jax.numpy as jnp
from jax import lax
from jax.experimental import pallas as pl
from jax.experimental.pallas import tpu as pltpu
from jax.sharding import PartitionSpec as P

DN = 128
DC = 512
LANES = 128
ANY = pl.BlockSpec(memory_space=pl.ANY)
WHOLE = pl.BlockSpec(memory_space=pltpu.VMEM)


def room(mebibytes):
    return pltpu.CompilerParams(vmem_limit_bytes=mebibytes * 1024 * 1024)

score_scale = 0.1353
LOG2E = 1.4426950408889634
HIDDEN = -1e30
FLOOR = -1e25


def lanes(x, width):
    return jnp.concatenate([x] * (width // LANES), axis=1) if width > LANES else x


def attend_kernel(pieces, extra, first, last, tile, *refs):
    refs = list(refs)
    fills = refs.pop(0)
    q_ref = refs.pop(0)
    keys = [refs.pop(0) for _ in pieces]
    if extra:
        new_ref = refs.pop(0)
        bias_ref = refs.pop(0)
    if not first:
        m_in, l_in, acc_in = refs.pop(0), refs.pop(0), refs.pop(0)
    scale = score_scale * LOG2E
    weights = []
    for at in range(0, q_ref.shape[0], tile):
        rows = slice(at, at + tile)
        q = q_ref[rows, : keys[0].shape[0]]
        scores = []
        for (start, width, which), ref in zip(pieces, keys):
            s = jnp.dot(q, ref[...], preferred_element_type=jnp.float32)
            slot = start + lax.broadcasted_iota(jnp.int32, (1, width), 1)
            scores.append(jnp.where(slot < fills[which], s, HIDDEN))
        if extra:
            s = lax.dot_general(
                q, new_ref[...], (((1,), (1,)), ((), ())), preferred_element_type=jnp.float32
            )
            bias = bias_ref[...]
            scores.append(s + jnp.concatenate([bias] * (tile // bias.shape[0]), axis=0))
        peak = functools.reduce(jnp.maximum, [jnp.max(s, axis=1, keepdims=True) for s in scores])
        peak = jnp.maximum(peak, FLOOR)
        if not first:
            old = m_in[rows, :1]
            peak = jnp.maximum(peak, old)
        total = 0.0
        acc = 0.0
        for i, s in enumerate(scores):
            e = jnp.exp2((s - peak) * scale)
            total = total + jnp.sum(e, axis=1, keepdims=True)
            w = e.astype(jnp.bfloat16)
            if i < len(pieces):
                acc = acc + lax.dot_general(
                    w, keys[i][:DC, :], (((1,), (1,)), ((), ())), preferred_element_type=jnp.float32
                )
            else:
                acc = acc + jnp.dot(w, new_ref[:, :DC], preferred_element_type=jnp.float32)
        if not first:
            keep = jnp.exp2((old - peak) * scale)
            total = total + l_in[rows, :1] * keep
            acc = acc + acc_in[rows, :] * keep
        if last:
            refs[0][rows, :] = (acc * (1.0 / total)).astype(jnp.bfloat16)
            weights.append(jnp.broadcast_to(peak * scale + jnp.log2(total), (tile, LANES)))
        else:
            m_out, l_out, acc_out = refs
            m_out[rows, :] = jnp.broadcast_to(peak, (tile, LANES))
            l_out[rows, :] = jnp.broadcast_to(total, (tile, LANES))
            acc_out[rows, :] = acc
    if not last:
        return
    out = refs[0]
    count = q_ref.shape[0]
    weight = jnp.concatenate(weights, axis=0)
    tail = out.shape[0] - count
    place = lax.broadcasted_iota(jnp.int32, (tail, LANES), 0)
    packed = jnp.zeros((tail, LANES), jnp.float32)
    for g in range(count // LANES):
        turned = jnp.transpose(weight[g * LANES : (g + 1) * LANES, :])
        packed = jnp.where(place == g, turned[:tail, :], packed)
    high = packed.astype(jnp.bfloat16)
    rest = packed - high.astype(jnp.float32)
    mid = rest.astype(jnp.bfloat16)
    low = (rest - mid.astype(jnp.float32)).astype(jnp.bfloat16)
    out[count:, :] = jnp.concatenate([high, mid, low, jnp.zeros_like(low)], axis=1)


def attend(fills, q, pieces, tile, new=None, state=None, last=False):
    rows = q.shape[0]
    spec = tuple((start, keys.shape[1], which) for start, which, keys in pieces)
    operands = [fills, q] + [keys for _, _, keys in pieces]
    if new is not None:
        operands += list(new)
    aliases = {}
    if state is not None:
        if not last:
            aliases = {len(operands) + i: i for i in range(3)}
        operands += list(state)
    if last:
        tail = -(-rows // (LANES * 16)) * 16
        out_shape = [jax.ShapeDtypeStruct((rows + tail, DC), jnp.bfloat16)]
    else:
        out_shape = [
            jax.ShapeDtypeStruct((rows, LANES), jnp.float32),
            jax.ShapeDtypeStruct((rows, LANES), jnp.float32),
            jax.ShapeDtypeStruct((rows, DC), jnp.float32),
        ]
    out = pl.pallas_call(
        functools.partial(attend_kernel, spec, new is not None, state is None, last, tile),
        in_specs=[pl.BlockSpec(memory_space=pltpu.SMEM)] + [WHOLE] * (len(operands) - 1),
        out_specs=[WHOLE] * len(out_shape),
        out_shape=out_shape,
        input_output_aliases=aliases,
        compiler_params=room(24),
        cost_estimate=pl.CostEstimate(flops=0, bytes_accessed=0, transcendentals=0),
        name="attend",
    )(*operands)
    return out[0] if last else out


def after_kernel(x_ref, *refs):
    pass


def after(x, *tokens):
    return pl.pallas_call(
        after_kernel,
        in_specs=[ANY] * (1 + len(tokens)),
        out_specs=ANY,
        out_shape=jax.ShapeDtypeStruct(x.shape, x.dtype),
        input_output_aliases={0: 0},
        compiler_params=room(1),
        name="after",
    )(x, *tokens)


def pack_kernel(order, me_ref, query_ref, dec_ref, span_kv_ref, dec_kv_ref, *out_refs):
    per, row = span_kv_ref.shape
    per_dec = dec_ref.shape[0]
    n = sum(len(x) for x in order)
    part = query_ref.shape[1] // n
    cut = part // per
    pad = -(-row // LANES) * LANES - row

    def padded(ref):
        x = ref[...].astype(jnp.float32)
        return jnp.concatenate([x, jnp.zeros((x.shape[0], pad), jnp.float32)], axis=1)

    dec_kv = padded(dec_kv_ref)
    tail = [padded(span_kv_ref)]
    for e in range(per_dec):
        for j in range(0, row + pad, per * LANES):
            ends = range(j, min(j + per * LANES, row + pad), LANES)
            strips = [dec_kv[e : e + 1, k : k + LANES] for k in ends]
            strips += [jnp.zeros((1, LANES), jnp.float32)] * (per - len(strips))
            tail.append(jnp.concatenate(strips, axis=0))
    tail = jnp.concatenate(tail, axis=1).astype(jnp.bfloat16)
    places = [(ref, i, r) for ref, rs in zip(out_refs, order) for i, r in enumerate(rs)]
    for out_ref, j, r in places:
        begin = (me_ref[0] ^ r) * part
        out_ref[j, :, :part] = query_ref[:, pl.ds(pl.multiple_of(begin, LANES), part)]
        for e in range(per_dec):
            strips = []
            for i in range(per):
                at = pl.multiple_of(begin + i * cut, LANES)
                strips.append(dec_ref[e : e + 1, pl.ds(at, cut)].astype(jnp.float32))
            at = part + e * cut
            out_ref[j, :, at : at + cut] = jnp.concatenate(strips, axis=0).astype(jnp.bfloat16)
        out_ref[j, :, part + per_dec * cut :] = tail


def pack(order, me, query, dec_query, span_kv, dec_kv):
    n = sum(len(x) for x in order)
    per, row = span_kv.shape
    per_dec = dec_kv.shape[0]
    part = query.shape[1] // n
    wide = -(-row // LANES) * LANES
    fold = -(-wide // (per * LANES)) * LANES
    total = part + per_dec * (part // per) + wide + per_dec * fold
    operands = (query, dec_query, span_kv, dec_kv)
    return pl.pallas_call(
        functools.partial(pack_kernel, order),
        grid=(1,),
        in_specs=[pl.BlockSpec(memory_space=pltpu.SMEM)]
        + [pl.BlockSpec(x.shape, lambda i: (0, 0)) for x in operands],
        out_specs=[pl.BlockSpec((len(x), per, total), lambda i: (0, 0, 0)) for x in order],
        out_shape=[jax.ShapeDtypeStruct((len(x), per, total), jnp.bfloat16) for x in order],
        compiler_params=room(60),
        name="pack",
    )(me, *operands)


def absorb_kernel(per_dec, order, me_ref, w_hbm, *refs):
    got_refs, refs = refs[: len(order)], refs[-6:]
    absorbed_ref, extra_ref, w_ref, placed, w_sem, sems = refs
    heads = w_ref.shape[0]
    n, per, total = placed.shape
    row = extra_ref.shape[1]
    count = absorbed_ref.shape[0] // heads
    wide = -(-row // LANES) * LANES
    fold = -(-wide // (per * LANES)) * LANES
    part = (total - wide - per_dec * fold) * per // (per + per_dec)
    width = part // heads
    cut = part // per
    at = part + per_dec * cut
    weights = pltpu.make_async_copy(w_hbm, w_ref, w_sem)
    weights.start()
    copies = [
        pltpu.make_async_copy(ref.at[i], placed.at[me_ref[0] ^ r], sems.at[r])
        for ref, rs in zip(got_refs, order)
        for i, r in enumerate(rs)
    ]
    for copy in copies:
        copy.start()
    for copy in copies:
        copy.wait()

    def unfold(x, length):
        strips = []
        for j in range(0, x.shape[1], length):
            strips += [x[i : i + 1, j : j + length] for i in range(per)]
        return jnp.concatenate(strips, axis=1)

    blocks = [placed[d].astype(jnp.float32) for d in range(n)]
    queries = [x[:, :part] for x in blocks]
    fresh = [x[:, at : at + wide] for x in blocks]
    for x in blocks:
        for e in range(per_dec):
            queries.append(unfold(x[:, part + e * cut : part + (e + 1) * cut], cut))
            begin = at + wide + e * fold
            fresh.append(unfold(x[:, begin : begin + fold], LANES)[:, :wide])
    q = jnp.concatenate(queries, axis=0).astype(jnp.bfloat16)
    new = jnp.concatenate(fresh, axis=0)
    blank = jnp.zeros((count, absorbed_ref.shape[1] - row), jnp.float32)
    weights.wait()
    for h in range(0, heads, 2):
        parts = []
        for g in (h, h + 1):
            mine = q[:, g * width : (g + 1) * width]
            latent = jnp.dot(mine[:, :DN], w_ref[g], preferred_element_type=jnp.float32)
            rope = mine[:, DN:].astype(jnp.float32)
            parts.append(jnp.concatenate([latent, rope, blank], axis=1))
        pair = jnp.concatenate(parts, axis=0).astype(jnp.bfloat16)
        absorbed_ref[h * count : (h + 2) * count, :] = pair
    blank = jnp.zeros((extra_ref.shape[0] - count, row), jnp.float32)
    extra_ref[...] = jnp.concatenate([new[:, :row], blank], axis=0).astype(jnp.bfloat16)


def absorb(count, per_dec, me, order, got, w_uk, row):
    heads = w_uk.shape[0]
    n = sum(len(x) for x in order)
    return pl.pallas_call(
        functools.partial(absorb_kernel, per_dec, order),
        in_specs=[pl.BlockSpec(memory_space=pltpu.SMEM)] + [ANY] * (1 + len(got)),
        out_shape=[
            jax.ShapeDtypeStruct((heads * count, -(-row // LANES) * LANES), jnp.bfloat16),
            jax.ShapeDtypeStruct((LANES, row), jnp.bfloat16),
        ],
        scratch_shapes=[
            pltpu.VMEM(w_uk.shape, w_uk.dtype),
            pltpu.VMEM((n, *got[0].shape[1:]), got[0].dtype),
            pltpu.SemaphoreType.DMA(()),
            pltpu.SemaphoreType.DMA((n,)),
        ],
        compiler_params=room(16),
        name="absorb",
    )(me, w_uk, *got)


def cut_kernel(spans, x_ref, *refs):
    for (a, b), ref in zip(spans, refs[-len(spans) :]):
        ref[...] = x_ref[:, a:b]


def cut(x, spans, tokens):
    return pl.pallas_call(
        functools.partial(cut_kernel, spans),
        in_specs=[WHOLE] + [ANY] * len(tokens),
        out_specs=[WHOLE] * len(spans),
        out_shape=[jax.ShapeDtypeStruct((x.shape[0], b - a), x.dtype) for a, b in spans],
        compiler_params=room(4),
        name="cut",
    )(x, *tokens)


def finish_kernel(count, m_ref, l_ref, acc_ref, far_ref, w_ref, span_ref, dec_ref):
    rows = m_ref.shape[0]
    heads = w_ref.shape[0]
    scale = score_scale * LOG2E
    parts = far_ref[rows:, :].astype(jnp.float32)
    packed = parts[:, :LANES] + parts[:, LANES : 2 * LANES] + parts[:, 2 * LANES : 3 * LANES]
    columns = []
    for g in range(rows // LANES):
        row = jnp.broadcast_to(packed[g : g + 1, :], (LANES, LANES))
        columns.append(jnp.transpose(row))
    far = jnp.concatenate(columns, axis=0)
    near = m_ref[...] * scale
    top = jnp.maximum(near, far)
    w_near = jnp.exp2(near - top)
    w_far = jnp.exp2(far - top)
    total = l_ref[...] * w_near + w_far
    inverse = 1.0 / total
    w_near = lanes(w_near * inverse, DC)
    w_far = lanes(w_far * inverse, DC)
    for h in range(heads):
        a, b = h * count, (h + 1) * count
        near_part = acc_ref[a:b, :] * w_near[a:b, :]
        far_part = far_ref[:rows, :].astype(jnp.float32)[a:b, :] * w_far[a:b, :]
        latent = (near_part + far_part).astype(jnp.bfloat16)
        done = jnp.dot(latent, w_ref[h], preferred_element_type=jnp.float32)
        span = span_ref.shape[0]
        span_ref[:, h * LANES : (h + 1) * LANES] = done[:span].astype(jnp.bfloat16)
        dec_ref[:, h * LANES : (h + 1) * LANES] = done[span:].astype(jnp.bfloat16)


def finish(count, span, state, far, w_uv):
    heads = w_uv.shape[0]
    wide = heads * w_uv.shape[2]
    return pl.pallas_call(
        functools.partial(finish_kernel, count),
        out_shape=(
            jax.ShapeDtypeStruct((span, wide), jnp.bfloat16),
            jax.ShapeDtypeStruct((count - span, wide), jnp.bfloat16),
        ),
        compiler_params=room(24),
        cost_estimate=pl.CostEstimate(
            flops=2 * count * heads * DC * w_uv.shape[2],
            bytes_accessed=2 * w_uv.size + 6 * state[2].size,
            transcendentals=0,
        ),
        name="finish",
    )(*state, far, w_uv)


def body(query, dec_query, cache_kv, span_kv, dec_kv, cache_fill, owner, slot, dec_len, w_uk, w_uv):
    me = lax.axis_index("seq")
    n = lax.axis_size("seq")
    pos_dev = cache_kv.shape[0]
    span = owner.shape[0]
    rows_dec = dec_len.shape[0]
    count = span + rows_dec
    heads = w_uk.shape[0]
    row = cache_kv.shape[1]

    def swap(x, stride):
        return lax.ppermute(x, "seq", [(i, i ^ stride) for i in range(n)])

    far, pair = n // 2, n // 4
    near = [1 << b for b in range(pair.bit_length() - 1)]
    keys = cache_kv.T
    edges = [i * (pos_dev // 8) for i in (0, 3, 6, 8)]

    place = me[None].astype(jnp.int32)
    order = [[r for r in range(n) if not r & 1], [r for r in range(n) if r & 1]]
    stay, go = pack(order, place, query, dec_query, span_kv, dec_kv)
    come = swap(go, 1)
    groups = {r: [(0, stay[i]), (1, come[i])] for i, r in enumerate(order[0])}
    for stride in near[1:]:
        away = [r for r in groups if r & stride]
        moved = swap(jnp.stack([x for r in away for _, x in groups[r]]), stride)
        held = len(groups[away[0]])
        for i, r in enumerate(away):
            kept = groups[r ^ stride]
            kept += [(o ^ stride, moved[i * held + j]) for j, (o, _) in enumerate(groups.pop(r))]
    got, order = [], []
    for r in sorted(groups):
        got.append(jnp.stack([x for _, x in groups[r]]))
        order.append([r ^ o for o, _ in groups[r]])
    got = got[:1] + [swap(x, r) for r, x in zip(sorted(groups)[1:], got[1:])]

    absorbed, extra = absorb(count, rows_dec // n, place, order, got, w_uk, row)
    other = swap(absorbed, pair)
    spans = [*zip(edges, edges[1:])]
    cuts = cut(keys, spans[:1], got[1:]) + cut(keys, spans[1:], [absorbed])
    pieces = [swap(x, far) for x in cuts]
    extra = after(extra, pieces[0])
    new_rows = extra[:span]
    blocks = [(0, cut(keys, [(0, pos_dev)], got[1:])[0])]
    for stride in near:
        blocks += [(offset ^ stride, swap(x, stride)) for offset, x in blocks]

    def spread(x):
        part = [(far, x)]
        for stride in near:
            part += [(offset ^ stride, swap(y, stride)) for offset, y in part]
        return part

    target = jnp.where(owner == me, slot, -1)
    onehot = jnp.arange(pos_dev, dtype=jnp.int32)[None, :] == target[:, None]
    placed = lax.dot_general(
        new_rows,
        onehot.astype(jnp.bfloat16),
        (((0,), (0,)), ((), ())),
        preferred_element_type=jnp.float32,
    ).astype(jnp.bfloat16)
    new_cache = jnp.where(jnp.any(onehot, axis=0)[None, :], placed, keys).T

    limits = jnp.concatenate([jnp.arange(1, span + 1, dtype=jnp.int32), dec_len])
    index = jnp.arange(LANES, dtype=jnp.int32)
    queries = jnp.arange(count, dtype=jnp.int32)
    seen = (index[None, :] < span) & (index[None, :] < limits[:, None])
    seen |= (index[None, :] >= span) & (index[None, :] == queries[:, None])
    bias = jnp.where(seen, 0.0, HIDDEN).astype(jnp.float32)
    held = [offset for offset, _ in blocks]
    offsets = held + [offset ^ far for offset in held]
    which = jnp.stack([me ^ offset for offset in offsets])
    fills = jnp.sum(
        jnp.where(which[:, None] == jnp.arange(n, dtype=jnp.int32)[None, :], cache_fill[None, :], 0),
        axis=1,
    )
    base = len(blocks)
    tile = heads // 2 * count

    def stage_of(c, part):
        return [(edges[c], base + i, x) for i, (_, x) in enumerate(part)]

    home = [(0, 0, keys)]
    side = [(0, i, x) for i, (_, x) in enumerate(blocks) if i]
    state = attend(fills, absorbed, home, tile, new=(extra, bias))
    lead = stage_of(0, spread(pieces[0]))
    state = attend(fills, absorbed, side, tile, state=state)
    first = stage_of(1, spread(after(pieces[1], state[0])))
    other = after(other, state[0], pieces[1])
    guest = attend(fills, other, home + side + lead, tile)
    second = stage_of(2, spread(after(pieces[2], guest[0])))
    first, second = first + second[:1], second[1:]
    guest = attend(fills, other, first, tile, state=guest)
    sent = attend(fills, other, second, tile, state=guest, last=True)
    back = swap(sent, pair)
    state = attend(fills, absorbed, lead + first + second, tile, state=state)
    span_out, dec_out = finish(count, span, state, back, w_uv)
    return (span_out, dec_out, new_cache)


def solution(mesh):
    in_specs = (
        P(("grp", "seq"), None),
        P(("grp", "seq"), None),
        P(("grp", "seq"), None),
        P(("grp", "seq"), None),
        P(("grp", "seq"), None),
        P("grp"),
        P("grp"),
        P("grp"),
        P("grp"),
        P("seq", None, None),
        P("seq", None, None),
    )
    out_specs = (P("grp", "seq"), P("grp", "seq"), P(("grp", "seq"), None))
    return jax.shard_map(body, mesh=mesh, in_specs=in_specs, out_specs=out_specs, check_vma=False)
```

```python
import functools

import jax
import jax.numpy as jnp
from jax import lax
from jax.experimental import pallas as pl
from jax.experimental.pallas import tpu as pltpu
from jax.sharding import PartitionSpec as P

DN = 128
DC = 512
LANES = 128
ANY = pl.BlockSpec(memory_space=pl.ANY)
WHOLE = pl.BlockSpec(memory_space=pltpu.VMEM)


def room(mebibytes):
    return pltpu.CompilerParams(vmem_limit_bytes=mebibytes * 1024 * 1024)

score_scale = 0.1353
LOG2E = 1.4426950408889634
HIDDEN = -1e30
FLOOR = -1e25


def lanes(x, width):
    return jnp.concatenate([x] * (width // LANES), axis=1) if width > LANES else x


def attend_kernel(pieces, extra, first, last, tile, *refs):
    refs = list(refs)
    fills = refs.pop(0)
    q_ref = refs.pop(0)
    keys = [refs.pop(0) for _ in pieces]
    if extra:
        new_ref = refs.pop(0)
        bias_ref = refs.pop(0)
    if not first:
        m_in, l_in, acc_in = refs.pop(0), refs.pop(0), refs.pop(0)
    scale = score_scale * LOG2E
    weights = []
    for at in range(0, q_ref.shape[0], tile):
        rows = slice(at, at + tile)
        q = q_ref[rows, : keys[0].shape[0]]
        scores = []
        for (start, width, which), ref in zip(pieces, keys):
            s = jnp.dot(q, ref[...], preferred_element_type=jnp.float32)
            slot = start + lax.broadcasted_iota(jnp.int32, (1, width), 1)
            scores.append(jnp.where(slot < fills[which], s, HIDDEN))
        if extra:
            s = lax.dot_general(
                q, new_ref[...], (((1,), (1,)), ((), ())), preferred_element_type=jnp.float32
            )
            bias = bias_ref[...]
            scores.append(s + jnp.concatenate([bias] * (tile // bias.shape[0]), axis=0))
        peak = functools.reduce(jnp.maximum, [jnp.max(s, axis=1, keepdims=True) for s in scores])
        peak = jnp.maximum(peak, FLOOR)
        if not first:
            old = m_in[rows, :1]
            peak = jnp.maximum(peak, old)
        total = 0.0
        acc = 0.0
        for i, s in enumerate(scores):
            e = jnp.exp2((s - peak) * scale)
            total = total + jnp.sum(e, axis=1, keepdims=True)
            w = e.astype(jnp.bfloat16)
            if i < len(pieces):
                acc = acc + lax.dot_general(
                    w, keys[i][:DC, :], (((1,), (1,)), ((), ())), preferred_element_type=jnp.float32
                )
            else:
                acc = acc + jnp.dot(w, new_ref[:, :DC], preferred_element_type=jnp.float32)
        if not first:
            keep = jnp.exp2((old - peak) * scale)
            total = total + l_in[rows, :1] * keep
            acc = acc + acc_in[rows, :] * keep
        if last:
            refs[0][rows, :] = (acc * (1.0 / total)).astype(jnp.bfloat16)
            weights.append(jnp.broadcast_to(peak * scale + jnp.log2(total), (tile, LANES)))
        else:
            m_out, l_out, acc_out = refs
            m_out[rows, :] = jnp.broadcast_to(peak, (tile, LANES))
            l_out[rows, :] = jnp.broadcast_to(total, (tile, LANES))
            acc_out[rows, :] = acc
    if not last:
        return
    out = refs[0]
    count = q_ref.shape[0]
    weight = jnp.concatenate(weights, axis=0)
    tail = out.shape[0] - count
    place = lax.broadcasted_iota(jnp.int32, (tail, LANES), 0)
    packed = jnp.zeros((tail, LANES), jnp.float32)
    for g in range(count // LANES):
        turned = jnp.transpose(weight[g * LANES : (g + 1) * LANES, :])
        packed = jnp.where(place == g, turned[:tail, :], packed)
    high = packed.astype(jnp.bfloat16)
    rest = packed - high.astype(jnp.float32)
    mid = rest.astype(jnp.bfloat16)
    low = (rest - mid.astype(jnp.float32)).astype(jnp.bfloat16)
    out[count:, :] = jnp.concatenate([high, mid, low, jnp.zeros_like(low)], axis=1)


def attend(fills, q, pieces, tile, new=None, state=None, last=False):
    rows = q.shape[0]
    spec = tuple((start, keys.shape[1], which) for start, which, keys in pieces)
    operands = [fills, q] + [keys for _, _, keys in pieces]
    if new is not None:
        operands += list(new)
    aliases = {}
    if state is not None:
        if not last:
            aliases = {len(operands) + i: i for i in range(3)}
        operands += list(state)
    if last:
        tail = -(-rows // (LANES * 16)) * 16
        out_shape = [jax.ShapeDtypeStruct((rows + tail, DC), jnp.bfloat16)]
    else:
        out_shape = [
            jax.ShapeDtypeStruct((rows, LANES), jnp.float32),
            jax.ShapeDtypeStruct((rows, LANES), jnp.float32),
            jax.ShapeDtypeStruct((rows, DC), jnp.float32),
        ]
    out = pl.pallas_call(
        functools.partial(attend_kernel, spec, new is not None, state is None, last, tile),
        in_specs=[pl.BlockSpec(memory_space=pltpu.SMEM)] + [WHOLE] * (len(operands) - 1),
        out_specs=[WHOLE] * len(out_shape),
        out_shape=out_shape,
        input_output_aliases=aliases,
        compiler_params=room(24),
        cost_estimate=pl.CostEstimate(flops=0, bytes_accessed=0, transcendentals=0),
        name="attend",
    )(*operands)
    return out[0] if last else out


def after_kernel(x_ref, *refs):
    pass


def after(x, *tokens):
    return pl.pallas_call(
        after_kernel,
        in_specs=[ANY] * (1 + len(tokens)),
        out_specs=ANY,
        out_shape=jax.ShapeDtypeStruct(x.shape, x.dtype),
        input_output_aliases={0: 0},
        compiler_params=room(1),
        name="after",
    )(x, *tokens)


def pack_kernel(order, me_ref, query_ref, dec_ref, span_kv_ref, dec_kv_ref, *out_refs):
    per, row = span_kv_ref.shape
    per_dec = dec_ref.shape[0]
    n = sum(len(x) for x in order)
    part = query_ref.shape[1] // n
    cut = part // per
    pad = -(-row // LANES) * LANES - row

    def padded(ref):
        x = ref[...].astype(jnp.float32)
        return jnp.concatenate([x, jnp.zeros((x.shape[0], pad), jnp.float32)], axis=1)

    dec_kv = padded(dec_kv_ref)
    tail = [padded(span_kv_ref)]
    for e in range(per_dec):
        for j in range(0, row + pad, per * LANES):
            ends = range(j, min(j + per * LANES, row + pad), LANES)
            strips = [dec_kv[e : e + 1, k : k + LANES] for k in ends]
            strips += [jnp.zeros((1, LANES), jnp.float32)] * (per - len(strips))
            tail.append(jnp.concatenate(strips, axis=0))
    tail = jnp.concatenate(tail, axis=1).astype(jnp.bfloat16)
    places = [(ref, i, r) for ref, rs in zip(out_refs, order) for i, r in enumerate(rs)]
    for out_ref, j, r in places:
        begin = (me_ref[0] ^ r) * part
        out_ref[j, :, :part] = query_ref[:, pl.ds(pl.multiple_of(begin, LANES), part)]
        for e in range(per_dec):
            strips = []
            for i in range(per):
                at = pl.multiple_of(begin + i * cut, LANES)
                strips.append(dec_ref[e : e + 1, pl.ds(at, cut)].astype(jnp.float32))
            at = part + e * cut
            out_ref[j, :, at : at + cut] = jnp.concatenate(strips, axis=0).astype(jnp.bfloat16)
        out_ref[j, :, part + per_dec * cut :] = tail


def pack(order, me, query, dec_query, span_kv, dec_kv):
    n = sum(len(x) for x in order)
    per, row = span_kv.shape
    per_dec = dec_kv.shape[0]
    part = query.shape[1] // n
    wide = -(-row // LANES) * LANES
    fold = -(-wide // (per * LANES)) * LANES
    total = part + per_dec * (part // per) + wide + per_dec * fold
    operands = (query, dec_query, span_kv, dec_kv)
    return pl.pallas_call(
        functools.partial(pack_kernel, order),
        grid=(1,),
        in_specs=[pl.BlockSpec(memory_space=pltpu.SMEM)]
        + [pl.BlockSpec(x.shape, lambda i: (0, 0)) for x in operands],
        out_specs=[pl.BlockSpec((len(x), per, total), lambda i: (0, 0, 0)) for x in order],
        out_shape=[jax.ShapeDtypeStruct((len(x), per, total), jnp.bfloat16) for x in order],
        compiler_params=room(60),
        name="pack",
    )(me, *operands)


def absorb_kernel(per_dec, order, me_ref, w_hbm, *refs):
    got_refs, refs = refs[: len(order)], refs[-6:]
    absorbed_ref, extra_ref, w_ref, placed, w_sem, sems = refs
    heads = w_ref.shape[0]
    n, per, total = placed.shape
    row = extra_ref.shape[1]
    count = absorbed_ref.shape[0] // heads
    wide = -(-row // LANES) * LANES
    fold = -(-wide // (per * LANES)) * LANES
    part = (total - wide - per_dec * fold) * per // (per + per_dec)
    width = part // heads
    cut = part // per
    at = part + per_dec * cut
    weights = pltpu.make_async_copy(w_hbm, w_ref, w_sem)
    weights.start()
    copies = [
        pltpu.make_async_copy(ref.at[i], placed.at[me_ref[0] ^ r], sems.at[r])
        for ref, rs in zip(got_refs, order)
        for i, r in enumerate(rs)
    ]
    for copy in copies:
        copy.start()
    for copy in copies:
        copy.wait()

    def unfold(x, length):
        strips = []
        for j in range(0, x.shape[1], length):
            strips += [x[i : i + 1, j : j + length] for i in range(per)]
        return jnp.concatenate(strips, axis=1)

    blocks = [placed[d].astype(jnp.float32) for d in range(n)]
    queries = [x[:, :part] for x in blocks]
    fresh = [x[:, at : at + wide] for x in blocks]
    for x in blocks:
        for e in range(per_dec):
            queries.append(unfold(x[:, part + e * cut : part + (e + 1) * cut], cut))
            begin = at + wide + e * fold
            fresh.append(unfold(x[:, begin : begin + fold], LANES)[:, :wide])
    q = jnp.concatenate(queries, axis=0).astype(jnp.bfloat16)
    new = jnp.concatenate(fresh, axis=0)
    blank = jnp.zeros((count, absorbed_ref.shape[1] - row), jnp.float32)
    weights.wait()
    for h in range(0, heads, 2):
        parts = []
        for g in (h, h + 1):
            mine = q[:, g * width : (g + 1) * width]
            latent = jnp.dot(mine[:, :DN], w_ref[g], preferred_element_type=jnp.float32)
            rope = mine[:, DN:].astype(jnp.float32)
            parts.append(jnp.concatenate([latent, rope, blank], axis=1))
        pair = jnp.concatenate(parts, axis=0).astype(jnp.bfloat16)
        absorbed_ref[h * count : (h + 2) * count, :] = pair
    blank = jnp.zeros((extra_ref.shape[0] - count, row), jnp.float32)
    extra_ref[...] = jnp.concatenate([new[:, :row], blank], axis=0).astype(jnp.bfloat16)


def absorb(count, per_dec, me, order, got, w_uk, row, tokens):
    heads = w_uk.shape[0]
    n = sum(len(x) for x in order)
    return pl.pallas_call(
        functools.partial(absorb_kernel, per_dec, order),
        in_specs=[pl.BlockSpec(memory_space=pltpu.SMEM)] + [ANY] * (1 + len(got) + len(tokens)),
        out_shape=[
            jax.ShapeDtypeStruct((heads * count, -(-row // LANES) * LANES), jnp.bfloat16),
            jax.ShapeDtypeStruct((LANES, row), jnp.bfloat16),
        ],
        scratch_shapes=[
            pltpu.VMEM(w_uk.shape, w_uk.dtype),
            pltpu.VMEM((n, *got[0].shape[1:]), got[0].dtype),
            pltpu.SemaphoreType.DMA(()),
            pltpu.SemaphoreType.DMA((n,)),
        ],
        compiler_params=room(16),
        name="absorb",
    )(me, w_uk, *got, *tokens)


def cut_kernel(spans, x_ref, *refs):
    for (a, b), ref in zip(spans, refs[-len(spans) :]):
        ref[...] = x_ref[:, a:b]


def cut(x, spans, tokens):
    return pl.pallas_call(
        functools.partial(cut_kernel, spans),
        in_specs=[WHOLE] + [ANY] * len(tokens),
        out_specs=[WHOLE] * len(spans),
        out_shape=[jax.ShapeDtypeStruct((x.shape[0], b - a), x.dtype) for a, b in spans],
        compiler_params=room(4),
        name="cut",
    )(x, *tokens)


def finish_kernel(count, m_ref, l_ref, acc_ref, far_ref, w_ref, span_ref, dec_ref):
    rows = m_ref.shape[0]
    heads = w_ref.shape[0]
    scale = score_scale * LOG2E
    parts = far_ref[rows:, :].astype(jnp.float32)
    packed = parts[:, :LANES] + parts[:, LANES : 2 * LANES] + parts[:, 2 * LANES : 3 * LANES]
    columns = []
    for g in range(rows // LANES):
        row = jnp.broadcast_to(packed[g : g + 1, :], (LANES, LANES))
        columns.append(jnp.transpose(row))
    far = jnp.concatenate(columns, axis=0)
    near = m_ref[...] * scale
    top = jnp.maximum(near, far)
    w_near = jnp.exp2(near - top)
    w_far = jnp.exp2(far - top)
    total = l_ref[...] * w_near + w_far
    inverse = 1.0 / total
    w_near = lanes(w_near * inverse, DC)
    w_far = lanes(w_far * inverse, DC)
    for h in range(heads):
        a, b = h * count, (h + 1) * count
        near_part = acc_ref[a:b, :] * w_near[a:b, :]
        far_part = far_ref[:rows, :].astype(jnp.float32)[a:b, :] * w_far[a:b, :]
        latent = (near_part + far_part).astype(jnp.bfloat16)
        done = jnp.dot(latent, w_ref[h], preferred_element_type=jnp.float32)
        span = span_ref.shape[0]
        span_ref[:, h * LANES : (h + 1) * LANES] = done[:span].astype(jnp.bfloat16)
        dec_ref[:, h * LANES : (h + 1) * LANES] = done[span:].astype(jnp.bfloat16)


def finish(count, span, state, far, w_uv):
    heads = w_uv.shape[0]
    wide = heads * w_uv.shape[2]
    return pl.pallas_call(
        functools.partial(finish_kernel, count),
        out_shape=(
            jax.ShapeDtypeStruct((span, wide), jnp.bfloat16),
            jax.ShapeDtypeStruct((count - span, wide), jnp.bfloat16),
        ),
        compiler_params=room(24),
        cost_estimate=pl.CostEstimate(
            flops=2 * count * heads * DC * w_uv.shape[2],
            bytes_accessed=2 * w_uv.size + 6 * state[2].size,
            transcendentals=0,
        ),
        name="finish",
    )(*state, far, w_uv)


def body(query, dec_query, cache_kv, span_kv, dec_kv, cache_fill, owner, slot, dec_len, w_uk, w_uv):
    me = lax.axis_index("seq")
    n = lax.axis_size("seq")
    pos_dev = cache_kv.shape[0]
    span = owner.shape[0]
    rows_dec = dec_len.shape[0]
    count = span + rows_dec
    heads = w_uk.shape[0]
    row = cache_kv.shape[1]

    def swap(x, stride):
        return lax.ppermute(x, "seq", [(i, i ^ stride) for i in range(n)])

    far, pair = n // 2, n // 4
    near = [1 << b for b in range(pair.bit_length() - 1)]
    keys = cache_kv.T
    edges = [i * (pos_dev // 8) for i in (0, 1, 5, 7, 8)]

    pieces = [swap(keys[:, : edges[1]], far)]

    place = me[None].astype(jnp.int32)
    order = [[r for r in range(n) if not r & 1], [r for r in range(n) if r & 1]]
    stay, go = pack(order, place, query, dec_query, span_kv, dec_kv)
    come = swap(go, 1)
    groups = {r: [(0, stay[i]), (1, come[i])] for i, r in enumerate(order[0])}
    for stride in near[1:]:
        away = [r for r in groups if r & stride]
        moved = swap(jnp.stack([x for r in away for _, x in groups[r]]), stride)
        held = len(groups[away[0]])
        for i, r in enumerate(away):
            kept = groups[r ^ stride]
            kept += [(o ^ stride, moved[i * held + j]) for j, (o, _) in enumerate(groups.pop(r))]
    got, order = [], []
    for r in sorted(groups):
        got.append(jnp.stack([x for _, x in groups[r]]))
        order.append([r ^ o for o, _ in groups[r]])
    got = got[:1] + [swap(x, r) for r, x in zip(sorted(groups)[1:], got[1:])]

    absorbed, extra = absorb(count, rows_dec // n, place, order, got, w_uk, row, pieces)
    new_rows = extra[:span]
    other = swap(absorbed, pair)
    spans = [*zip(edges, edges[1:])]
    cuts = cut(keys, spans[1:2], got[1:]) + cut(keys, spans[2:], [absorbed])
    pieces += [swap(x, far) for x in cuts]
    blocks = [(0, cut(keys, [(0, pos_dev)], got[1:])[0])]
    for stride in near:
        blocks += [(offset ^ stride, swap(x, stride)) for offset, x in blocks]

    def spread(x):
        part = [(far, x)]
        for stride in near:
            part += [(offset ^ stride, swap(y, stride)) for offset, y in part]
        return part

    target = jnp.where(owner == me, slot, -1)
    onehot = jnp.arange(pos_dev, dtype=jnp.int32)[None, :] == target[:, None]
    placed = lax.dot_general(
        new_rows,
        onehot.astype(jnp.bfloat16),
        (((0,), (0,)), ((), ())),
        preferred_element_type=jnp.float32,
    ).astype(jnp.bfloat16)
    new_cache = jnp.where(jnp.any(onehot, axis=0)[None, :], placed, keys).T

    limits = jnp.concatenate([jnp.arange(1, span + 1, dtype=jnp.int32), dec_len])
    index = jnp.arange(LANES, dtype=jnp.int32)
    queries = jnp.arange(count, dtype=jnp.int32)
    seen = (index[None, :] < span) & (index[None, :] < limits[:, None])
    seen |= (index[None, :] >= span) & (index[None, :] == queries[:, None])
    bias = jnp.where(seen, 0.0, HIDDEN).astype(jnp.float32)
    held = [offset for offset, _ in blocks]
    offsets = held + [offset ^ far for offset in held]
    which = jnp.stack([me ^ offset for offset in offsets])
    fills = jnp.sum(
        jnp.where(which[:, None] == jnp.arange(n, dtype=jnp.int32)[None, :], cache_fill[None, :], 0),
        axis=1,
    )
    base = len(blocks)
    tile = heads // 2 * count

    def stage_of(c, part):
        return [(edges[c], base + i, x) for i, (_, x) in enumerate(part)]

    home = [(0, 0, keys)]
    side = [(0, i, x) for i, (_, x) in enumerate(blocks) if i]
    state = attend(fills, absorbed, home, tile, new=(extra, bias))
    lead = stage_of(1, spread(after(pieces[1], state[0])))
    lead += stage_of(0, spread(pieces[0]))
    state = attend(fills, absorbed, side, tile, state=state)
    other = after(other, state[0])
    guest = attend(fills, other, home + side, tile)
    first = stage_of(2, spread(after(pieces[2], guest[0])))
    other = after(other, pieces[2])
    guest = attend(fills, other, lead, tile, state=guest)
    second = stage_of(3, spread(after(pieces[3], guest[0])))
    first, second = first + second[:1], second[1:]
    guest = attend(fills, other, first, tile, state=guest)
    sent = attend(fills, other, second, tile, state=guest, last=True)
    back = swap(sent, pair)
    state = attend(fills, absorbed, lead + first + second, tile, state=state)
    span_out, dec_out = finish(count, span, state, back, w_uv)
    return (span_out, dec_out, new_cache)


def solution(mesh):
    in_specs = (
        P(("grp", "seq"), None),
        P(("grp", "seq"), None),
        P(("grp", "seq"), None),
        P(("grp", "seq"), None),
        P(("grp", "seq"), None),
        P("grp"),
        P("grp"),
        P("grp"),
        P("grp"),
        P("seq", None, None),
        P("seq", None, None),
    )
    out_specs = (P("grp", "seq"), P("grp", "seq"), P(("grp", "seq"), None))
    return jax.shard_map(body, mesh=mesh, in_specs=in_specs, out_specs=out_specs, check_vma=False)
```

```python
import functools

import jax
import jax.numpy as jnp
from jax import lax
from jax.experimental import pallas as pl
from jax.experimental.pallas import tpu as pltpu
from jax.sharding import PartitionSpec as P

DN = 128
DC = 512
LANES = 128
ANY = pl.BlockSpec(memory_space=pl.ANY)
WHOLE = pl.BlockSpec(memory_space=pltpu.VMEM)


def room(mebibytes):
    return pltpu.CompilerParams(vmem_limit_bytes=mebibytes * 1024 * 1024)

score_scale = 0.1353
LOG2E = 1.4426950408889634
HIDDEN = -1e30
FLOOR = -1e25


def lanes(x, width):
    return jnp.concatenate([x] * (width // LANES), axis=1) if width > LANES else x


def attend_kernel(pieces, extra, first, last, tile, *refs):
    refs = list(refs)
    fills = refs.pop(0)
    q_ref = refs.pop(0)
    keys = [refs.pop(0) for _ in pieces]
    if extra:
        new_ref = refs.pop(0)
        bias_ref = refs.pop(0)
    if not first:
        m_in, l_in, acc_in = refs.pop(0), refs.pop(0), refs.pop(0)
    scale = score_scale * LOG2E
    weights = []
    sides = DC // (keys[0].shape[0] - DC)
    count = q_ref.shape[0] * sides // (sides + 1)
    fold = count // sides
    folded = q_ref[count:, :].astype(jnp.float32)
    ropes = jnp.split(folded, sides, axis=1)
    for at in range(0, count, tile):
        rows = slice(at, at + tile)
        q = q_ref[rows, :]
        rope = jnp.concatenate(ropes[at // fold : (at + tile) // fold], axis=0)
        rope = rope.astype(jnp.bfloat16)
        scores = []
        for (start, width, which), ref in zip(pieces, keys):
            s = jnp.dot(q, ref[:DC, :], preferred_element_type=jnp.float32)
            s = s + jnp.dot(rope, ref[DC:, :], preferred_element_type=jnp.float32)
            slot = start + lax.broadcasted_iota(jnp.int32, (1, width), 1)
            scores.append(jnp.where(slot < fills[which], s, HIDDEN))
        if extra:
            across = (((1,), (1,)), ((), ()))
            s = lax.dot_general(
                q, new_ref[:, :DC], across, preferred_element_type=jnp.float32
            ) + lax.dot_general(rope, new_ref[:, DC:], across, preferred_element_type=jnp.float32)
            bias = bias_ref[...]
            scores.append(s + jnp.concatenate([bias] * (tile // bias.shape[0]), axis=0))
        peak = functools.reduce(jnp.maximum, [jnp.max(s, axis=1, keepdims=True) for s in scores])
        peak = jnp.maximum(peak, FLOOR)
        if not first:
            old = m_in[rows, :1]
            peak = jnp.maximum(peak, old)
        total = 0.0
        acc = 0.0
        for i, s in enumerate(scores):
            e = jnp.exp2((s - peak) * scale)
            total = total + jnp.sum(e, axis=1, keepdims=True)
            w = e.astype(jnp.bfloat16)
            if i < len(pieces):
                acc = acc + lax.dot_general(
                    w, keys[i][:DC, :], (((1,), (1,)), ((), ())), preferred_element_type=jnp.float32
                )
            else:
                acc = acc + jnp.dot(w, new_ref[:, :DC], preferred_element_type=jnp.float32)
        if not first:
            keep = jnp.exp2((old - peak) * scale)
            total = total + l_in[rows, :1] * keep
            acc = acc + acc_in[rows, :] * keep
        if last:
            refs[0][rows, :] = (acc * (1.0 / total)).astype(jnp.bfloat16)
            weights.append(jnp.broadcast_to(peak * scale + jnp.log2(total), (tile, LANES)))
        else:
            m_out, l_out, acc_out = refs
            m_out[rows, :] = jnp.broadcast_to(peak, (tile, LANES))
            l_out[rows, :] = jnp.broadcast_to(total, (tile, LANES))
            acc_out[rows, :] = acc
    if not last:
        return
    out = refs[0]
    weight = jnp.concatenate(weights, axis=0)
    tail = out.shape[0] - count
    place = lax.broadcasted_iota(jnp.int32, (tail, LANES), 0)
    packed = jnp.zeros((tail, LANES), jnp.float32)
    for g in range(count // LANES):
        turned = jnp.transpose(weight[g * LANES : (g + 1) * LANES, :])
        packed = jnp.where(place == g, turned[:tail, :], packed)
    high = packed.astype(jnp.bfloat16)
    rest = packed - high.astype(jnp.float32)
    mid = rest.astype(jnp.bfloat16)
    low = (rest - mid.astype(jnp.float32)).astype(jnp.bfloat16)
    out[count:, :] = jnp.concatenate([high, mid, low, jnp.zeros_like(low)], axis=1)


def attend(fills, q, pieces, tile, new=None, state=None, last=False):
    row = pieces[0][2].shape[0]
    rows = q.shape[0] * DC // row
    spec = tuple((start, keys.shape[1], which) for start, which, keys in pieces)
    operands = [fills, q] + [keys for _, _, keys in pieces]
    if new is not None:
        operands += list(new)
    aliases = {}
    if state is not None:
        if not last:
            aliases = {len(operands) + i: i for i in range(3)}
        operands += list(state)
    if last:
        tail = -(-rows // (LANES * 16)) * 16
        out_shape = [jax.ShapeDtypeStruct((rows + tail, DC), jnp.bfloat16)]
    else:
        out_shape = [
            jax.ShapeDtypeStruct((rows, LANES), jnp.float32),
            jax.ShapeDtypeStruct((rows, LANES), jnp.float32),
            jax.ShapeDtypeStruct((rows, DC), jnp.float32),
        ]
    out = pl.pallas_call(
        functools.partial(attend_kernel, spec, new is not None, state is None, last, tile),
        in_specs=[pl.BlockSpec(memory_space=pltpu.SMEM)] + [WHOLE] * (len(operands) - 1),
        out_specs=[WHOLE] * len(out_shape),
        out_shape=out_shape,
        input_output_aliases=aliases,
        compiler_params=room(24),
        cost_estimate=pl.CostEstimate(flops=0, bytes_accessed=0, transcendentals=0),
        name="attend",
    )(*operands)
    return out[0] if last else out


def after_kernel(x_ref, *refs):
    pass


def after(x, *tokens):
    return pl.pallas_call(
        after_kernel,
        in_specs=[ANY] * (1 + len(tokens)),
        out_specs=ANY,
        out_shape=jax.ShapeDtypeStruct(x.shape, x.dtype),
        input_output_aliases={0: 0},
        compiler_params=room(1),
        name="after",
    )(x, *tokens)


def pack_kernel(order, me_ref, query_ref, dec_ref, span_kv_ref, dec_kv_ref, *out_refs):
    per, row = span_kv_ref.shape
    per_dec = dec_ref.shape[0]
    n = sum(len(x) for x in order)
    part = query_ref.shape[1] // n
    cut = part // per
    pad = -(-row // LANES) * LANES - row

    def padded(ref):
        x = ref[...].astype(jnp.float32)
        return jnp.concatenate([x, jnp.zeros((x.shape[0], pad), jnp.float32)], axis=1)

    dec_kv = padded(dec_kv_ref)
    tail = [padded(span_kv_ref)]
    for e in range(per_dec):
        for j in range(0, row + pad, per * LANES):
            ends = range(j, min(j + per * LANES, row + pad), LANES)
            strips = [dec_kv[e : e + 1, k : k + LANES] for k in ends]
            strips += [jnp.zeros((1, LANES), jnp.float32)] * (per - len(strips))
            tail.append(jnp.concatenate(strips, axis=0))
    tail = jnp.concatenate(tail, axis=1).astype(jnp.bfloat16)
    places = [(ref, i, r) for ref, rs in zip(out_refs, order) for i, r in enumerate(rs)]
    for out_ref, j, r in places:
        begin = (me_ref[0] ^ r) * part
        out_ref[j, :, :part] = query_ref[:, pl.ds(pl.multiple_of(begin, LANES), part)]
        for e in range(per_dec):
            strips = []
            for i in range(per):
                at = pl.multiple_of(begin + i * cut, LANES)
                strips.append(dec_ref[e : e + 1, pl.ds(at, cut)].astype(jnp.float32))
            at = part + e * cut
            out_ref[j, :, at : at + cut] = jnp.concatenate(strips, axis=0).astype(jnp.bfloat16)
        out_ref[j, :, part + per_dec * cut :] = tail


def pack(order, me, query, dec_query, span_kv, dec_kv):
    n = sum(len(x) for x in order)
    per, row = span_kv.shape
    per_dec = dec_kv.shape[0]
    part = query.shape[1] // n
    wide = -(-row // LANES) * LANES
    fold = -(-wide // (per * LANES)) * LANES
    total = part + per_dec * (part // per) + wide + per_dec * fold
    operands = (query, dec_query, span_kv, dec_kv)
    return pl.pallas_call(
        functools.partial(pack_kernel, order),
        grid=(1,),
        in_specs=[pl.BlockSpec(memory_space=pltpu.SMEM)]
        + [pl.BlockSpec(x.shape, lambda i: (0, 0)) for x in operands],
        out_specs=[pl.BlockSpec((len(x), per, total), lambda i: (0, 0, 0)) for x in order],
        out_shape=[jax.ShapeDtypeStruct((len(x), per, total), jnp.bfloat16) for x in order],
        compiler_params=room(60),
        name="pack",
    )(me, *operands)


def absorb_kernel(per_dec, order, me_ref, w_hbm, *refs):
    got_refs, refs = refs[: len(order)], refs[-6:]
    absorbed_ref, extra_ref, w_ref, placed, w_sem, sems = refs
    heads = w_ref.shape[0]
    n, per, total = placed.shape
    row = extra_ref.shape[1]
    count = absorbed_ref.shape[0] * DC // row // heads
    wide = -(-row // LANES) * LANES
    fold = -(-wide // (per * LANES)) * LANES
    part = (total - wide - per_dec * fold) * per // (per + per_dec)
    width = part // heads
    cut = part // per
    at = part + per_dec * cut
    weights = pltpu.make_async_copy(w_hbm, w_ref, w_sem)
    weights.start()
    copies = [
        pltpu.make_async_copy(ref.at[i], placed.at[me_ref[0] ^ r], sems.at[r])
        for ref, rs in zip(got_refs, order)
        for i, r in enumerate(rs)
    ]
    for copy in copies:
        copy.start()
    for copy in copies:
        copy.wait()

    def unfold(x, length):
        strips = []
        for j in range(0, x.shape[1], length):
            strips += [x[i : i + 1, j : j + length] for i in range(per)]
        return jnp.concatenate(strips, axis=1)

    blocks = [placed[d].astype(jnp.float32) for d in range(n)]
    queries = [x[:, :part] for x in blocks]
    fresh = [x[:, at : at + wide] for x in blocks]
    for x in blocks:
        for e in range(per_dec):
            queries.append(unfold(x[:, part + e * cut : part + (e + 1) * cut], cut))
            begin = at + wide + e * fold
            fresh.append(unfold(x[:, begin : begin + fold], LANES)[:, :wide])
    q = jnp.concatenate(queries, axis=0).astype(jnp.bfloat16)
    new = jnp.concatenate(fresh, axis=0)
    weights.wait()
    ropes = []
    for h in range(0, heads, 2):
        parts = []
        for g in (h, h + 1):
            mine = q[:, g * width : (g + 1) * width]
            parts.append(jnp.dot(mine[:, :DN], w_ref[g], preferred_element_type=jnp.float32))
            ropes.append(mine[:, DN:].astype(jnp.float32))
        pair = jnp.concatenate(parts, axis=0).astype(jnp.bfloat16)
        absorbed_ref[h * count : (h + 2) * count, :] = pair
    ropes = jnp.split(jnp.concatenate(ropes, axis=0), DC // (row - DC), axis=0)
    absorbed_ref[heads * count :, :] = jnp.concatenate(ropes, axis=1).astype(jnp.bfloat16)
    blank = jnp.zeros((extra_ref.shape[0] - count, row), jnp.float32)
    extra_ref[...] = jnp.concatenate([new[:, :row], blank], axis=0).astype(jnp.bfloat16)


def absorb(count, per_dec, me, order, got, w_uk, row, tokens):
    heads = w_uk.shape[0]
    n = sum(len(x) for x in order)
    return pl.pallas_call(
        functools.partial(absorb_kernel, per_dec, order),
        in_specs=[pl.BlockSpec(memory_space=pltpu.SMEM)] + [ANY] * (1 + len(got) + len(tokens)),
        out_shape=[
            jax.ShapeDtypeStruct((heads * count * row // DC, DC), jnp.bfloat16),
            jax.ShapeDtypeStruct((LANES, row), jnp.bfloat16),
        ],
        scratch_shapes=[
            pltpu.VMEM(w_uk.shape, w_uk.dtype),
            pltpu.VMEM((n, *got[0].shape[1:]), got[0].dtype),
            pltpu.SemaphoreType.DMA(()),
            pltpu.SemaphoreType.DMA((n,)),
        ],
        compiler_params=room(16),
        name="absorb",
    )(me, w_uk, *got, *tokens)


def cut_kernel(spans, x_ref, *refs):
    for (a, b), ref in zip(spans, refs[-len(spans) :]):
        ref[...] = x_ref[:, a:b]


def cut(x, spans, tokens):
    return pl.pallas_call(
        functools.partial(cut_kernel, spans),
        in_specs=[WHOLE] + [ANY] * len(tokens),
        out_specs=[WHOLE] * len(spans),
        out_shape=[jax.ShapeDtypeStruct((x.shape[0], b - a), x.dtype) for a, b in spans],
        compiler_params=room(4),
        name="cut",
    )(x, *tokens)


def finish_kernel(count, m_ref, l_ref, acc_ref, far_ref, w_ref, span_ref, dec_ref):
    rows = m_ref.shape[0]
    heads = w_ref.shape[0]
    scale = score_scale * LOG2E
    parts = far_ref[rows:, :].astype(jnp.float32)
    packed = parts[:, :LANES] + parts[:, LANES : 2 * LANES] + parts[:, 2 * LANES : 3 * LANES]
    columns = []
    for g in range(rows // LANES):
        row = jnp.broadcast_to(packed[g : g + 1, :], (LANES, LANES))
        columns.append(jnp.transpose(row))
    far = jnp.concatenate(columns, axis=0)
    near = m_ref[...] * scale
    top = jnp.maximum(near, far)
    w_near = jnp.exp2(near - top)
    w_far = jnp.exp2(far - top)
    total = l_ref[...] * w_near + w_far
    inverse = 1.0 / total
    w_near = lanes(w_near * inverse, DC)
    w_far = lanes(w_far * inverse, DC)
    for h in range(heads):
        a, b = h * count, (h + 1) * count
        near_part = acc_ref[a:b, :] * w_near[a:b, :]
        far_part = far_ref[:rows, :].astype(jnp.float32)[a:b, :] * w_far[a:b, :]
        latent = (near_part + far_part).astype(jnp.bfloat16)
        done = jnp.dot(latent, w_ref[h], preferred_element_type=jnp.float32)
        span = span_ref.shape[0]
        span_ref[:, h * LANES : (h + 1) * LANES] = done[:span].astype(jnp.bfloat16)
        dec_ref[:, h * LANES : (h + 1) * LANES] = done[span:].astype(jnp.bfloat16)


def finish(count, span, state, far, w_uv):
    heads = w_uv.shape[0]
    wide = heads * w_uv.shape[2]
    return pl.pallas_call(
        functools.partial(finish_kernel, count),
        out_shape=(
            jax.ShapeDtypeStruct((span, wide), jnp.bfloat16),
            jax.ShapeDtypeStruct((count - span, wide), jnp.bfloat16),
        ),
        compiler_params=room(24),
        cost_estimate=pl.CostEstimate(
            flops=2 * count * heads * DC * w_uv.shape[2],
            bytes_accessed=2 * w_uv.size + 6 * state[2].size,
            transcendentals=0,
        ),
        name="finish",
    )(*state, far, w_uv)


def body(query, dec_query, cache_kv, span_kv, dec_kv, cache_fill, owner, slot, dec_len, w_uk, w_uv):
    me = lax.axis_index("seq")
    n = lax.axis_size("seq")
    pos_dev = cache_kv.shape[0]
    span = owner.shape[0]
    rows_dec = dec_len.shape[0]
    count = span + rows_dec
    heads = w_uk.shape[0]
    row = cache_kv.shape[1]

    def swap(x, stride):
        return lax.ppermute(x, "seq", [(i, i ^ stride) for i in range(n)])

    far, pair = n // 2, n // 4
    near = [1 << b for b in range(pair.bit_length() - 1)]
    keys = cache_kv.T
    edges = [i * (pos_dev // 8) for i in (0, 1, 5, 7, 8)]

    pieces = [swap(keys[:, : edges[1]], far)]

    place = me[None].astype(jnp.int32)
    order = [[r for r in range(n) if not r & 1], [r for r in range(n) if r & 1]]
    stay, go = pack(order, place, query, dec_query, span_kv, dec_kv)
    come = swap(go, 1)
    groups = {r: [(0, stay[i]), (1, come[i])] for i, r in enumerate(order[0])}
    for stride in near[1:]:
        away = [r for r in groups if r & stride]
        moved = swap(jnp.stack([x for r in away for _, x in groups[r]]), stride)
        held = len(groups[away[0]])
        for i, r in enumerate(away):
            kept = groups[r ^ stride]
            kept += [(o ^ stride, moved[i * held + j]) for j, (o, _) in enumerate(groups.pop(r))]
    got, order = [], []
    for r in sorted(groups):
        got.append(jnp.stack([x for _, x in groups[r]]))
        order.append([r ^ o for o, _ in groups[r]])
    got = got[:1] + [swap(x, r) for r, x in zip(sorted(groups)[1:], got[1:])]

    absorbed, extra = absorb(count, rows_dec // n, place, order, got, w_uk, row, pieces)
    new_rows = extra[:span]
    other = swap(absorbed, pair)
    spans = [*zip(edges, edges[1:])]
    cuts = cut(keys, spans[1:2], got[1:]) + cut(keys, spans[2:], [absorbed])
    pieces += [swap(x, far) for x in cuts]
    blocks = [(0, cut(keys, [(0, pos_dev)], got[1:])[0])]
    for stride in near:
        blocks += [(offset ^ stride, swap(x, stride)) for offset, x in blocks]

    def spread(x):
        part = [(far, x)]
        for stride in near:
            part += [(offset ^ stride, swap(y, stride)) for offset, y in part]
        return part

    target = jnp.where(owner == me, slot, -1)
    onehot = jnp.arange(pos_dev, dtype=jnp.int32)[None, :] == target[:, None]
    placed = lax.dot_general(
        new_rows,
        onehot.astype(jnp.bfloat16),
        (((0,), (0,)), ((), ())),
        preferred_element_type=jnp.float32,
    ).astype(jnp.bfloat16)
    new_cache = jnp.where(jnp.any(onehot, axis=0)[None, :], placed, keys).T

    limits = jnp.concatenate([jnp.arange(1, span + 1, dtype=jnp.int32), dec_len])
    index = jnp.arange(LANES, dtype=jnp.int32)
    queries = jnp.arange(count, dtype=jnp.int32)
    seen = (index[None, :] < span) & (index[None, :] < limits[:, None])
    seen |= (index[None, :] >= span) & (index[None, :] == queries[:, None])
    bias = jnp.where(seen, 0.0, HIDDEN).astype(jnp.float32)
    held = [offset for offset, _ in blocks]
    offsets = held + [offset ^ far for offset in held]
    which = jnp.stack([me ^ offset for offset in offsets])
    fills = jnp.sum(
        jnp.where(which[:, None] == jnp.arange(n, dtype=jnp.int32)[None, :], cache_fill[None, :], 0),
        axis=1,
    )
    base = len(blocks)
    tile = heads // 2 * count

    def stage_of(c, part):
        return [(edges[c], base + i, x) for i, (_, x) in enumerate(part)]

    home = [(0, 0, keys)]
    side = [(0, i, x) for i, (_, x) in enumerate(blocks) if i]
    state = attend(fills, absorbed, home, tile, new=(extra, bias))
    lead = stage_of(1, spread(after(pieces[1], state[0])))
    lead += stage_of(0, spread(pieces[0]))
    state = attend(fills, absorbed, side, tile, state=state)
    other = after(other, state[0])
    guest = attend(fills, other, home + side, tile)
    first = stage_of(2, spread(after(pieces[2], guest[0])))
    other = after(other, pieces[2])
    guest = attend(fills, other, lead, tile, state=guest)
    second = stage_of(3, spread(after(pieces[3], guest[0])))
    first, second = first + second[:1], second[1:]
    guest = attend(fills, other, first, tile, state=guest)
    sent = attend(fills, other, second, tile, state=guest, last=True)
    back = swap(sent, pair)
    state = attend(fills, absorbed, lead + first + second, tile, state=state)
    span_out, dec_out = finish(count, span, state, back, w_uv)
    return (span_out, dec_out, new_cache)


def solution(mesh):
    in_specs = (
        P(("grp", "seq"), None),
        P(("grp", "seq"), None),
        P(("grp", "seq"), None),
        P(("grp", "seq"), None),
        P(("grp", "seq"), None),
        P("grp"),
        P("grp"),
        P("grp"),
        P("grp"),
        P("seq", None, None),
        P("seq", None, None),
    )
    out_specs = (P("grp", "seq"), P("grp", "seq"), P(("grp", "seq"), None))
    return jax.shard_map(body, mesh=mesh, in_specs=in_specs, out_specs=out_specs, check_vma=False)
```

```python
import functools

import jax
import jax.numpy as jnp
from jax import lax
from jax.experimental import pallas as pl
from jax.experimental.pallas import tpu as pltpu
from jax.sharding import PartitionSpec as P

DN = 128
DC = 512
LANES = 128
ANY = pl.BlockSpec(memory_space=pl.ANY)
WHOLE = pl.BlockSpec(memory_space=pltpu.VMEM)


def room(mebibytes):
    return pltpu.CompilerParams(vmem_limit_bytes=mebibytes * 1024 * 1024)

score_scale = 0.1353
LOG2E = 1.4426950408889634
HIDDEN = -1e30
FLOOR = -1e25


def lanes(x, width):
    return jnp.concatenate([x] * (width // LANES), axis=1) if width > LANES else x


def attend_kernel(pieces, extra, first, last, tile, *refs):
    refs = list(refs)
    fills = refs.pop(0)
    q_ref = refs.pop(0)
    keys = [refs.pop(0) for _ in pieces]
    if extra:
        new_ref = refs.pop(0)
        bias_ref = refs.pop(0)
    if not first:
        m_in, l_in, acc_in = refs.pop(0), refs.pop(0), refs.pop(0)
    scale = score_scale * LOG2E
    weights = []
    sides = DC // (keys[0].shape[0] - DC)
    count = q_ref.shape[0] * sides // (sides + 1)
    fold = count // sides
    folded = q_ref[count:, :].astype(jnp.float32)
    ropes = jnp.split(folded, sides, axis=1)
    for at in range(0, count, tile):
        rows = slice(at, at + tile)
        q = q_ref[rows, :]
        rope = jnp.concatenate(ropes[at // fold : (at + tile) // fold], axis=0)
        rope = rope.astype(jnp.bfloat16)
        scores = []
        for (start, width, which), ref in zip(pieces, keys):
            s = jnp.dot(q, ref[:DC, :], preferred_element_type=jnp.float32)
            s = s + jnp.dot(rope, ref[DC:, :], preferred_element_type=jnp.float32)
            slot = start + lax.broadcasted_iota(jnp.int32, (1, width), 1)
            scores.append(jnp.where(slot < fills[which], s, HIDDEN))
        if extra:
            across = (((1,), (1,)), ((), ()))
            s = lax.dot_general(
                q, new_ref[:, :DC], across, preferred_element_type=jnp.float32
            ) + lax.dot_general(rope, new_ref[:, DC:], across, preferred_element_type=jnp.float32)
            bias = bias_ref[...]
            scores.append(s + jnp.concatenate([bias] * (tile // bias.shape[0]), axis=0))
        peak = functools.reduce(jnp.maximum, [jnp.max(s, axis=1, keepdims=True) for s in scores])
        peak = jnp.maximum(peak, FLOOR)
        if not first:
            old = m_in[rows, :1]
            peak = jnp.maximum(peak, old)
        total = 0.0
        acc = 0.0
        for i, s in enumerate(scores):
            e = jnp.exp2((s - peak) * scale)
            total = total + jnp.sum(e, axis=1, keepdims=True)
            w = e.astype(jnp.bfloat16)
            if i < len(pieces):
                acc = acc + lax.dot_general(
                    w, keys[i][:DC, :], (((1,), (1,)), ((), ())), preferred_element_type=jnp.float32
                )
            else:
                acc = acc + jnp.dot(w, new_ref[:, :DC], preferred_element_type=jnp.float32)
        if not first:
            keep = jnp.exp2((old - peak) * scale)
            total = total + l_in[rows, :1] * keep
            acc = acc + acc_in[rows, :] * keep
        if last:
            refs[0][rows, :] = (acc * (1.0 / total)).astype(jnp.bfloat16)
            weights.append(jnp.broadcast_to(peak * scale + jnp.log2(total), (tile, LANES)))
        else:
            m_out, l_out, acc_out = refs
            m_out[rows, :] = jnp.broadcast_to(peak, (tile, LANES))
            l_out[rows, :] = jnp.broadcast_to(total, (tile, LANES))
            acc_out[rows, :] = acc
    if not last:
        return
    out = refs[0]
    weight = jnp.concatenate(weights, axis=0)
    tail = out.shape[0] - count
    place = lax.broadcasted_iota(jnp.int32, (tail, LANES), 0)
    packed = jnp.zeros((tail, LANES), jnp.float32)
    for g in range(count // LANES):
        turned = jnp.transpose(weight[g * LANES : (g + 1) * LANES, :])
        packed = jnp.where(place == g, turned[:tail, :], packed)
    high = packed.astype(jnp.bfloat16)
    rest = packed - high.astype(jnp.float32)
    mid = rest.astype(jnp.bfloat16)
    low = (rest - mid.astype(jnp.float32)).astype(jnp.bfloat16)
    out[count:, :] = jnp.concatenate([high, mid, low, jnp.zeros_like(low)], axis=1)


def attend(fills, q, pieces, tile, new=None, state=None, last=False):
    row = pieces[0][2].shape[0]
    rows = q.shape[0] * DC // row
    spec = tuple((start, keys.shape[1], which) for start, which, keys in pieces)
    operands = [fills, q] + [keys for _, _, keys in pieces]
    if new is not None:
        operands += list(new)
    aliases = {}
    if state is not None:
        if not last:
            aliases = {len(operands) + i: i for i in range(3)}
        operands += list(state)
    if last:
        tail = -(-rows // (LANES * 16)) * 16
        out_shape = [jax.ShapeDtypeStruct((rows + tail, DC), jnp.bfloat16)]
    else:
        out_shape = [
            jax.ShapeDtypeStruct((rows, LANES), jnp.float32),
            jax.ShapeDtypeStruct((rows, LANES), jnp.float32),
            jax.ShapeDtypeStruct((rows, DC), jnp.float32),
        ]
    out = pl.pallas_call(
        functools.partial(attend_kernel, spec, new is not None, state is None, last, tile),
        in_specs=[pl.BlockSpec(memory_space=pltpu.SMEM)] + [WHOLE] * (len(operands) - 1),
        out_specs=[WHOLE] * len(out_shape),
        out_shape=out_shape,
        input_output_aliases=aliases,
        compiler_params=room(24),
        cost_estimate=pl.CostEstimate(flops=0, bytes_accessed=0, transcendentals=0),
        name="attend",
    )(*operands)
    return out[0] if last else out


def after_kernel(x_ref, *refs):
    pass


def after(x, *tokens):
    return pl.pallas_call(
        after_kernel,
        in_specs=[ANY] * (1 + len(tokens)),
        out_specs=ANY,
        out_shape=jax.ShapeDtypeStruct(x.shape, x.dtype),
        input_output_aliases={0: 0},
        compiler_params=room(1),
        name="after",
    )(x, *tokens)


def pack_kernel(order, me_ref, query_ref, dec_ref, span_kv_ref, dec_kv_ref, *out_refs):
    per, row = span_kv_ref.shape
    per_dec = dec_ref.shape[0]
    n = sum(len(x) for x in order)
    part = query_ref.shape[1] // n
    cut = part // per
    pad = -(-row // LANES) * LANES - row

    def padded(ref):
        x = ref[...].astype(jnp.float32)
        return jnp.concatenate([x, jnp.zeros((x.shape[0], pad), jnp.float32)], axis=1)

    dec_kv = padded(dec_kv_ref)
    tail = [padded(span_kv_ref)]
    for e in range(per_dec):
        for j in range(0, row + pad, per * LANES):
            ends = range(j, min(j + per * LANES, row + pad), LANES)
            strips = [dec_kv[e : e + 1, k : k + LANES] for k in ends]
            strips += [jnp.zeros((1, LANES), jnp.float32)] * (per - len(strips))
            tail.append(jnp.concatenate(strips, axis=0))
    tail = jnp.concatenate(tail, axis=1).astype(jnp.bfloat16)
    places = [(ref, i, r) for ref, rs in zip(out_refs, order) for i, r in enumerate(rs)]
    for out_ref, j, r in places:
        begin = (me_ref[0] ^ r) * part
        out_ref[j, :, :part] = query_ref[:, pl.ds(pl.multiple_of(begin, LANES), part)]
        for e in range(per_dec):
            strips = []
            for i in range(per):
                at = pl.multiple_of(begin + i * cut, LANES)
                strips.append(dec_ref[e : e + 1, pl.ds(at, cut)].astype(jnp.float32))
            at = part + e * cut
            out_ref[j, :, at : at + cut] = jnp.concatenate(strips, axis=0).astype(jnp.bfloat16)
        out_ref[j, :, part + per_dec * cut :] = tail


def pack(order, me, query, dec_query, span_kv, dec_kv):
    n = sum(len(x) for x in order)
    per, row = span_kv.shape
    per_dec = dec_kv.shape[0]
    part = query.shape[1] // n
    wide = -(-row // LANES) * LANES
    fold = -(-wide // (per * LANES)) * LANES
    total = part + per_dec * (part // per) + wide + per_dec * fold
    operands = (query, dec_query, span_kv, dec_kv)
    return pl.pallas_call(
        functools.partial(pack_kernel, order),
        grid=(1,),
        in_specs=[pl.BlockSpec(memory_space=pltpu.SMEM)]
        + [pl.BlockSpec(x.shape, lambda i: (0, 0)) for x in operands],
        out_specs=[pl.BlockSpec((len(x), per, total), lambda i: (0, 0, 0)) for x in order],
        out_shape=[jax.ShapeDtypeStruct((len(x), per, total), jnp.bfloat16) for x in order],
        compiler_params=room(60),
        name="pack",
    )(me, *operands)


def absorb_kernel(per_dec, order, me_ref, w_hbm, *refs):
    got_refs, refs = refs[: len(order)], refs[-6:]
    absorbed_ref, extra_ref, w_ref, placed, w_sem, sems = refs
    heads = w_ref.shape[0]
    n, per, total = placed.shape
    row = extra_ref.shape[1]
    count = absorbed_ref.shape[0] * DC // row // heads
    wide = -(-row // LANES) * LANES
    fold = -(-wide // (per * LANES)) * LANES
    part = (total - wide - per_dec * fold) * per // (per + per_dec)
    width = part // heads
    cut = part // per
    at = part + per_dec * cut
    weights = pltpu.make_async_copy(w_hbm, w_ref, w_sem)
    weights.start()
    copies = [
        pltpu.make_async_copy(ref.at[i], placed.at[me_ref[0] ^ r], sems.at[r])
        for ref, rs in zip(got_refs, order)
        for i, r in enumerate(rs)
    ]
    for copy in copies:
        copy.start()
    for copy in copies:
        copy.wait()

    def unfold(x, length):
        strips = []
        for j in range(0, x.shape[1], length):
            strips += [x[i : i + 1, j : j + length] for i in range(per)]
        return jnp.concatenate(strips, axis=1)

    blocks = [placed[d].astype(jnp.float32) for d in range(n)]
    queries = [x[:, :part] for x in blocks]
    fresh = [x[:, at : at + wide] for x in blocks]
    for x in blocks:
        for e in range(per_dec):
            queries.append(unfold(x[:, part + e * cut : part + (e + 1) * cut], cut))
            begin = at + wide + e * fold
            fresh.append(unfold(x[:, begin : begin + fold], LANES)[:, :wide])
    q = jnp.concatenate(queries, axis=0).astype(jnp.bfloat16)
    new = jnp.concatenate(fresh, axis=0)
    weights.wait()
    ropes = []
    for h in range(0, heads, 2):
        parts = []
        for g in (h, h + 1):
            mine = q[:, g * width : (g + 1) * width]
            parts.append(jnp.dot(mine[:, :DN], w_ref[g], preferred_element_type=jnp.float32))
            ropes.append(mine[:, DN:].astype(jnp.float32))
        pair = jnp.concatenate(parts, axis=0).astype(jnp.bfloat16)
        absorbed_ref[h * count : (h + 2) * count, :] = pair
    ropes = jnp.split(jnp.concatenate(ropes, axis=0), DC // (row - DC), axis=0)
    absorbed_ref[heads * count :, :] = jnp.concatenate(ropes, axis=1).astype(jnp.bfloat16)
    blank = jnp.zeros((extra_ref.shape[0] - count, row), jnp.float32)
    extra_ref[...] = jnp.concatenate([new[:, :row], blank], axis=0).astype(jnp.bfloat16)


def absorb(count, per_dec, me, order, got, w_uk, row, tokens):
    heads = w_uk.shape[0]
    n = sum(len(x) for x in order)
    return pl.pallas_call(
        functools.partial(absorb_kernel, per_dec, order),
        in_specs=[pl.BlockSpec(memory_space=pltpu.SMEM)] + [ANY] * (1 + len(got) + len(tokens)),
        out_shape=[
            jax.ShapeDtypeStruct((heads * count * row // DC, DC), jnp.bfloat16),
            jax.ShapeDtypeStruct((LANES, row), jnp.bfloat16),
        ],
        scratch_shapes=[
            pltpu.VMEM(w_uk.shape, w_uk.dtype),
            pltpu.VMEM((n, *got[0].shape[1:]), got[0].dtype),
            pltpu.SemaphoreType.DMA(()),
            pltpu.SemaphoreType.DMA((n,)),
        ],
        compiler_params=room(16),
        name="absorb",
    )(me, w_uk, *got, *tokens)


def cut_kernel(spans, x_ref, *refs):
    for (a, b), ref in zip(spans, refs[-len(spans) :]):
        ref[...] = x_ref[:, a:b]


def cut(x, spans, tokens):
    return pl.pallas_call(
        functools.partial(cut_kernel, spans),
        in_specs=[WHOLE] + [ANY] * len(tokens),
        out_specs=[WHOLE] * len(spans),
        out_shape=[jax.ShapeDtypeStruct((x.shape[0], b - a), x.dtype) for a, b in spans],
        compiler_params=room(4),
        name="cut",
    )(x, *tokens)


def finish_kernel(count, m_ref, l_ref, acc_ref, far_ref, w_ref, span_ref, dec_ref):
    rows = m_ref.shape[0]
    heads = w_ref.shape[0]
    scale = score_scale * LOG2E
    parts = far_ref[rows:, :].astype(jnp.float32)
    packed = parts[:, :LANES] + parts[:, LANES : 2 * LANES] + parts[:, 2 * LANES : 3 * LANES]
    columns = []
    for g in range(rows // LANES):
        row = jnp.broadcast_to(packed[g : g + 1, :], (LANES, LANES))
        columns.append(jnp.transpose(row))
    far = jnp.concatenate(columns, axis=0)
    near = m_ref[...] * scale
    top = jnp.maximum(near, far)
    w_near = jnp.exp2(near - top)
    w_far = jnp.exp2(far - top)
    total = l_ref[...] * w_near + w_far
    inverse = 1.0 / total
    w_near = lanes(w_near * inverse, DC)
    w_far = lanes(w_far * inverse, DC)
    for h in range(heads):
        a, b = h * count, (h + 1) * count
        near_part = acc_ref[a:b, :] * w_near[a:b, :]
        far_part = far_ref[:rows, :].astype(jnp.float32)[a:b, :] * w_far[a:b, :]
        latent = (near_part + far_part).astype(jnp.bfloat16)
        done = jnp.dot(latent, w_ref[h], preferred_element_type=jnp.float32)
        span = span_ref.shape[0]
        span_ref[:, h * LANES : (h + 1) * LANES] = done[:span].astype(jnp.bfloat16)
        dec_ref[:, h * LANES : (h + 1) * LANES] = done[span:].astype(jnp.bfloat16)


def finish(count, span, state, far, w_uv):
    heads = w_uv.shape[0]
    wide = heads * w_uv.shape[2]
    return pl.pallas_call(
        functools.partial(finish_kernel, count),
        out_shape=(
            jax.ShapeDtypeStruct((span, wide), jnp.bfloat16),
            jax.ShapeDtypeStruct((count - span, wide), jnp.bfloat16),
        ),
        compiler_params=room(24),
        cost_estimate=pl.CostEstimate(
            flops=2 * count * heads * DC * w_uv.shape[2],
            bytes_accessed=2 * w_uv.size + 6 * state[2].size,
            transcendentals=0,
        ),
        name="finish",
    )(*state, far, w_uv)


def body(query, dec_query, cache_kv, span_kv, dec_kv, cache_fill, owner, slot, dec_len, w_uk, w_uv):
    me = lax.axis_index("seq")
    n = lax.axis_size("seq")
    pos_dev = cache_kv.shape[0]
    span = owner.shape[0]
    rows_dec = dec_len.shape[0]
    count = span + rows_dec
    heads = w_uk.shape[0]
    row = cache_kv.shape[1]

    def swap(x, stride):
        return lax.ppermute(x, "seq", [(i, i ^ stride) for i in range(n)])

    far, pair = n // 2, n // 4
    near = [1 << b for b in range(pair.bit_length() - 1)]
    keys = cache_kv.T
    edges = [i * (pos_dev // 8) for i in (0, 1, 4, 6, 8)]

    pieces = [swap(keys[:, : edges[1]], far)]

    place = me[None].astype(jnp.int32)
    order = [[r for r in range(n) if not r & 1], [r for r in range(n) if r & 1]]
    stay, go = pack(order, place, query, dec_query, span_kv, dec_kv)
    come = swap(go, 1)
    groups = {r: [(0, stay[i]), (1, come[i])] for i, r in enumerate(order[0])}
    for stride in near[1:]:
        away = [r for r in groups if r & stride]
        moved = swap(jnp.stack([x for r in away for _, x in groups[r]]), stride)
        held = len(groups[away[0]])
        for i, r in enumerate(away):
            kept = groups[r ^ stride]
            kept += [(o ^ stride, moved[i * held + j]) for j, (o, _) in enumerate(groups.pop(r))]
    got, order = [], []
    for r in sorted(groups):
        got.append(jnp.stack([x for _, x in groups[r]]))
        order.append([r ^ o for o, _ in groups[r]])
    got = got[:1] + [swap(x, r) for r, x in zip(sorted(groups)[1:], got[1:])]

    absorbed, extra = absorb(count, rows_dec // n, place, order, got, w_uk, row, pieces)
    new_rows = extra[:span]
    other = swap(absorbed, pair)
    spans = [*zip(edges, edges[1:])]
    cuts = cut(keys, spans[1:2], got[1:]) + cut(keys, spans[2:], [absorbed])
    pieces += [swap(x, far) for x in cuts]
    blocks = [(0, cut(keys, [(0, pos_dev)], got[1:])[0])]
    for stride in near:
        blocks += [(offset ^ stride, swap(x, stride)) for offset, x in blocks]

    def spread(x):
        part = [(far, x)]
        for stride in near:
            part += [(offset ^ stride, swap(y, stride)) for offset, y in part]
        return part

    target = jnp.where(owner == me, slot, -1)
    onehot = jnp.arange(pos_dev, dtype=jnp.int32)[None, :] == target[:, None]
    placed = lax.dot_general(
        new_rows,
        onehot.astype(jnp.bfloat16),
        (((0,), (0,)), ((), ())),
        preferred_element_type=jnp.float32,
    ).astype(jnp.bfloat16)
    new_cache = jnp.where(jnp.any(onehot, axis=0)[None, :], placed, keys).T

    limits = jnp.concatenate([jnp.arange(1, span + 1, dtype=jnp.int32), dec_len])
    index = jnp.arange(LANES, dtype=jnp.int32)
    queries = jnp.arange(count, dtype=jnp.int32)
    seen = (index[None, :] < span) & (index[None, :] < limits[:, None])
    seen |= (index[None, :] >= span) & (index[None, :] == queries[:, None])
    bias = jnp.where(seen, 0.0, HIDDEN).astype(jnp.float32)
    held = [offset for offset, _ in blocks]
    offsets = held + [offset ^ far for offset in held]
    which = jnp.stack([me ^ offset for offset in offsets])
    fills = jnp.sum(
        jnp.where(which[:, None] == jnp.arange(n, dtype=jnp.int32)[None, :], cache_fill[None, :], 0),
        axis=1,
    )
    base = len(blocks)
    tile = heads // 2 * count

    def stage_of(c, part):
        return [(edges[c], base + i, x) for i, (_, x) in enumerate(part)]

    home = [(0, 0, keys)]
    side = [(0, i, x) for i, (_, x) in enumerate(blocks) if i]
    state = attend(fills, absorbed, home, tile, new=(extra, bias))
    lead = stage_of(1, spread(after(pieces[1], state[0])))
    lead += stage_of(0, spread(pieces[0]))
    state = attend(fills, absorbed, side, tile, state=state)
    other = after(other, state[0])
    guest = attend(fills, other, home + side, tile)
    first = stage_of(2, spread(after(pieces[2], guest[0])))
    other = after(other, pieces[2])
    guest = attend(fills, other, lead, tile, state=guest)
    second = stage_of(3, spread(after(pieces[3], guest[0])))
    first, second = first + second[:1], second[1:]
    guest = attend(fills, other, first, tile, state=guest)
    sent = attend(fills, other, second, tile, state=guest, last=True)
    back = swap(sent, pair)
    state = attend(fills, absorbed, lead + first + second, tile, state=state)
    span_out, dec_out = finish(count, span, state, back, w_uv)
    return (span_out, dec_out, new_cache)


def solution(mesh):
    in_specs = (
        P(("grp", "seq"), None),
        P(("grp", "seq"), None),
        P(("grp", "seq"), None),
        P(("grp", "seq"), None),
        P(("grp", "seq"), None),
        P("grp"),
        P("grp"),
        P("grp"),
        P("grp"),
        P("seq", None, None),
        P("seq", None, None),
    )
    out_specs = (P("grp", "seq"), P("grp", "seq"), P(("grp", "seq"), None))
    return jax.shard_map(body, mesh=mesh, in_specs=in_specs, out_specs=out_specs, check_vma=False)
```

```python
import functools

import jax
import jax.numpy as jnp
from jax import lax
from jax.experimental import pallas as pl
from jax.experimental.pallas import tpu as pltpu
from jax.sharding import PartitionSpec as P

DN = 128
DC = 512
LANES = 128
ANY = pl.BlockSpec(memory_space=pl.ANY)
WHOLE = pl.BlockSpec(memory_space=pltpu.VMEM)


def room(mebibytes):
    return pltpu.CompilerParams(vmem_limit_bytes=mebibytes * 1024 * 1024)

score_scale = 0.1353
LOG2E = 1.4426950408889634
HIDDEN = -1e30
FLOOR = -1e25


def lanes(x, width):
    return jnp.concatenate([x] * (width // LANES), axis=1) if width > LANES else x


def attend_kernel(pieces, extra, first, last, tile, *refs):
    refs = list(refs)
    fills = refs.pop(0)
    q_ref = refs.pop(0)
    keys = [refs.pop(0) for _ in pieces]
    if extra:
        new_ref = refs.pop(0)
        bias_ref = refs.pop(0)
    if not first:
        m_in, l_in, acc_in = refs.pop(0), refs.pop(0), refs.pop(0)
    scale = score_scale * LOG2E
    weights = []
    sides = DC // (keys[0].shape[0] - DC)
    count = q_ref.shape[0] * sides // (sides + 1)
    fold = count // sides
    folded = q_ref[count:, :].astype(jnp.float32)
    ropes = jnp.split(folded, sides, axis=1)
    for at in range(0, count, tile):
        rows = slice(at, at + tile)
        q = q_ref[rows, :]
        rope = jnp.concatenate(ropes[at // fold : (at + tile) // fold], axis=0)
        rope = rope.astype(jnp.bfloat16)
        scores = []
        for (start, width, which), ref in zip(pieces, keys):
            s = jnp.dot(q, ref[:DC, :], preferred_element_type=jnp.float32)
            s = s + jnp.dot(rope, ref[DC:, :], preferred_element_type=jnp.float32)
            slot = start + lax.broadcasted_iota(jnp.int32, (1, width), 1)
            scores.append(jnp.where(slot < fills[which], s, HIDDEN))
        if extra:
            across = (((1,), (1,)), ((), ()))
            s = lax.dot_general(
                q, new_ref[:, :DC], across, preferred_element_type=jnp.float32
            ) + lax.dot_general(rope, new_ref[:, DC:], across, preferred_element_type=jnp.float32)
            bias = bias_ref[...]
            scores.append(s + jnp.concatenate([bias] * (tile // bias.shape[0]), axis=0))
        peak = functools.reduce(jnp.maximum, [jnp.max(s, axis=1, keepdims=True) for s in scores])
        peak = jnp.maximum(peak, FLOOR)
        if not first:
            old = m_in[rows, :1]
            peak = jnp.maximum(peak, old)
        total = 0.0
        acc = 0.0
        for i, s in enumerate(scores):
            e = jnp.exp2((s - peak) * scale)
            total = total + jnp.sum(e, axis=1, keepdims=True)
            w = e.astype(jnp.bfloat16)
            if i < len(pieces):
                acc = acc + lax.dot_general(
                    w, keys[i][:DC, :], (((1,), (1,)), ((), ())), preferred_element_type=jnp.float32
                )
            else:
                acc = acc + jnp.dot(w, new_ref[:, :DC], preferred_element_type=jnp.float32)
        if not first:
            keep = jnp.exp2((old - peak) * scale)
            total = total + l_in[rows, :1] * keep
            acc = acc + acc_in[rows, :] * keep
        if last:
            refs[0][rows, :] = (acc * (1.0 / total)).astype(jnp.bfloat16)
            weights.append(jnp.broadcast_to(peak * scale + jnp.log2(total), (tile, LANES)))
        else:
            m_out, l_out, acc_out = refs
            m_out[rows, :] = jnp.broadcast_to(peak, (tile, LANES))
            l_out[rows, :] = jnp.broadcast_to(total, (tile, LANES))
            acc_out[rows, :] = acc
    if not last:
        return
    out = refs[0]
    weight = jnp.concatenate(weights, axis=0)
    tail = out.shape[0] - count
    place = lax.broadcasted_iota(jnp.int32, (tail, LANES), 0)
    packed = jnp.zeros((tail, LANES), jnp.float32)
    for g in range(count // LANES):
        turned = jnp.transpose(weight[g * LANES : (g + 1) * LANES, :])
        packed = jnp.where(place == g, turned[:tail, :], packed)
    high = packed.astype(jnp.bfloat16)
    rest = packed - high.astype(jnp.float32)
    mid = rest.astype(jnp.bfloat16)
    low = (rest - mid.astype(jnp.float32)).astype(jnp.bfloat16)
    out[count:, :] = jnp.concatenate([high, mid, low, jnp.zeros_like(low)], axis=1)


def attend(fills, q, pieces, tile, new=None, state=None, last=False):
    row = pieces[0][2].shape[0]
    rows = q.shape[0] * DC // row
    spec = tuple((start, keys.shape[1], which) for start, which, keys in pieces)
    operands = [fills, q] + [keys for _, _, keys in pieces]
    if new is not None:
        operands += list(new)
    aliases = {}
    if state is not None:
        if not last:
            aliases = {len(operands) + i: i for i in range(3)}
        operands += list(state)
    if last:
        tail = -(-rows // (LANES * 16)) * 16
        out_shape = [jax.ShapeDtypeStruct((rows + tail, DC), jnp.bfloat16)]
    else:
        out_shape = [
            jax.ShapeDtypeStruct((rows, LANES), jnp.float32),
            jax.ShapeDtypeStruct((rows, LANES), jnp.float32),
            jax.ShapeDtypeStruct((rows, DC), jnp.float32),
        ]
    out = pl.pallas_call(
        functools.partial(attend_kernel, spec, new is not None, state is None, last, tile),
        in_specs=[pl.BlockSpec(memory_space=pltpu.SMEM)] + [WHOLE] * (len(operands) - 1),
        out_specs=[WHOLE] * len(out_shape),
        out_shape=out_shape,
        input_output_aliases=aliases,
        compiler_params=room(24),
        cost_estimate=pl.CostEstimate(flops=0, bytes_accessed=0, transcendentals=0),
        name="attend",
    )(*operands)
    return out[0] if last else out


def after_kernel(x_ref, *refs):
    pass


def after(x, *tokens):
    return pl.pallas_call(
        after_kernel,
        in_specs=[ANY] * (1 + len(tokens)),
        out_specs=ANY,
        out_shape=jax.ShapeDtypeStruct(x.shape, x.dtype),
        input_output_aliases={0: 0},
        compiler_params=room(1),
        name="after",
    )(x, *tokens)


def pack_kernel(order, me_ref, query_ref, dec_ref, span_kv_ref, dec_kv_ref, *out_refs):
    per, row = span_kv_ref.shape
    per_dec = dec_ref.shape[0]
    n = sum(len(x) for x in order)
    part = query_ref.shape[1] // n
    cut = part // per
    pad = -(-row // LANES) * LANES - row

    def padded(ref):
        x = ref[...].astype(jnp.float32)
        return jnp.concatenate([x, jnp.zeros((x.shape[0], pad), jnp.float32)], axis=1)

    dec_kv = padded(dec_kv_ref)
    tail = [padded(span_kv_ref)]
    for e in range(per_dec):
        for j in range(0, row + pad, per * LANES):
            ends = range(j, min(j + per * LANES, row + pad), LANES)
            strips = [dec_kv[e : e + 1, k : k + LANES] for k in ends]
            strips += [jnp.zeros((1, LANES), jnp.float32)] * (per - len(strips))
            tail.append(jnp.concatenate(strips, axis=0))
    tail = jnp.concatenate(tail, axis=1).astype(jnp.bfloat16)
    places = [(ref, i, r) for ref, rs in zip(out_refs, order) for i, r in enumerate(rs)]
    for out_ref, j, r in places:
        begin = (me_ref[0] ^ r) * part
        out_ref[j, :, :part] = query_ref[:, pl.ds(pl.multiple_of(begin, LANES), part)]
        for e in range(per_dec):
            strips = []
            for i in range(per):
                at = pl.multiple_of(begin + i * cut, LANES)
                strips.append(dec_ref[e : e + 1, pl.ds(at, cut)].astype(jnp.float32))
            at = part + e * cut
            out_ref[j, :, at : at + cut] = jnp.concatenate(strips, axis=0).astype(jnp.bfloat16)
        out_ref[j, :, part + per_dec * cut :] = tail


def pack(order, me, query, dec_query, span_kv, dec_kv):
    n = sum(len(x) for x in order)
    per, row = span_kv.shape
    per_dec = dec_kv.shape[0]
    part = query.shape[1] // n
    wide = -(-row // LANES) * LANES
    fold = -(-wide // (per * LANES)) * LANES
    total = part + per_dec * (part // per) + wide + per_dec * fold
    operands = (query, dec_query, span_kv, dec_kv)
    return pl.pallas_call(
        functools.partial(pack_kernel, order),
        grid=(1,),
        in_specs=[pl.BlockSpec(memory_space=pltpu.SMEM)]
        + [pl.BlockSpec(x.shape, lambda i: (0, 0)) for x in operands],
        out_specs=[pl.BlockSpec((len(x), per, total), lambda i: (0, 0, 0)) for x in order],
        out_shape=[jax.ShapeDtypeStruct((len(x), per, total), jnp.bfloat16) for x in order],
        compiler_params=room(60),
        name="pack",
    )(me, *operands)


def absorb_kernel(per_dec, order, me_ref, w_hbm, *refs):
    got_refs, refs = refs[: len(order)], refs[-6:]
    absorbed_ref, extra_ref, w_ref, placed, w_sem, sems = refs
    heads = w_ref.shape[0]
    n, per, total = placed.shape
    row = extra_ref.shape[1]
    count = absorbed_ref.shape[0] * DC // row // heads
    wide = -(-row // LANES) * LANES
    fold = -(-wide // (per * LANES)) * LANES
    part = (total - wide - per_dec * fold) * per // (per + per_dec)
    width = part // heads
    cut = part // per
    at = part + per_dec * cut
    weights = pltpu.make_async_copy(w_hbm, w_ref, w_sem)
    weights.start()
    copies = [
        pltpu.make_async_copy(ref.at[i], placed.at[me_ref[0] ^ r], sems.at[r])
        for ref, rs in zip(got_refs, order)
        for i, r in enumerate(rs)
    ]
    for copy in copies:
        copy.start()
    for copy in copies:
        copy.wait()

    def unfold(x, length):
        strips = []
        for j in range(0, x.shape[1], length):
            strips += [x[i : i + 1, j : j + length] for i in range(per)]
        return jnp.concatenate(strips, axis=1)

    blocks = [placed[d].astype(jnp.float32) for d in range(n)]
    queries = [x[:, :part] for x in blocks]
    fresh = [x[:, at : at + wide] for x in blocks]
    for x in blocks:
        for e in range(per_dec):
            queries.append(unfold(x[:, part + e * cut : part + (e + 1) * cut], cut))
            begin = at + wide + e * fold
            fresh.append(unfold(x[:, begin : begin + fold], LANES)[:, :wide])
    q = jnp.concatenate(queries, axis=0).astype(jnp.bfloat16)
    new = jnp.concatenate(fresh, axis=0)
    weights.wait()
    ropes = []
    for h in range(0, heads, 2):
        parts = []
        for g in (h, h + 1):
            mine = q[:, g * width : (g + 1) * width]
            parts.append(jnp.dot(mine[:, :DN], w_ref[g], preferred_element_type=jnp.float32))
            ropes.append(mine[:, DN:].astype(jnp.float32))
        pair = jnp.concatenate(parts, axis=0).astype(jnp.bfloat16)
        absorbed_ref[h * count : (h + 2) * count, :] = pair
    ropes = jnp.split(jnp.concatenate(ropes, axis=0), DC // (row - DC), axis=0)
    absorbed_ref[heads * count :, :] = jnp.concatenate(ropes, axis=1).astype(jnp.bfloat16)
    blank = jnp.zeros((extra_ref.shape[0] - count, row), jnp.float32)
    extra_ref[...] = jnp.concatenate([new[:, :row], blank], axis=0).astype(jnp.bfloat16)


def absorb(count, per_dec, me, order, got, w_uk, row, tokens):
    heads = w_uk.shape[0]
    n = sum(len(x) for x in order)
    return pl.pallas_call(
        functools.partial(absorb_kernel, per_dec, order),
        in_specs=[pl.BlockSpec(memory_space=pltpu.SMEM)] + [ANY] * (1 + len(got) + len(tokens)),
        out_shape=[
            jax.ShapeDtypeStruct((heads * count * row // DC, DC), jnp.bfloat16),
            jax.ShapeDtypeStruct((LANES, row), jnp.bfloat16),
        ],
        scratch_shapes=[
            pltpu.VMEM(w_uk.shape, w_uk.dtype),
            pltpu.VMEM((n, *got[0].shape[1:]), got[0].dtype),
            pltpu.SemaphoreType.DMA(()),
            pltpu.SemaphoreType.DMA((n,)),
        ],
        compiler_params=room(16),
        name="absorb",
    )(me, w_uk, *got, *tokens)


def cut_kernel(spans, x_ref, *refs):
    for (a, b), ref in zip(spans, refs[-len(spans) :]):
        ref[...] = x_ref[:, a:b]


def cut(x, spans, tokens):
    return pl.pallas_call(
        functools.partial(cut_kernel, spans),
        in_specs=[WHOLE] + [ANY] * len(tokens),
        out_specs=[WHOLE] * len(spans),
        out_shape=[jax.ShapeDtypeStruct((x.shape[0], b - a), x.dtype) for a, b in spans],
        compiler_params=room(4),
        name="cut",
    )(x, *tokens)


def finish_kernel(count, m_ref, l_ref, acc_ref, far_ref, w_ref, span_ref, dec_ref):
    rows = m_ref.shape[0]
    heads = w_ref.shape[0]
    scale = score_scale * LOG2E
    parts = far_ref[rows:, :].astype(jnp.float32)
    packed = parts[:, :LANES] + parts[:, LANES : 2 * LANES] + parts[:, 2 * LANES : 3 * LANES]
    columns = []
    for g in range(rows // LANES):
        row = jnp.broadcast_to(packed[g : g + 1, :], (LANES, LANES))
        columns.append(jnp.transpose(row))
    far = jnp.concatenate(columns, axis=0)
    near = m_ref[...] * scale
    top = jnp.maximum(near, far)
    w_near = jnp.exp2(near - top)
    w_far = jnp.exp2(far - top)
    total = l_ref[...] * w_near + w_far
    inverse = 1.0 / total
    w_near = lanes(w_near * inverse, DC)
    w_far = lanes(w_far * inverse, DC)
    for h in range(heads):
        a, b = h * count, (h + 1) * count
        near_part = acc_ref[a:b, :] * w_near[a:b, :]
        far_part = far_ref[:rows, :].astype(jnp.float32)[a:b, :] * w_far[a:b, :]
        latent = (near_part + far_part).astype(jnp.bfloat16)
        done = jnp.dot(latent, w_ref[h], preferred_element_type=jnp.float32)
        span = span_ref.shape[0]
        span_ref[:, h * LANES : (h + 1) * LANES] = done[:span].astype(jnp.bfloat16)
        dec_ref[:, h * LANES : (h + 1) * LANES] = done[span:].astype(jnp.bfloat16)


def finish(count, span, state, far, w_uv):
    heads = w_uv.shape[0]
    wide = heads * w_uv.shape[2]
    return pl.pallas_call(
        functools.partial(finish_kernel, count),
        out_shape=(
            jax.ShapeDtypeStruct((span, wide), jnp.bfloat16),
            jax.ShapeDtypeStruct((count - span, wide), jnp.bfloat16),
        ),
        compiler_params=room(24),
        cost_estimate=pl.CostEstimate(
            flops=2 * count * heads * DC * w_uv.shape[2],
            bytes_accessed=2 * w_uv.size + 6 * state[2].size,
            transcendentals=0,
        ),
        name="finish",
    )(*state, far, w_uv)


def body(query, dec_query, cache_kv, span_kv, dec_kv, cache_fill, owner, slot, dec_len, w_uk, w_uv):
    me = lax.axis_index("seq")
    n = lax.axis_size("seq")
    pos_dev = cache_kv.shape[0]
    span = owner.shape[0]
    rows_dec = dec_len.shape[0]
    count = span + rows_dec
    heads = w_uk.shape[0]
    row = cache_kv.shape[1]

    def swap(x, stride):
        return lax.ppermute(x, "seq", [(i, i ^ stride) for i in range(n)])

    far, pair = n // 2, n // 4
    near = [1 << b for b in range(pair.bit_length() - 1)]
    keys = cache_kv.T
    edges = [i * (pos_dev // 8) for i in (0, 1, 4, 7, 8)]

    pieces = [swap(keys[:, : edges[1]], far)]

    place = me[None].astype(jnp.int32)
    order = [[r for r in range(n) if not r & 1], [r for r in range(n) if r & 1]]
    stay, go = pack(order, place, query, dec_query, span_kv, dec_kv)
    come = swap(go, 1)
    groups = {r: [(0, stay[i]), (1, come[i])] for i, r in enumerate(order[0])}
    for stride in near[1:]:
        away = [r for r in groups if r & stride]
        moved = swap(jnp.stack([x for r in away for _, x in groups[r]]), stride)
        held = len(groups[away[0]])
        for i, r in enumerate(away):
            kept = groups[r ^ stride]
            kept += [(o ^ stride, moved[i * held + j]) for j, (o, _) in enumerate(groups.pop(r))]
    got, order = [], []
    for r in sorted(groups):
        got.append(jnp.stack([x for _, x in groups[r]]))
        order.append([r ^ o for o, _ in groups[r]])
    got = got[:1] + [swap(x, r) for r, x in zip(sorted(groups)[1:], got[1:])]

    absorbed, extra = absorb(count, rows_dec // n, place, order, got, w_uk, row, pieces)
    new_rows = extra[:span]
    other = swap(absorbed, pair)
    spans = [*zip(edges, edges[1:])]
    cuts = cut(keys, spans[1:2], got[1:]) + cut(keys, spans[2:], [absorbed])
    pieces += [swap(x, far) for x in cuts]
    blocks = [(0, cut(keys, [(0, pos_dev)], got[1:])[0])]
    for stride in near:
        blocks += [(offset ^ stride, swap(x, stride)) for offset, x in blocks]

    def spread(x):
        part = [(far, x)]
        for stride in near:
            part += [(offset ^ stride, swap(y, stride)) for offset, y in part]
        return part

    target = jnp.where(owner == me, slot, -1)
    onehot = jnp.arange(pos_dev, dtype=jnp.int32)[None, :] == target[:, None]
    placed = lax.dot_general(
        new_rows,
        onehot.astype(jnp.bfloat16),
        (((0,), (0,)), ((), ())),
        preferred_element_type=jnp.float32,
    ).astype(jnp.bfloat16)
    new_cache = jnp.where(jnp.any(onehot, axis=0)[None, :], placed, keys).T

    limits = jnp.concatenate([jnp.arange(1, span + 1, dtype=jnp.int32), dec_len])
    index = jnp.arange(LANES, dtype=jnp.int32)
    queries = jnp.arange(count, dtype=jnp.int32)
    seen = (index[None, :] < span) & (index[None, :] < limits[:, None])
    seen |= (index[None, :] >= span) & (index[None, :] == queries[:, None])
    bias = jnp.where(seen, 0.0, HIDDEN).astype(jnp.float32)
    held = [offset for offset, _ in blocks]
    offsets = held + [offset ^ far for offset in held]
    which = jnp.stack([me ^ offset for offset in offsets])
    fills = jnp.sum(
        jnp.where(which[:, None] == jnp.arange(n, dtype=jnp.int32)[None, :], cache_fill[None, :], 0),
        axis=1,
    )
    base = len(blocks)
    tile = heads // 2 * count

    def stage_of(c, part):
        return [(edges[c], base + i, x) for i, (_, x) in enumerate(part)]

    home = [(0, 0, keys)]
    side = [(0, i, x) for i, (_, x) in enumerate(blocks) if i]
    state = attend(fills, absorbed, home, tile, new=(extra, bias))
    lead = stage_of(1, spread(after(pieces[1], state[0])))
    lead += stage_of(0, spread(pieces[0]))
    state = attend(fills, absorbed, side, tile, state=state)
    other = after(other, state[0])
    guest = attend(fills, other, home + side, tile)
    first = stage_of(2, spread(after(pieces[2], guest[0])))
    other = after(other, pieces[2])
    guest = attend(fills, other, lead, tile, state=guest)
    second = stage_of(3, spread(after(pieces[3], guest[0])))
    first, second = first + second[:1], second[1:]
    guest = attend(fills, other, first, tile, state=guest)
    sent = attend(fills, other, second, tile, state=guest, last=True)
    back = swap(sent, pair)
    state = attend(fills, absorbed, lead + first + second, tile, state=state)
    span_out, dec_out = finish(count, span, state, back, w_uv)
    return (span_out, dec_out, new_cache)


def solution(mesh):
    in_specs = (
        P(("grp", "seq"), None),
        P(("grp", "seq"), None),
        P(("grp", "seq"), None),
        P(("grp", "seq"), None),
        P(("grp", "seq"), None),
        P("grp"),
        P("grp"),
        P("grp"),
        P("grp"),
        P("seq", None, None),
        P("seq", None, None),
    )
    out_specs = (P("grp", "seq"), P("grp", "seq"), P(("grp", "seq"), None))
    return jax.shard_map(body, mesh=mesh, in_specs=in_specs, out_specs=out_specs, check_vma=False)
```
